32 devices in a mesh: dp: 8 (over z, core), blk: 4 (over y, x).
Axes of the slice: x: 2, y: 2, z: 4, core: 2. Of those that a mesh axis runs over, the one named last changes fastest.
Arguments:
- features: bfloat16 [8192, 12800], P(('dp', 'blk')), may hold values from -6 to 6
- cotangent: bfloat16 [8192, 12800], P(('dp', 'blk')), may hold values from -6 to 6
- send_order: int32 [32, 256], P(('dp', 'blk')), may hold values from 0 to 255, each once within a row
- pair_index: int32 [96, 2], P(('dp', 'blk')), may hold values from 0 to 1, as said below
- edge_mask: int32 [96, 128, 128], P(('dp', 'blk')), may hold values 0 or 1
- distance: float32 [96, 128, 128], P(('dp', 'blk')), may hold values from 0.8 to 4.8
- radial_weight: float32 [512, 5], replicated, may hold values from -1.5 to 1.5
- mix_weight: bfloat16 [2560, 512], replicated, may hold values from -0.25 to 0.25
- out_weight: bfloat16 [2560, 512], replicated, may hold values from -0.25 to 0.25
Outputs:
- updated: bfloat16 [8192, 12800], P(('dp', 'blk'))
- mix_grad: float32 [2560, 512], P('blk')
- out_grad: float32 [2560, 512], P('blk')
The draws below stay inside these ranges and needn't reach their ends.
Inputs may be any that keep to these rules, and one draw needn't show every extreme that they name: `pair_index`: each device's 3 pairs are distinct; both entries are local block numbers. Each row of send_order is a permutation of the device's rows.
All inputs are finite; a program needn't handle non-finite values. No bound on the sum of `edge_mask` on one device may be relied on, other than what follows from the above.
Results may differ from the reference program's by a relative error of at most 0.0059.
Values may be sent and summed in bfloat16 or wider, within the bound.
No kernel may reach another device: no remote copies, remote signals or barrier semaphores. Data moves between devices by JAX's collectives and lax.ppermute only.
A program may use at most 192 MiB of HBM per device.

```python
import math
import jax
import jax.numpy as jnp
import numpy as np
from jax import lax

C = 512
LMAX = 4
LDEG = 25
BLOCK = 128
ROWS = 256
PAIRS = 3
NRBF = 512
WROWS = 2560
ATOMS = 8192
PAIR_ROWS = 96
N_DP = 8
N_BLK = 4
DEVICES = 32


def draw_pair_index(key, part):
    blocks = ROWS // BLOCK
    keys = jax.random.split(key, PAIR_ROWS // PAIRS)
    picks = jax.vmap(lambda one: jax.random.permutation(one, blocks * blocks)[:PAIRS])(keys)
    pairs = jnp.stack([picks // blocks, picks % blocks], axis=-1)
    return pairs.reshape(PAIR_ROWS, 2).astype(jnp.int32)


def plant(values, own_key, low, high):
    spot = [jax.random.randint(jax.random.fold_in(own_key, axis), (), 0, length) for axis, length in enumerate(values.shape)]
    longest = values.shape.index(max(values.shape))
    neighbour = spot[:longest] + [(spot[longest] + 1) % values.shape[longest]] + spot[longest + 1:]
    return values.at[tuple(spot)].set(low).at[tuple(neighbour)].set(high)


def shard_levels(stream_key, shape, shards, smallest, largest):
    def one(axis_at, blocks):
        steps = jax.random.uniform(jax.random.fold_in(jax.random.fold_in(stream_key, 6), axis_at), (blocks,), jnp.float32, smallest / len(shards), largest / len(shards))
        return jnp.repeat(jnp.exp(steps), shape[axis_at] // blocks).reshape((-1,) + (1,) * (len(shape) - axis_at - 1))

    loudness = one(*shards[0])
    for cut in shards[1:]:
        loudness = loudness * one(*cut)
    return loudness


def noise(key, dims, deviation, most, pieces=(), held_as=jnp.bfloat16):
    result = jax.random.normal(key, dims, jnp.float32) * deviation
    if len(pieces) > 0:
        result = shard_levels(key, dims, pieces, -0.22, 0.18) * result
    return jnp.clip(result, min=-most, max=most).astype(held_as)


def setup_inputs(seed: int = 0) -> dict:
    arg_keys = jax.random.split(jax.random.key(seed), 10)
    features = noise(arg_keys[0], (ATOMS, LDEG * C), 1.0, 6.0, ((0, 32),))
    cotangent = noise(arg_keys[1], (ATOMS, LDEG * C), 1.0, 6.0, ((0, 32),))
    send_order = jax.vmap(lambda own: jax.random.permutation(own, ROWS))(jax.random.split(arg_keys[2], DEVICES)).reshape((DEVICES, ROWS)).astype(jnp.int32)
    pair_index = draw_pair_index(jax.random.fold_in(arg_keys[9], 71), 0)
    edge_mask = plant((jax.random.randint(arg_keys[4], (PAIR_ROWS, BLOCK, BLOCK), 0, 4) < 1).astype(jnp.int32), jax.random.fold_in(arg_keys[4], 1), 0, 1)
    distance = jnp.clip(0.8 + 4 * jax.random.uniform(arg_keys[5], (PAIR_ROWS, BLOCK, BLOCK), jnp.float32) ** shard_levels(arg_keys[5], (PAIR_ROWS, BLOCK, BLOCK), ((0, 32),), -0.2, 0.2), 0.8, 4.8)
    radial_weight = noise(arg_keys[6], (NRBF, LMAX + 1), 0.25, 1.5, (), jnp.float32)
    mix_weight = noise(arg_keys[7], (WROWS, C), C ** -0.5, 0.25)
    out_weight = noise(arg_keys[8], (WROWS, C), C ** -0.5, 0.25)
    return {"features": features, "cotangent": cotangent, "send_order": send_order, "pair_index": pair_index, "edge_mask": edge_mask, "distance": distance, "radial_weight": radial_weight, "mix_weight": mix_weight, "out_weight": out_weight}


edge_scale = 0.25
cut_radius = 5.0


def degree_table():
    table = np.zeros((LMAX + 1, LDEG), np.float32)
    for level in range(LMAX + 1):
        table[level, level * level:(level + 1) * (level + 1)] = 1.0
    return table


def gate_one(item, radial_weight):
    mask, dist = item
    centers = cut_radius * jnp.arange(NRBF, dtype=jnp.float32) / (NRBF - 1)
    gamma = 0.5 * ((NRBF - 1) / cut_radius) ** 2
    basis = jnp.exp(-gamma * (dist[..., None] - centers) ** 2)
    radial = jnp.einsum("ijk,kl->ijl", basis, radial_weight, precision=lax.Precision.HIGHEST)
    envelope = 0.5 * (jnp.cos(math.pi * dist / cut_radius) + 1.0) * mask.astype(jnp.float32) * edge_scale
    per_level = radial * envelope[..., None]
    expanded = jnp.einsum("ijl,lk->ijk", per_level, jnp.asarray(degree_table()), precision=lax.Precision.HIGHEST)
    return expanded.astype(jnp.bfloat16)


def gate_of(mask, dist, radial_weight):
    return lax.map(lambda item: gate_one(item, radial_weight), (mask, dist))


def per_degree(rows, weight, form):
    parts = []
    for level in range(LMAX + 1):
        left = rows[:, level * level:(level + 1) * (level + 1)].astype(jnp.float32)
        right = weight[level * C:(level + 1) * C].astype(jnp.float32)
        parts.append(jnp.einsum(form, left, right))
    return jnp.concatenate(parts, axis=1)


def grad_degree(left_rows, right_rows):
    parts = []
    for level in range(LMAX + 1):
        left = left_rows[:, level * level:(level + 1) * (level + 1)].astype(jnp.float32)
        right = right_rows[:, level * level:(level + 1) * (level + 1)].astype(jnp.float32)
        parts.append(jnp.einsum("rkc,rkd->cd", left, right))
    return jnp.concatenate(parts, axis=0)


def device_pass(rows, cot, pairs, mask, dist, radial_weight, mix_weight, out_weight):
    blocks = ROWS // BLOCK
    hidden = rows.reshape(ROWS, LDEG, C)
    grad_rows = cot.reshape(ROWS, LDEG, C)
    gate = gate_of(mask, dist, radial_weight).astype(jnp.float32)
    source = per_degree(hidden, mix_weight, "rkc,cd->rkd").astype(jnp.bfloat16)
    source_blocks = source.reshape(blocks, BLOCK, LDEG, C).astype(jnp.float32)
    gathered = jnp.zeros((blocks, BLOCK, LDEG, C), jnp.float32)
    for pair in range(PAIRS):
        dest, src = pairs[pair, 0], pairs[pair, 1]
        gathered = gathered.at[dest].add(jnp.einsum("ijk,jkc->ikc", gate[pair], source_blocks[src]))
    message = gathered.astype(jnp.bfloat16).reshape(ROWS, LDEG, C)
    mixed = per_degree(message, out_weight, "rkc,cd->rkd")
    updated = (hidden.astype(jnp.float32) + mixed).astype(jnp.bfloat16)
    out_part = grad_degree(message, grad_rows)
    dmessage = per_degree(grad_rows, out_weight, "rkd,cd->rkc").astype(jnp.bfloat16)
    dmessage_blocks = dmessage.reshape(blocks, BLOCK, LDEG, C).astype(jnp.float32)
    dsource = jnp.zeros((blocks, BLOCK, LDEG, C), jnp.float32)
    for pair in range(PAIRS):
        dest, src = pairs[pair, 0], pairs[pair, 1]
        dsource = dsource.at[src].add(jnp.einsum("ijk,ikc->jkc", gate[pair], dmessage_blocks[dest]))
    dsource = dsource.astype(jnp.bfloat16).reshape(ROWS, LDEG, C)
    mix_part = grad_degree(hidden, dsource)
    return updated.reshape(ROWS, LDEG * C), mix_part, out_part


def reference(features, cotangent, send_order, pair_index, edge_mask, distance, radial_weight, mix_weight, out_weight):
    count = N_DP * N_BLK
    width = LDEG * C
    cap = ROWS // N_DP
    grid = features.reshape(N_DP, N_BLK, ROWS, width)
    order = send_order.reshape(N_DP, N_BLK, ROWS, 1).astype(jnp.int32)
    sent = jnp.take_along_axis(grid, order, axis=2)
    moved = sent.reshape(N_DP, N_BLK, N_DP, cap, width).transpose(2, 1, 0, 3, 4).reshape(count, ROWS, width)
    inputs = (moved, cotangent.reshape(count, ROWS, width), pair_index.reshape(count, PAIRS, 2).astype(jnp.int32),
              edge_mask.reshape(count, PAIRS, BLOCK, BLOCK), distance.reshape(count, PAIRS, BLOCK, BLOCK))

    def step(carry, item):
        rows, cot, pairs, mask, dist = item
        updated, mix_part, out_part = device_pass(rows, cot, pairs, mask, dist, radial_weight, mix_weight, out_weight)
        return (carry[0] + mix_part, carry[1] + out_part), updated

    zeros = jnp.zeros((WROWS, C), jnp.float32)
    totals, updated = lax.scan(step, (zeros, zeros), inputs)
    return updated.reshape(ATOMS, width), totals[0], totals[1]
```

```python
import functools
import math

import jax
import jax.numpy as jnp
import numpy as np
from jax import lax
from jax.experimental import pallas as pl
from jax.experimental.pallas import tpu as pltpu
from jax.sharding import PartitionSpec as P

LMAX = 4
LDEG = 25
BLOCK = 128
CUT_RADIUS = 5.0
EDGE_SCALE = 0.25
GROUPS = ((0, 1), (4,), (3,), (2,))
VMEM_LIMIT = 48 * 1024 * 1024


def params(*semantics):
    return pltpu.CompilerParams(dimension_semantics=semantics, vmem_limit_bytes=VMEM_LIMIT)


def span(degrees):
    return degrees[0] ** 2, (degrees[-1] + 1) ** 2


def regroup_kernel(order_ref, rows_ref, out_ref, pick_ref):
    @pl.when(pl.program_id(0) == 0)
    def _():
        local = lax.broadcasted_iota(jnp.int32, pick_ref.shape, 0)
        pick_ref[...] = (local == order_ref[...]).astype(jnp.float32).astype(jnp.bfloat16)

    out_ref[...] = lax.dot_general(
        pick_ref[...], rows_ref[...], (((0,), (0,)), ((), ())), preferred_element_type=jnp.float32
    ).astype(jnp.bfloat16)


def pick_rows(order, features, width, degrees):
    rows = features.shape[0]
    first, last = span(degrees)
    return pl.pallas_call(
        regroup_kernel,
        grid=(last - first,),
        in_specs=[
            pl.BlockSpec((1, rows), lambda i: (0, 0)),
            pl.BlockSpec((rows, width), lambda i: (0, first + i)),
        ],
        out_specs=pl.BlockSpec((rows, width), lambda i: (0, i)),
        out_shape=jax.ShapeDtypeStruct((rows, (last - first) * width), jnp.bfloat16),
        scratch_shapes=[pltpu.VMEM((rows, rows), jnp.bfloat16)],
        compiler_params=params("arbitrary"),
        name="pick_rows",
    )(order, features)


GATE_ROWS = 8


def gate_kernel(pairs_ref, mask_ref, dist_ref, weight_ref, out_ref, radial_ref, *, basis_count):
    pair, step = pl.program_id(0), pl.program_id(1)

    @pl.when((pair == 0) & (step == 0))
    def _():
        out_ref[...] = jnp.zeros_like(out_ref)

    half = math.sqrt(0.5)
    dist = dist_ref[0]
    scaled = dist * (half * (basis_count - 1) / CUT_RADIUS)
    centers = lax.broadcasted_iota(jnp.int32, (basis_count, BLOCK), 0).astype(jnp.float32) * half
    weights = weight_ref[...]
    levels = LMAX + 1
    for row in range(GATE_ROWS):
        offset = scaled[row : row + 1, :] - centers
        phi = jnp.exp(-(offset * offset))
        high = phi.astype(jnp.bfloat16)
        low = (phi - high.astype(jnp.float32)).astype(jnp.bfloat16)
        radial = jnp.dot(weights, high, preferred_element_type=jnp.float32)
        radial = radial + jnp.dot(weights, low, preferred_element_type=jnp.float32)
        radial = radial[0:8] + radial[8:16]
        for level in range(levels):
            radial_ref[level, row : row + 1, :] = radial[level : level + 1, :]
    envelope = (
        (0.5 * EDGE_SCALE)
        * (jnp.cos((math.pi / CUT_RADIUS) * dist) + 1.0)
        * mask_ref[0].astype(jnp.float32)
    )
    dest = pl.multiple_of(pairs_ref[pair, 0] * BLOCK + step * GATE_ROWS, GATE_ROWS)
    src = pl.multiple_of(pairs_ref[pair, 1] * BLOCK, BLOCK)
    for level in range(levels):
        out_ref[level, pl.ds(dest, GATE_ROWS), pl.ds(src, BLOCK)] = radial_ref[level] * envelope


def gate_matrices(pairs, mask, dist, radial_weight, rows):
    count = pairs.shape[0]
    levels = radial_weight.shape[1]
    transposed = radial_weight.T
    high = transposed.astype(jnp.bfloat16)
    low = (transposed - high.astype(jnp.float32)).astype(jnp.bfloat16)
    pad = ((0, 8 - levels), (0, 0))
    weights = jnp.concatenate([jnp.pad(high, pad), jnp.pad(low, pad)], axis=0)
    kernel = functools.partial(gate_kernel, basis_count=radial_weight.shape[0])
    wide = pl.pallas_call(
        kernel,
        grid_spec=pltpu.PrefetchScalarGridSpec(
            num_scalar_prefetch=1,
            grid=(count, BLOCK // GATE_ROWS),
            in_specs=[
                pl.BlockSpec((1, GATE_ROWS, BLOCK), lambda p, s, pairs: (p, s, 0)),
                pl.BlockSpec((1, GATE_ROWS, BLOCK), lambda p, s, pairs: (p, s, 0)),
                pl.BlockSpec(weights.shape, lambda p, s, pairs: (0, 0)),
            ],
            out_specs=pl.BlockSpec((levels, rows, rows), lambda p, s, pairs: (0, 0, 0)),
            scratch_shapes=[pltpu.VMEM((levels, GATE_ROWS, BLOCK), jnp.float32)],
        ),
        out_shape=jax.ShapeDtypeStruct((levels, rows, rows), jnp.float32),
        compiler_params=params("arbitrary", "arbitrary"),
        cost_estimate=pl.CostEstimate(
            flops=2 * 2 * 256 * count * BLOCK * BLOCK * radial_weight.shape[0],
            bytes_accessed=2 * 4 * count * BLOCK * BLOCK,
            transcendentals=count * BLOCK * BLOCK * radial_weight.shape[0],
        ),
        name="gate",
    )(pairs, mask, dist, weights)
    return wide.astype(jnp.bfloat16)


def product_kernel(left_ref, right_ref, out_ref):
    out_ref[...] = jnp.dot(
        left_ref[...], right_ref[...], preferred_element_type=jnp.float32
    ).astype(jnp.bfloat16)


def degree_products(left, right):
    width = left.shape[1]
    block = pl.BlockSpec((width, width), lambda i: (i, 0))
    return pl.pallas_call(
        product_kernel,
        grid=(left.shape[0] // width,),
        in_specs=[block, block],
        out_specs=block,
        out_shape=jax.ShapeDtypeStruct(left.shape, jnp.bfloat16),
        compiler_params=params("arbitrary"),
        name="degree_products",
    )(left, right)


def outer_kernel(gate_ref, rows_ref, cot_ref, out_ref, sum_ref):
    step = pl.program_id(0)
    mixed = jnp.dot(gate_ref[0], rows_ref[...], preferred_element_type=jnp.float32).astype(jnp.bfloat16)
    part = lax.dot_general(
        mixed, cot_ref[...], (((0,), (0,)), ((), ())), preferred_element_type=jnp.float32
    )

    @pl.when(step == 0)
    def _():
        sum_ref[...] = part

    @pl.when(step > 0)
    def _():
        sum_ref[...] += part

    @pl.when(step == pl.num_programs(0) - 1)
    def _():
        out_ref[...] = sum_ref[...].astype(jnp.bfloat16)


def outer_sum(gate, local, cotangent, width, level, base):
    rows = local.shape[0]
    first, last = span((level,))
    return pl.pallas_call(
        outer_kernel,
        grid=(last - first,),
        in_specs=[
            pl.BlockSpec((1, rows, rows), lambda i: (level, 0, 0)),
            pl.BlockSpec((rows, width), lambda i: (0, first - base + i)),
            pl.BlockSpec((rows, width), lambda i: (0, first + i)),
        ],
        out_specs=pl.BlockSpec((width, width), lambda i: (0, 0)),
        out_shape=jax.ShapeDtypeStruct((width, width), jnp.bfloat16),
        scratch_shapes=[pltpu.VMEM((width, width), jnp.float32)],
        compiler_params=params("arbitrary"),
        cost_estimate=pl.CostEstimate(
            flops=2 * (last - first) * rows * width * (rows + width),
            bytes_accessed=4 * (last - first) * rows * width,
            transcendentals=0,
        ),
        name="outer_sum",
    )(gate, local, cotangent)


def update_kernel(gate_ref, rows_ref, map_ref, *refs):
    out_ref = refs[-1]
    hidden = rows_ref[...]
    mixed = jnp.dot(gate_ref[0], hidden, preferred_element_type=jnp.float32).astype(jnp.bfloat16)
    added = jnp.dot(mixed, map_ref[...], preferred_element_type=jnp.float32)
    out_ref[...] = (hidden.astype(jnp.float32) + added).astype(jnp.bfloat16)


def update(gate, local, maps, width, degrees, total, held):
    rows = local.shape[0]
    base, last = span(degrees)

    def level_of(i):
        comp = base + i
        level = degrees[0]
        for other in degrees[1:]:
            level = level + (comp >= other * other).astype(jnp.int32)
        return level

    in_specs = [
        pl.BlockSpec((1, rows, rows), lambda i: (level_of(i), 0, 0)),
        pl.BlockSpec((rows, width), lambda i: (0, i)),
        pl.BlockSpec((width, width), lambda i: (level_of(i), 0)),
    ]
    operands = [gate, local, maps]
    aliases = {}
    if held is not None:
        in_specs.append(pl.BlockSpec(memory_space=pl.ANY))
        operands.append(held)
        aliases = {3: 0}
    return pl.pallas_call(
        update_kernel,
        grid=(last - base,),
        in_specs=in_specs,
        out_specs=pl.BlockSpec((rows, width), lambda i: (0, base + i)),
        out_shape=jax.ShapeDtypeStruct((rows, total), jnp.bfloat16),
        input_output_aliases=aliases,
        compiler_params=params("arbitrary"),
        cost_estimate=pl.CostEstimate(
            flops=2 * (last - base) * rows * width * (rows + width),
            bytes_accessed=4 * (last - base) * rows * width,
            transcendentals=0,
        ),
        name="update",
    )(*operands)


def summed(pieces, axis, count):
    rows, width = pieces.shape
    got = lax.all_to_all(pieces, axis, split_axis=0, concat_axis=0, tiled=True)
    return got.reshape(count, rows // count, width).astype(jnp.float32).sum(axis=0).astype(jnp.bfloat16)


def body(
    features,
    cotangent,
    send_order,
    pair_index,
    edge_mask,
    distance,
    radial_weight,
    mix_weight,
    out_weight,
    *,
    n_dp,
    n_blk,
):
    rows, total = features.shape
    width = mix_weight.shape[1]
    locals_ = []
    for degrees in GROUPS:
        sent = pick_rows(send_order, features, width, degrees)
        locals_.append(lax.all_to_all(sent, "dp", split_axis=0, concat_axis=0, tiled=True))
    gate = gate_matrices(pair_index, edge_mask, distance, radial_weight, rows)
    maps = degree_products(mix_weight, out_weight)
    updated = None
    outer = [None] * (LMAX + 1)
    for degrees, local in zip(GROUPS, locals_):
        base = span(degrees)[0]
        for level in degrees:
            part = outer_sum(gate, local, cotangent, width, level, base)
            owned = summed(summed(part, "blk", n_blk), "dp", n_dp)
            outer[level] = lax.all_gather(owned, ("blk", "dp"), axis=0, tiled=True)
        updated = update(gate, local, maps, width, degrees, total, updated)
    shard = mix_weight.shape[0] // n_blk
    start = lax.axis_index("blk") * shard
    stacked = jnp.concatenate(outer, axis=0)
    mine = lax.dynamic_slice_in_dim(stacked, start, shard, axis=0)
    flipped = mix_weight.reshape(LMAX + 1, width, width).swapaxes(1, 2).reshape(mix_weight.shape)
    maps_mine = lax.dynamic_slice_in_dim(flipped, start, shard, axis=0)
    piece = math.gcd(shard, width)
    mix_parts, out_parts = [], []
    for at in range(0, shard, piece):
        first = (start + at) // width * width
        left = lax.dynamic_slice_in_dim(out_weight, first, width, axis=0)
        right = lax.dynamic_slice_in_dim(stacked, first, width, axis=0)
        mix_parts.append(
            jnp.einsum("ed,cd->ec", mine[at : at + piece], left, preferred_element_type=jnp.float32)
        )
        out_parts.append(
            jnp.dot(maps_mine[at : at + piece], right, preferred_element_type=jnp.float32)
        )
    return updated, jnp.concatenate(mix_parts, axis=0), jnp.concatenate(out_parts, axis=0)


def solution(mesh):
    in_specs = (
        P(("dp", "blk"), None),
        P(("dp", "blk"), None),
        P(("dp", "blk"), None),
        P(("dp", "blk"), None),
        P(("dp", "blk"), None, None),
        P(("dp", "blk"), None, None),
        P(),
        P(),
        P(),
    )
    out_specs = (P(("dp", "blk"), None), P("blk", None), P("blk", None))
    run = functools.partial(body, n_dp=mesh.shape["dp"], n_blk=mesh.shape["blk"])
    return jax.shard_map(run, mesh=mesh, in_specs=in_specs, out_specs=out_specs, check_vma=False)
```

```python
import functools
import math

import jax
import jax.numpy as jnp
from jax import lax
from jax.experimental import pallas as pl
from jax.experimental.pallas import tpu as pltpu
from jax.sharding import PartitionSpec as P

LMAX = 4
BLOCK = 128
CUT_RADIUS = 5.0
EDGE_SCALE = 0.25
GROUPS = ((0, 1, 2), (4,), (3,))
VMEM_LIMIT = 48 * 1024 * 1024
GATE_ROWS = 16
WHOLE = pl.BlockSpec(memory_space=pltpu.VMEM)


def params(*semantics):
    return pltpu.CompilerParams(dimension_semantics=semantics, vmem_limit_bytes=VMEM_LIMIT)


def after(value, *others):
    return lax.optimization_barrier((value, *others))[0]


def span(degrees):
    return degrees[0] ** 2, (degrees[-1] + 1) ** 2


def tree_sum(parts):
    parts = [part.astype(jnp.float32) for part in parts]
    while len(parts) > 1:
        parts = [parts[i] + parts[i + 1] for i in range(0, len(parts), 2)]
    return parts[0].astype(jnp.bfloat16)


def pick_kernel(order_ref, rows_ref, out_ref, pick_ref):
    @pl.when(pl.program_id(0) == 0)
    def _():
        local = lax.broadcasted_iota(jnp.int32, pick_ref.shape, 0)
        pick_ref[...] = (local == order_ref[...]).astype(jnp.float32).astype(jnp.bfloat16)

    out_ref[...] = lax.dot_general(
        pick_ref[...], rows_ref[...], (((0,), (0,)), ((), ())), preferred_element_type=jnp.float32
    ).astype(jnp.bfloat16)


def pick_rows(order, features, width, degrees):
    rows = features.shape[0]
    first, last = span(degrees)
    per = 3 if math.gcd(first, last - first) % 3 == 0 else 1
    return pl.pallas_call(
        pick_kernel,
        grid=((last - first) // per,),
        in_specs=[
            pl.BlockSpec((1, rows), lambda i: (0, 0)),
            pl.BlockSpec((rows, per * width), lambda i: (0, first // per + i)),
        ],
        out_specs=pl.BlockSpec((rows, per * width), lambda i: (0, i)),
        out_shape=jax.ShapeDtypeStruct((rows, (last - first) * width), jnp.bfloat16),
        scratch_shapes=[pltpu.VMEM((rows, rows), jnp.bfloat16)],
        compiler_params=params("arbitrary"),
        name="pick_rows",
    )(order, features)


def gate_kernel(pairs_ref, mask_ref, dist_ref, weight_ref, out_ref, radial_ref, *, basis_count):
    pair, step = pl.program_id(0), pl.program_id(1)

    @pl.when((pair == 0) & (step == 0))
    def _():
        out_ref[...] = jnp.zeros_like(out_ref)

    half = math.sqrt(0.5)
    dist = dist_ref[0]
    scaled = dist * (half * (basis_count - 1) / CUT_RADIUS)
    centers = lax.broadcasted_iota(jnp.int32, (basis_count, BLOCK), 0).astype(jnp.float32) * half
    weights = weight_ref[...]
    levels = LMAX + 1
    for row in range(GATE_ROWS):
        offset = scaled[row : row + 1, :] - centers
        phi = jnp.exp(-(offset * offset))
        high = phi.astype(jnp.bfloat16)
        low = (phi - high.astype(jnp.float32)).astype(jnp.bfloat16)
        radial = jnp.dot(weights, high, preferred_element_type=jnp.float32)
        radial = radial + jnp.dot(weights, low, preferred_element_type=jnp.float32)
        radial = radial[0:8] + radial[8:16]
        for level in range(levels):
            radial_ref[level, row : row + 1, :] = radial[level : level + 1, :]
    envelope = (
        (0.5 * EDGE_SCALE)
        * (jnp.cos((math.pi / CUT_RADIUS) * dist) + 1.0)
        * mask_ref[0].astype(jnp.float32)
    )
    dest = pl.multiple_of(pairs_ref[pair, 0] * BLOCK + step * GATE_ROWS, GATE_ROWS)
    src = pl.multiple_of(pairs_ref[pair, 1] * BLOCK, BLOCK)
    for level in range(levels):
        out_ref[level, pl.ds(dest, GATE_ROWS), pl.ds(src, BLOCK)] = (
            radial_ref[level] * envelope
        ).astype(jnp.bfloat16)


def gate_matrices(pairs, mask, dist, radial_weight, rows):
    count = pairs.shape[0]
    levels = radial_weight.shape[1]
    transposed = radial_weight.T
    high = transposed.astype(jnp.bfloat16)
    low = (transposed - high.astype(jnp.float32)).astype(jnp.bfloat16)
    pad = ((0, 8 - levels), (0, 0))
    weights = jnp.concatenate([jnp.pad(high, pad), jnp.pad(low, pad)], axis=0)
    kernel = functools.partial(gate_kernel, basis_count=radial_weight.shape[0])
    edges = pl.BlockSpec((1, GATE_ROWS, BLOCK), lambda p, s, pairs: (p, s, 0))
    return pl.pallas_call(
        kernel,
        grid_spec=pltpu.PrefetchScalarGridSpec(
            num_scalar_prefetch=1,
            grid=(count, BLOCK // GATE_ROWS),
            in_specs=[edges, edges, pl.BlockSpec(weights.shape, lambda p, s, pairs: (0, 0))],
            out_specs=pl.BlockSpec((levels, rows, rows), lambda p, s, pairs: (0, 0, 0)),
            scratch_shapes=[pltpu.VMEM((levels, GATE_ROWS, BLOCK), jnp.float32)],
        ),
        out_shape=jax.ShapeDtypeStruct((levels, rows, rows), jnp.bfloat16),
        compiler_params=params("arbitrary", "arbitrary"),
        cost_estimate=pl.CostEstimate(
            flops=2 * 3 * 512 * count * BLOCK * BLOCK * radial_weight.shape[0],
            bytes_accessed=2 * 4 * count * BLOCK * BLOCK,
            transcendentals=count * BLOCK * BLOCK * radial_weight.shape[0],
        ),
        name="gate",
    )(pairs, mask, dist, weights)


def product_kernel(left_ref, right_ref, out_ref):
    out_ref[...] = jnp.dot(
        left_ref[...], right_ref[...], preferred_element_type=jnp.float32
    ).astype(jnp.bfloat16)


def degree_products(left, right):
    width = left.shape[1]
    block = pl.BlockSpec((width, width), lambda i: (i, 0))
    return pl.pallas_call(
        product_kernel,
        grid=(left.shape[0] // width,),
        in_specs=[block, block],
        out_specs=block,
        out_shape=jax.ShapeDtypeStruct(left.shape, jnp.bfloat16),
        compiler_params=params("arbitrary"),
        name="degree_products",
    )(left, right)


def flip_kernel(rows_ref, out_ref):
    out_ref[...] = rows_ref[...].astype(jnp.float32).T.astype(jnp.bfloat16)


def flip_cotangent(cotangent, width, level):
    rows = cotangent.shape[0]
    first, last = span((level,))
    return pl.pallas_call(
        flip_kernel,
        grid=(last - first,),
        in_specs=[pl.BlockSpec((rows, width), lambda i: (0, first + i))],
        out_specs=pl.BlockSpec((width, rows), lambda i: (0, i)),
        out_shape=jax.ShapeDtypeStruct((width, (last - first) * rows), jnp.bfloat16),
        compiler_params=params("arbitrary"),
        name="flip_cotangent",
    )(cotangent)


def outer_kernel(place_ref, gate_ref, local_ref, *refs, pieces, levels, base):
    count = len(levels)
    cots, outs = refs[:count], refs[count : count + pieces]
    mixed_ref, sum_ref = refs[count + pieces :]
    rows, width = local_ref.shape[0], mixed_ref.shape[1]
    for slot, level in enumerate(levels):
        first, last = span((level,))
        for comp in range(first, last):
            at = (comp - base) * width
            mixed_ref[(comp - first) * rows : (comp - first + 1) * rows, :] = jnp.dot(
                gate_ref[level], local_ref[:, at : at + width], preferred_element_type=jnp.float32
            ).astype(jnp.bfloat16)
        depth = (last - first) * rows
        flipped = jnp.dot(
            cots[slot][...], mixed_ref[0:depth, :], preferred_element_type=jnp.float32
        )
        sum_ref[slot * width : (slot + 1) * width, :] = flipped.T.astype(jnp.bfloat16)
    height = outs[0].shape[0]
    for step in range(pieces):
        row = pl.multiple_of((place_ref[0] ^ step) * height, height)
        outs[step][...] = sum_ref[pl.ds(row, height), :]


def outer_sum(place, gate, local, cots, width, degrees, pieces):
    rows = gate.shape[1]
    base = span(degrees)[0]
    height = len(degrees) * width // pieces
    deepest = 2 * degrees[-1] + 1
    total = sum(2 * level + 1 for level in degrees)
    return pl.pallas_call(
        functools.partial(outer_kernel, pieces=pieces, levels=degrees, base=base),
        in_specs=[pl.BlockSpec(memory_space=pltpu.SMEM)] + [WHOLE] * (2 + len(cots)),
        out_specs=[WHOLE] * pieces,
        out_shape=[jax.ShapeDtypeStruct((height, width), jnp.bfloat16)] * pieces,
        scratch_shapes=[
            pltpu.VMEM((deepest * rows, width), jnp.bfloat16),
            pltpu.VMEM((len(degrees) * width, width), jnp.bfloat16),
        ],
        compiler_params=params(),
        cost_estimate=pl.CostEstimate(
            flops=2 * total * rows * width * (rows + width),
            bytes_accessed=4 * total * rows * width,
            transcendentals=0,
        ),
        name="outer_sum",
    )(place, gate, local, *cots)


def update_kernel(gate_ref, map_ref, local_ref, *refs, degrees):
    out_ref, ready_ref, sems = refs[-3:]
    width = map_ref.shape[1]
    base, last = span(degrees)
    copies = []
    for comp in range(base, last):
        level = math.isqrt(comp)
        at = (comp - base) * width
        hidden = local_ref[:, at : at + width]
        mixed = jnp.dot(gate_ref[level], hidden, preferred_element_type=jnp.float32)
        added = jnp.dot(
            mixed.astype(jnp.bfloat16),
            map_ref[level * width : (level + 1) * width, :],
            preferred_element_type=jnp.float32,
        )
        ready_ref[comp - base] = (hidden.astype(jnp.float32) + added).astype(jnp.bfloat16)
        copies.append(
            pltpu.make_async_copy(
                ready_ref.at[comp - base],
                out_ref.at[:, pl.ds(comp * width, width)],
                sems.at[comp - base],
            )
        )
        copies[-1].start()
    for copy in copies:
        copy.wait()


def update(gate, maps, local, width, degrees, total, held):
    rows = gate.shape[1]
    base, last = span(degrees)
    in_specs = [WHOLE] * 3
    operands = [gate, maps, local]
    aliases = {}
    if held is not None:
        in_specs.append(pl.BlockSpec(memory_space=pl.ANY))
        operands.append(held)
        aliases = {3: 0}
    return pl.pallas_call(
        functools.partial(update_kernel, degrees=degrees),
        in_specs=in_specs,
        out_specs=pl.BlockSpec(memory_space=pl.ANY),
        out_shape=jax.ShapeDtypeStruct((rows, total), jnp.bfloat16),
        scratch_shapes=[
            pltpu.VMEM((last - base, rows, width), jnp.bfloat16),
            pltpu.SemaphoreType.DMA((last - base,)),
        ],
        input_output_aliases=aliases,
        compiler_params=params(),
        cost_estimate=pl.CostEstimate(
            flops=2 * (last - base) * rows * width * (rows + width),
            bytes_accessed=4 * (last - base) * rows * width,
            transcendentals=0,
        ),
        name="update",
    )(*operands)


def place_kernel(place_ref, *refs):
    parts, out_ref = refs[:-1], refs[-1]
    height = parts[0].shape[0]
    for step, part in enumerate(parts):
        row = pl.multiple_of((place_ref[0] ^ step) * height, height)
        out_ref[pl.ds(row, height), :] = part[...]


def placed(place, parts):
    height, width = parts[0].shape
    return pl.pallas_call(
        place_kernel,
        in_specs=[pl.BlockSpec(memory_space=pltpu.SMEM)] + [WHOLE] * len(parts),
        out_specs=WHOLE,
        out_shape=jax.ShapeDtypeStruct((height * len(parts), width), jnp.bfloat16),
        compiler_params=params(),
        name="placed",
    )(place, *parts)


def finish_kernel(place_ref, map_ref, flip_ref, *refs, groups, piece):
    count = len(groups) - 1
    earlier, parts = refs[:count], refs[count:-3]
    mix_ref, out_ref, outer_ref = refs[-3:]
    width = map_ref.shape[0]

    @pl.when(pl.program_id(0) == 0)
    def _():
        for degrees, value in zip(groups, earlier):
            outer_ref[degrees[0] * width : (degrees[-1] + 1) * width, :] = value[...]
        height = parts[0].shape[0]
        for step, part in enumerate(parts):
            row = groups[-1][0] * width + (place_ref[0] ^ step) * height
            outer_ref[pl.ds(pl.multiple_of(row, height), height), :] = part[...]

    row = pl.multiple_of((place_ref[1] + pl.program_id(0)) * piece, piece)
    first = pl.multiple_of(row // width * width, width)
    mix_ref[...] = lax.dot_general(
        outer_ref[pl.ds(row, piece), :],
        map_ref[...],
        (((1,), (1,)), ((), ())),
        preferred_element_type=jnp.float32,
    )
    out_ref[...] = jnp.dot(
        flip_ref[...], outer_ref[pl.ds(first, width), :], preferred_element_type=jnp.float32
    )


def finish(place, out_weight, flipped, earlier, parts, shard, piece):
    total, width = out_weight.shape
    mine = pl.BlockSpec((piece, width), lambda i, place: (place[1] + i, 0))
    whole = [pl.BlockSpec(value.shape, lambda i, place: (0, 0)) for value in (*earlier, *parts)]
    return pl.pallas_call(
        functools.partial(finish_kernel, groups=GROUPS, piece=piece),
        grid_spec=pltpu.PrefetchScalarGridSpec(
            num_scalar_prefetch=1,
            grid=(shard // piece,),
            in_specs=[
                pl.BlockSpec(
                    (width, width), lambda i, place: ((place[1] + i) * piece // width, 0)
                ),
                mine,
            ]
            + whole,
            out_specs=[pl.BlockSpec((piece, width), lambda i, place: (i, 0))] * 2,
            scratch_shapes=[pltpu.VMEM((total, width), jnp.bfloat16)],
        ),
        out_shape=[jax.ShapeDtypeStruct((shard, width), jnp.float32)] * 2,
        compiler_params=params("arbitrary"),
        name="finish",
    )(place, out_weight, flipped, *earlier, *parts)


def body(
    features,
    cotangent,
    send_order,
    pair_index,
    edge_mask,
    distance,
    radial_weight,
    mix_weight,
    out_weight,
    *,
    n_dp,
    n_blk,
):
    rows, total = features.shape
    width = mix_weight.shape[1]
    pieces = 2 * n_blk
    shard = mix_weight.shape[0] // n_blk
    piece = math.gcd(shard, width)
    at_dp, at_blk = lax.axis_index("dp"), lax.axis_index("blk")
    place = jnp.stack(
        [at_dp % 2 * n_blk + at_blk, at_blk * (shard // piece)]
    ).astype(jnp.int32)

    def over_dp(value, step):
        return lax.ppermute(value, "dp", [(i, i ^ step) for i in range(n_dp)])

    def over_plane(value, step):
        pairs = [
            (d * n_blk + b, (d ^ (step // n_blk)) * n_blk + (b ^ (step % n_blk)))
            for d in range(n_dp)
            for b in range(n_blk)
        ]
        return lax.ppermute(value, ("dp", "blk"), pairs)

    sent, came = [], []
    for degrees in GROUPS:
        source = after(features, sent[-1]) if sent else features
        sent.append(pick_rows(send_order, source, width, degrees))
    for value in sent:
        value = after(value, came[-1]) if came else value
        came.append(lax.all_to_all(value, "dp", split_axis=0, concat_axis=0, tiled=True))

    distance = after(distance, *sent)
    gate = gate_matrices(pair_index, edge_mask, distance, radial_weight, rows)
    cotangent, mix_weight, out_weight = lax.optimization_barrier(
        (cotangent, mix_weight, out_weight, gate)
    )[:3]
    cots = [flip_cotangent(cotangent, width, level) for level in range(LMAX + 1)]
    maps = degree_products(mix_weight, out_weight)
    flipped = mix_weight.reshape(LMAX + 1, width, width).swapaxes(1, 2).reshape(mix_weight.shape)
    ready = [gate, maps, flipped, *cots]
    updated = None
    earlier, gathered = [], []
    for degrees, local in zip(GROUPS, came):
        local = after(local, *ready)
        split = outer_sum(
            place, gate, local, [cots[level] for level in degrees], width, degrees, pieces
        )
        if gathered:
            split = lax.optimization_barrier((*split, *gathered))[:pieces]
        owned = tree_sum(
            [split[0]] + [over_plane(split[step], step) for step in range(1, pieces)]
        )
        owned = tree_sum([owned] + [over_dp(owned, 2 * step) for step in range(1, n_dp // 2)])
        gathered = [owned] + [over_plane(owned, step) for step in range(1, pieces)]
        if degrees != GROUPS[-1]:
            earlier.append(placed(place, gathered))
        updated = update(gate, maps, local, width, degrees, total, updated)
        ready = []
    mix_grad, out_grad = finish(place, out_weight, flipped, earlier, gathered, shard, piece)
    return updated, mix_grad, out_grad


def solution(mesh):
    in_specs = (
        P(("dp", "blk"), None),
        P(("dp", "blk"), None),
        P(("dp", "blk"), None),
        P(("dp", "blk"), None),
        P(("dp", "blk"), None, None),
        P(("dp", "blk"), None, None),
        P(),
        P(),
        P(),
    )
    out_specs = (P(("dp", "blk"), None), P("blk", None), P("blk", None))
    run = functools.partial(body, n_dp=mesh.shape["dp"], n_blk=mesh.shape["blk"])
    return jax.shard_map(run, mesh=mesh, in_specs=in_specs, out_specs=out_specs, check_vma=False)
```

```python
import functools
import math

import jax
import jax.numpy as jnp
from jax import lax
from jax.experimental import pallas as pl
from jax.experimental.pallas import tpu as pltpu
from jax.sharding import PartitionSpec as P

LMAX = 4
BLOCK = 128
CUT_RADIUS = 5.0
EDGE_SCALE = 0.25
GROUPS = ((0, 1, 2), (4,), (3,))
VMEM_LIMIT = 48 * 1024 * 1024
GATE_ROWS = 16
WHOLE = pl.BlockSpec(memory_space=pltpu.VMEM)


def params(*semantics):
    return pltpu.CompilerParams(dimension_semantics=semantics, vmem_limit_bytes=VMEM_LIMIT)


def after(value, *others):
    return lax.optimization_barrier((value, *others))[0]


def span(degrees):
    return degrees[0] ** 2, (degrees[-1] + 1) ** 2


def tree_sum(parts):
    parts = [part.astype(jnp.float32) for part in parts]
    while len(parts) > 1:
        parts = [parts[i] + parts[i + 1] for i in range(0, len(parts), 2)]
    return parts[0].astype(jnp.bfloat16)


def pick_kernel(order_ref, rows_ref, out_ref, pick_ref):
    @pl.when(pl.program_id(0) == 0)
    def _():
        local = lax.broadcasted_iota(jnp.int32, pick_ref.shape, 0)
        pick_ref[...] = (local == order_ref[...]).astype(jnp.float32).astype(jnp.bfloat16)

    out_ref[...] = lax.dot_general(
        pick_ref[...], rows_ref[...], (((0,), (0,)), ((), ())), preferred_element_type=jnp.float32
    ).astype(jnp.bfloat16)


def pick_rows(order, features, width, degrees):
    rows = features.shape[0]
    first, last = span(degrees)
    per = 3 if math.gcd(first, last - first) % 3 == 0 else 1
    return pl.pallas_call(
        pick_kernel,
        grid=((last - first) // per,),
        in_specs=[
            pl.BlockSpec((1, rows), lambda i: (0, 0)),
            pl.BlockSpec((rows, per * width), lambda i: (0, first // per + i)),
        ],
        out_specs=pl.BlockSpec((rows, per * width), lambda i: (0, i)),
        out_shape=jax.ShapeDtypeStruct((rows, (last - first) * width), jnp.bfloat16),
        scratch_shapes=[pltpu.VMEM((rows, rows), jnp.bfloat16)],
        compiler_params=params("arbitrary"),
        name="pick_rows",
    )(order, features)


def gate_kernel(pairs_ref, mask_ref, dist_ref, weight_ref, out_ref, radial_ref, *, basis_count):
    pair, step = pl.program_id(0), pl.program_id(1)

    @pl.when((pair == 0) & (step == 0))
    def _():
        out_ref[...] = jnp.zeros_like(out_ref)

    half = math.sqrt(0.5)
    dist = dist_ref[0]
    scaled = dist * (half * (basis_count - 1) / CUT_RADIUS)
    centers = lax.broadcasted_iota(jnp.int32, (basis_count, BLOCK), 0).astype(jnp.float32) * half
    weights = weight_ref[...]
    levels = LMAX + 1
    for row in range(GATE_ROWS):
        offset = scaled[row : row + 1, :] - centers
        phi = jnp.exp(-(offset * offset))
        high = phi.astype(jnp.bfloat16)
        low = (phi - high.astype(jnp.float32)).astype(jnp.bfloat16)
        radial = jnp.dot(weights, high, preferred_element_type=jnp.float32)
        radial = radial + jnp.dot(weights, low, preferred_element_type=jnp.float32)
        radial = radial[0:8] + radial[8:16]
        for level in range(levels):
            radial_ref[level, row : row + 1, :] = radial[level : level + 1, :]
    envelope = (
        (0.5 * EDGE_SCALE)
        * (jnp.cos((math.pi / CUT_RADIUS) * dist) + 1.0)
        * mask_ref[0].astype(jnp.float32)
    )
    dest = pl.multiple_of(pairs_ref[pair, 0] * BLOCK + step * GATE_ROWS, GATE_ROWS)
    src = pl.multiple_of(pairs_ref[pair, 1] * BLOCK, BLOCK)
    for level in range(levels):
        out_ref[level, pl.ds(dest, GATE_ROWS), pl.ds(src, BLOCK)] = (
            radial_ref[level] * envelope
        ).astype(jnp.bfloat16)


def gate_matrices(pairs, mask, dist, radial_weight, rows):
    count = pairs.shape[0]
    levels = radial_weight.shape[1]
    transposed = radial_weight.T
    high = transposed.astype(jnp.bfloat16)
    low = (transposed - high.astype(jnp.float32)).astype(jnp.bfloat16)
    pad = ((0, 8 - levels), (0, 0))
    weights = jnp.concatenate([jnp.pad(high, pad), jnp.pad(low, pad)], axis=0)
    kernel = functools.partial(gate_kernel, basis_count=radial_weight.shape[0])
    edges = pl.BlockSpec((1, GATE_ROWS, BLOCK), lambda p, s, pairs: (p, s, 0))
    return pl.pallas_call(
        kernel,
        grid_spec=pltpu.PrefetchScalarGridSpec(
            num_scalar_prefetch=1,
            grid=(count, BLOCK // GATE_ROWS),
            in_specs=[edges, edges, pl.BlockSpec(weights.shape, lambda p, s, pairs: (0, 0))],
            out_specs=pl.BlockSpec((levels, rows, rows), lambda p, s, pairs: (0, 0, 0)),
            scratch_shapes=[pltpu.VMEM((levels, GATE_ROWS, BLOCK), jnp.float32)],
        ),
        out_shape=jax.ShapeDtypeStruct((levels, rows, rows), jnp.bfloat16),
        compiler_params=params("arbitrary", "arbitrary"),
        cost_estimate=pl.CostEstimate(
            flops=2 * 3 * 512 * count * BLOCK * BLOCK * radial_weight.shape[0],
            bytes_accessed=2 * 4 * count * BLOCK * BLOCK,
            transcendentals=count * BLOCK * BLOCK * radial_weight.shape[0],
        ),
        name="gate",
    )(pairs, mask, dist, weights)


def product_kernel(left_ref, right_ref, out_ref):
    out_ref[...] = jnp.dot(
        left_ref[...], right_ref[...], preferred_element_type=jnp.float32
    ).astype(jnp.bfloat16)


def degree_products(left, right):
    width = left.shape[1]
    block = pl.BlockSpec((width, width), lambda i: (i, 0))
    return pl.pallas_call(
        product_kernel,
        grid=(left.shape[0] // width,),
        in_specs=[block, block],
        out_specs=block,
        out_shape=jax.ShapeDtypeStruct(left.shape, jnp.bfloat16),
        compiler_params=params("arbitrary"),
        name="degree_products",
    )(left, right)


def flip_kernel(rows_ref, out_ref):
    out_ref[...] = rows_ref[...].astype(jnp.float32).T.astype(jnp.bfloat16)


def flip_cotangent(cotangent, width, level):
    rows = cotangent.shape[0]
    first, last = span((level,))
    return pl.pallas_call(
        flip_kernel,
        grid=(last - first,),
        in_specs=[pl.BlockSpec((rows, width), lambda i: (0, first + i))],
        out_specs=pl.BlockSpec((width, rows), lambda i: (0, i)),
        out_shape=jax.ShapeDtypeStruct((width, (last - first) * rows), jnp.bfloat16),
        compiler_params=params("arbitrary"),
        name="flip_cotangent",
    )(cotangent)


def outer_kernel(place_ref, gate_ref, local_ref, *refs, pieces, levels, base):
    count = len(levels)
    cots = refs[:count]
    near_ref, far_ref, mixed_ref, sum_ref = refs[count:]
    rows, width = local_ref.shape[0], mixed_ref.shape[1]
    for slot, level in enumerate(levels):
        first, last = span((level,))
        for comp in range(first, last):
            at = (comp - base) * width
            mixed_ref[(comp - first) * rows : (comp - first + 1) * rows, :] = jnp.dot(
                gate_ref[level], local_ref[:, at : at + width], preferred_element_type=jnp.float32
            ).astype(jnp.bfloat16)
        depth = (last - first) * rows
        flipped = jnp.dot(
            cots[slot][...], mixed_ref[0:depth, :], preferred_element_type=jnp.float32
        )
        sum_ref[slot * width : (slot + 1) * width, :] = flipped.T
    half = pieces // 2
    height = near_ref.shape[0] // half
    for step in range(half):
        to = slice(step * height, (step + 1) * height)
        row = pl.multiple_of((place_ref[0] ^ step) * height, height)
        near_ref[to, :] = sum_ref[pl.ds(row, height), :]
        row = pl.multiple_of((place_ref[0] ^ (step + half)) * height, height)
        far_ref[to, :] = sum_ref[pl.ds(row, height), :].astype(jnp.bfloat16)


def outer_sum(place, gate, local, cots, width, degrees, pieces):
    rows = gate.shape[1]
    base = span(degrees)[0]
    half = len(degrees) * width // 2
    deepest = 2 * degrees[-1] + 1
    total = sum(2 * level + 1 for level in degrees)
    return pl.pallas_call(
        functools.partial(outer_kernel, pieces=pieces, levels=degrees, base=base),
        in_specs=[pl.BlockSpec(memory_space=pltpu.SMEM)] + [WHOLE] * (2 + len(cots)),
        out_specs=[WHOLE] * 2,
        out_shape=[
            jax.ShapeDtypeStruct((half, width), jnp.float32),
            jax.ShapeDtypeStruct((half, width), jnp.bfloat16),
        ],
        scratch_shapes=[
            pltpu.VMEM((deepest * rows, width), jnp.bfloat16),
            pltpu.VMEM((len(degrees) * width, width), jnp.float32),
        ],
        compiler_params=params(),
        cost_estimate=pl.CostEstimate(
            flops=2 * total * rows * width * (rows + width),
            bytes_accessed=4 * total * rows * width,
            transcendentals=0,
        ),
        name="outer_sum",
    )(place, gate, local, *cots)


def update_kernel(gate_ref, map_ref, local_ref, *refs, degrees):
    out_ref, ready_ref, sems = refs[-3:]
    width = map_ref.shape[1]
    base, last = span(degrees)
    copies = []
    for comp in range(base, last):
        level = math.isqrt(comp)
        at = (comp - base) * width
        hidden = local_ref[:, at : at + width]
        mixed = jnp.dot(gate_ref[level], hidden, preferred_element_type=jnp.float32)
        added = jnp.dot(
            mixed.astype(jnp.bfloat16),
            map_ref[level * width : (level + 1) * width, :],
            preferred_element_type=jnp.float32,
        )
        ready_ref[comp - base] = (hidden.astype(jnp.float32) + added).astype(jnp.bfloat16)
        copies.append(
            pltpu.make_async_copy(
                ready_ref.at[comp - base],
                out_ref.at[:, pl.ds(comp * width, width)],
                sems.at[comp - base],
            )
        )
        copies[-1].start()
    for copy in copies:
        copy.wait()


def update(gate, maps, local, width, degrees, total, held):
    rows = gate.shape[1]
    base, last = span(degrees)
    in_specs = [WHOLE] * 3
    operands = [gate, maps, local]
    aliases = {}
    if held is not None:
        in_specs.append(pl.BlockSpec(memory_space=pl.ANY))
        operands.append(held)
        aliases = {3: 0}
    return pl.pallas_call(
        functools.partial(update_kernel, degrees=degrees),
        in_specs=in_specs,
        out_specs=pl.BlockSpec(memory_space=pl.ANY),
        out_shape=jax.ShapeDtypeStruct((rows, total), jnp.bfloat16),
        scratch_shapes=[
            pltpu.VMEM((last - base, rows, width), jnp.bfloat16),
            pltpu.SemaphoreType.DMA((last - base,)),
        ],
        input_output_aliases=aliases,
        compiler_params=params(),
        cost_estimate=pl.CostEstimate(
            flops=2 * (last - base) * rows * width * (rows + width),
            bytes_accessed=4 * (last - base) * rows * width,
            transcendentals=0,
        ),
        name="update",
    )(*operands)


def finish_kernel(place_ref, map_ref, flip_ref, *refs, piece, pieces):
    halves = refs[:-3]
    mix_ref, out_ref, outer_ref = refs[-3:]
    width = map_ref.shape[0]

    @pl.when(pl.program_id(0) == 0)
    def _():
        for index, degrees in enumerate(GROUPS):
            height = len(degrees) * width // pieces
            for step in range(pieces):
                value = halves[2 * index + step // (pieces // 2)]
                at = step % (pieces // 2) * height
                row = degrees[0] * width + (place_ref[0] ^ step) * height
                outer_ref[pl.ds(pl.multiple_of(row, height), height), :] = value[
                    at : at + height, :
                ]

    row = pl.multiple_of((place_ref[1] + pl.program_id(0)) * piece, piece)
    first = pl.multiple_of(row // width * width, width)
    mix_ref[...] = lax.dot_general(
        outer_ref[pl.ds(row, piece), :],
        map_ref[...],
        (((1,), (1,)), ((), ())),
        preferred_element_type=jnp.float32,
    )
    out_ref[...] = jnp.dot(
        flip_ref[...], outer_ref[pl.ds(first, width), :], preferred_element_type=jnp.float32
    )


def finish(place, out_weight, flipped, halves, shard, piece, pieces):
    total, width = out_weight.shape
    mine = pl.BlockSpec((piece, width), lambda i, place: (place[1] + i, 0))
    whole = [pl.BlockSpec(value.shape, lambda i, place: (0, 0)) for value in halves]
    return pl.pallas_call(
        functools.partial(finish_kernel, piece=piece, pieces=pieces),
        grid_spec=pltpu.PrefetchScalarGridSpec(
            num_scalar_prefetch=1,
            grid=(shard // piece,),
            in_specs=[
                pl.BlockSpec(
                    (width, width), lambda i, place: ((place[1] + i) * piece // width, 0)
                ),
                mine,
            ]
            + whole,
            out_specs=[pl.BlockSpec((piece, width), lambda i, place: (i, 0))] * 2,
            scratch_shapes=[pltpu.VMEM((total, width), jnp.bfloat16)],
        ),
        out_shape=[jax.ShapeDtypeStruct((shard, width), jnp.float32)] * 2,
        compiler_params=params("arbitrary"),
        name="finish",
    )(place, out_weight, flipped, *halves)


def body(
    features,
    cotangent,
    send_order,
    pair_index,
    edge_mask,
    distance,
    radial_weight,
    mix_weight,
    out_weight,
    *,
    n_dp,
    n_blk,
):
    rows, total = features.shape
    width = mix_weight.shape[1]
    pieces = 2 * n_blk
    shard = mix_weight.shape[0] // n_blk
    piece = math.gcd(shard, width)
    at_dp, at_blk = lax.axis_index("dp"), lax.axis_index("blk")
    place = jnp.stack(
        [at_dp % 2 * n_blk + at_blk, at_blk * (shard // piece)]
    ).astype(jnp.int32)

    def over_dp(value, step):
        return lax.ppermute(value, "dp", [(i, i ^ step) for i in range(n_dp)])

    def over_blk(value, step):
        return lax.ppermute(value, "blk", [(i, i ^ step) for i in range(n_blk)])

    def sum_everywhere(near, far):
        height = near.shape[0] // n_blk
        chip = near + over_dp(far, 1).astype(jnp.float32)
        own = chip[:height]
        for step in range(1, n_blk):
            sent_part = chip[step * height : (step + 1) * height].astype(jnp.bfloat16)
            own = own + over_blk(sent_part, step).astype(jnp.float32)
        own = own.astype(jnp.bfloat16)
        own = tree_sum([own] + [over_dp(own, 2 * step) for step in range(1, n_dp // 2)])
        near = jnp.concatenate([own] + [over_blk(own, step) for step in range(1, n_blk)], axis=0)
        return near, over_dp(near, 1)

    sent, came = [], []
    for degrees in GROUPS:
        source = after(features, sent[-1]) if sent else features
        sent.append(pick_rows(send_order, source, width, degrees))

    gate = gate_matrices(pair_index, edge_mask, after(distance, *sent), radial_weight, rows)
    cotangent, mix_weight, out_weight = lax.optimization_barrier(
        (cotangent, mix_weight, out_weight, gate)
    )[:3]
    cots = [flip_cotangent(cotangent, width, level) for level in range(LMAX + 1)]
    maps = degree_products(mix_weight, out_weight)
    flipped = mix_weight.reshape(LMAX + 1, width, width).swapaxes(1, 2).reshape(mix_weight.shape)
    updated = None
    waits = [gate]
    halves = []
    for index, degrees in enumerate(GROUPS):
        if index == 0:
            came = lax.all_to_all(sent[0], "dp", split_axis=0, concat_axis=0, tiled=True)
        local = came
        if index + 1 < len(GROUPS):
            following = after(sent[index + 1], came, *waits)
            came = lax.all_to_all(following, "dp", split_axis=0, concat_axis=0, tiled=True)
        if index == 0:
            local = after(local, gate, maps, flipped, *cots)
        near, far = outer_sum(
            place, gate, local, [cots[level] for level in degrees], width, degrees, pieces
        )
        if halves:
            near, far = lax.optimization_barrier((near, far, *halves))[:2]
        halves.extend(sum_everywhere(near, far))
        updated = update(gate, maps, local, width, degrees, total, updated)
        waits = [updated, halves[-1]]
    mix_grad, out_grad = finish(place, out_weight, flipped, halves, shard, piece, pieces)
    return updated, mix_grad, out_grad


def solution(mesh):
    in_specs = (
        P(("dp", "blk"), None),
        P(("dp", "blk"), None),
        P(("dp", "blk"), None),
        P(("dp", "blk"), None),
        P(("dp", "blk"), None, None),
        P(("dp", "blk"), None, None),
        P(),
        P(),
        P(),
    )
    out_specs = (P(("dp", "blk"), None), P("blk", None), P("blk", None))
    run = functools.partial(body, n_dp=mesh.shape["dp"], n_blk=mesh.shape["blk"])
    return jax.shard_map(run, mesh=mesh, in_specs=in_specs, out_specs=out_specs, check_vma=False)
```

```python
import functools
import math

import jax
import jax.numpy as jnp
from jax import lax
from jax.experimental import pallas as pl
from jax.experimental.pallas import tpu as pltpu
from jax.sharding import PartitionSpec as P

LMAX = 4
BLOCK = 128
CUT_RADIUS = 5.0
EDGE_SCALE = 0.25
FIRST, SECOND, SPREAD, LAST = (4,), (3,), (0, 1), (2,)
ORDER = FIRST + SPREAD + SECOND + LAST
VMEM_LIMIT = 48 * 1024 * 1024
GATE_ROWS = 16
WHOLE = pl.BlockSpec(memory_space=pltpu.VMEM)
ANY = pl.BlockSpec(memory_space=pl.ANY)
SCALARS = pl.BlockSpec(memory_space=pltpu.SMEM)


def params(*semantics):
    return pltpu.CompilerParams(dimension_semantics=semantics, vmem_limit_bytes=VMEM_LIMIT)


def after(value, *others):
    return lax.optimization_barrier((value, *others))[0]


def span(degrees):
    return degrees[0] ** 2, (degrees[-1] + 1) ** 2


def tree_sum(parts):
    parts = [part.astype(jnp.float32) for part in parts]
    while len(parts) > 1:
        parts = [parts[i] + parts[i + 1] for i in range(0, len(parts), 2)]
    return parts[0].astype(jnp.bfloat16)


def chosen_rows(order_ref, rows):
    local = lax.broadcasted_iota(jnp.int32, (rows, rows), 0)
    return (local == order_ref[...]).astype(jnp.float32).T.astype(jnp.bfloat16)


def column_copies(source, held_ref, sems, first, width):
    return [
        pltpu.make_async_copy(
            source.at[:, pl.ds((first + i) * width, width)], held_ref.at[i], sems.at[i]
        )
        for i in range(held_ref.shape[0])
    ]


def pick_kernel(order_ref, rows_ref, out_ref, held_ref, ready_ref, in_sems, out_sems, *, first):
    count, rows, width = held_ref.shape
    loads = column_copies(rows_ref, held_ref, in_sems, first, width)
    for load in loads:
        load.start()
    pick = chosen_rows(order_ref, rows)
    stores = []
    for i in range(count):
        loads[i].wait()
        ready_ref[i] = jnp.dot(pick, held_ref[i], preferred_element_type=jnp.float32).astype(
            jnp.bfloat16
        )
        stores.append(
            pltpu.make_async_copy(
                ready_ref.at[i], out_ref.at[:, pl.ds(i * width, width)], out_sems.at[i]
            )
        )
        stores[-1].start()
    for store in stores:
        store.wait()


def pick_rows(order, features, width, degrees):
    rows = features.shape[0]
    first, last = span(degrees)
    count = last - first
    return pl.pallas_call(
        functools.partial(pick_kernel, first=first),
        in_specs=[WHOLE, ANY],
        out_specs=ANY,
        out_shape=jax.ShapeDtypeStruct((rows, count * width), jnp.bfloat16),
        scratch_shapes=[
            pltpu.VMEM((count, rows, width), jnp.bfloat16),
            pltpu.VMEM((count, rows, width), jnp.bfloat16),
            pltpu.SemaphoreType.DMA((count,)),
            pltpu.SemaphoreType.DMA((count,)),
        ],
        compiler_params=params(),
        name="pick_rows",
    )(order, features)


def pick_pieces_kernel(place_ref, order_ref, rows_ref, *refs, n_dp, first):
    outs = refs[:n_dp]
    held_ref, ready_ref, in_sems = refs[n_dp:]
    count, rows, width = held_ref.shape
    loads = column_copies(rows_ref, held_ref, in_sems, first, width)
    for load in loads:
        load.start()
    pick = chosen_rows(order_ref, rows)
    for i in range(count):
        loads[i].wait()
        ready_ref[:, i * width : (i + 1) * width] = jnp.dot(
            pick, held_ref[i], preferred_element_type=jnp.float32
        ).astype(jnp.bfloat16)
    cap = rows // n_dp
    for step in range(n_dp):
        row = pl.multiple_of((place_ref[2] ^ step) * cap, cap)
        outs[step][...] = ready_ref[pl.ds(row, cap), :]


def pick_pieces(place, order, features, width, degrees, n_dp):
    rows = features.shape[0]
    first, last = span(degrees)
    count = last - first
    return pl.pallas_call(
        functools.partial(pick_pieces_kernel, n_dp=n_dp, first=first),
        in_specs=[SCALARS, WHOLE, ANY],
        out_specs=[WHOLE] * n_dp,
        out_shape=[jax.ShapeDtypeStruct((rows // n_dp, count * width), jnp.bfloat16)] * n_dp,
        scratch_shapes=[
            pltpu.VMEM((count, rows, width), jnp.bfloat16),
            pltpu.VMEM((rows, count * width), jnp.bfloat16),
            pltpu.SemaphoreType.DMA((count,)),
        ],
        compiler_params=params(),
        name="pick_pieces",
    )(place, order, features)


def join_kernel(place_ref, *refs):
    parts, out_ref = refs[:-1], refs[-1]
    cap = parts[0].shape[0]
    for step, part in enumerate(parts):
        row = pl.multiple_of((place_ref[2] ^ step) * cap, cap)
        out_ref[pl.ds(row, cap), :] = part[...]


def join_pieces(place, parts):
    cap, width = parts[0].shape
    return pl.pallas_call(
        join_kernel,
        in_specs=[SCALARS] + [WHOLE] * len(parts),
        out_specs=WHOLE,
        out_shape=jax.ShapeDtypeStruct((cap * len(parts), width), jnp.bfloat16),
        compiler_params=params(),
        name="join_pieces",
    )(place, *parts)


def gate_kernel(pairs_ref, mask_ref, dist_ref, weight_ref, out_ref, radial_ref, *, basis_count):
    pair, step = pl.program_id(0), pl.program_id(1)

    @pl.when((pair == 0) & (step == 0))
    def _():
        out_ref[...] = jnp.zeros_like(out_ref)

    half = math.sqrt(0.5 * math.log2(math.e))
    dist = dist_ref[0]
    scaled = dist * (half * (basis_count - 1) / CUT_RADIUS)
    centers = lax.broadcasted_iota(jnp.int32, (basis_count, BLOCK), 0).astype(jnp.float32) * half
    weights = weight_ref[...]
    levels = LMAX + 1
    for row in range(GATE_ROWS):
        offset = scaled[row : row + 1, :] - centers
        phi = jnp.exp2(-(offset * offset))
        high = phi.astype(jnp.bfloat16)
        low = (phi - high.astype(jnp.float32)).astype(jnp.bfloat16)
        radial = jnp.dot(weights, high, preferred_element_type=jnp.float32)
        radial = radial + jnp.dot(weights, low, preferred_element_type=jnp.float32)
        radial = radial[0:8] + radial[8:16]
        for level in range(levels):
            radial_ref[level, row : row + 1, :] = radial[level : level + 1, :]
    envelope = (
        (0.5 * EDGE_SCALE)
        * (jnp.cos((math.pi / CUT_RADIUS) * dist) + 1.0)
        * mask_ref[0].astype(jnp.float32)
    )
    dest = pl.multiple_of(pairs_ref[pair, 0] * BLOCK + step * GATE_ROWS, GATE_ROWS)
    src = pl.multiple_of(pairs_ref[pair, 1] * BLOCK, BLOCK)
    for level in range(levels):
        out_ref[level, pl.ds(dest, GATE_ROWS), pl.ds(src, BLOCK)] = (
            radial_ref[level] * envelope
        ).astype(jnp.bfloat16)


def gate_matrices(pairs, mask, dist, radial_weight, rows):
    count = pairs.shape[0]
    levels = radial_weight.shape[1]
    transposed = radial_weight.T
    high = transposed.astype(jnp.bfloat16)
    low = (transposed - high.astype(jnp.float32)).astype(jnp.bfloat16)
    pad = ((0, 8 - levels), (0, 0))
    weights = jnp.concatenate([jnp.pad(high, pad), jnp.pad(low, pad)], axis=0)
    kernel = functools.partial(gate_kernel, basis_count=radial_weight.shape[0])
    edges = pl.BlockSpec((1, GATE_ROWS, BLOCK), lambda p, s, pairs: (p, s, 0))
    return pl.pallas_call(
        kernel,
        grid_spec=pltpu.PrefetchScalarGridSpec(
            num_scalar_prefetch=1,
            grid=(count, BLOCK // GATE_ROWS),
            in_specs=[edges, edges, pl.BlockSpec(weights.shape, lambda p, s, pairs: (0, 0))],
            out_specs=pl.BlockSpec((levels, rows, rows), lambda p, s, pairs: (0, 0, 0)),
            scratch_shapes=[pltpu.VMEM((levels, GATE_ROWS, BLOCK), jnp.float32)],
        ),
        out_shape=jax.ShapeDtypeStruct((levels, rows, rows), jnp.bfloat16),
        compiler_params=params("arbitrary", "arbitrary"),
        cost_estimate=pl.CostEstimate(
            flops=2 * 3 * 512 * count * BLOCK * BLOCK * radial_weight.shape[0],
            bytes_accessed=2 * 4 * count * BLOCK * BLOCK,
            transcendentals=count * BLOCK * BLOCK * radial_weight.shape[0],
        ),
        name="gate",
    )(pairs, mask, dist, weights)


def product_kernel(left_ref, right_ref, out_ref):
    out_ref[...] = jnp.dot(
        left_ref[...], right_ref[...], preferred_element_type=jnp.float32
    ).astype(jnp.bfloat16)


def degree_products(left, right):
    width = left.shape[1]
    block = pl.BlockSpec((width, width), lambda i: (i, 0))
    return pl.pallas_call(
        product_kernel,
        grid=(left.shape[0] // width,),
        in_specs=[block, block],
        out_specs=block,
        out_shape=jax.ShapeDtypeStruct(left.shape, jnp.bfloat16),
        compiler_params=params("arbitrary"),
        name="degree_products",
    )(left, right)


def flip_kernel(rows_ref, out_ref):
    out_ref[...] = rows_ref[...].T


def flip_cotangent(cotangent, width, level):
    rows = cotangent.shape[0]
    first, last = span((level,))
    return pl.pallas_call(
        flip_kernel,
        grid=(last - first,),
        in_specs=[pl.BlockSpec((rows, width), lambda i: (0, first + i))],
        out_specs=pl.BlockSpec((width, rows), lambda i: (0, i)),
        out_shape=jax.ShapeDtypeStruct((width, (last - first) * rows), jnp.bfloat16),
        compiler_params=params("arbitrary"),
        name="flip_cotangent",
    )(cotangent)


def outer_kernel(place_ref, gate_ref, *refs, pieces, groups):
    levels = sum(groups, ())
    locals_, cots = refs[: len(groups)], refs[len(groups) : len(groups) + len(levels)]
    near_ref, far_ref, mixed_ref, sum_ref = refs[len(groups) + len(levels) :]
    rows, width = locals_[0].shape[0], mixed_ref.shape[1]
    slot = 0
    for local_ref, degrees in zip(locals_, groups):
        base = span(degrees)[0]
        for level in degrees:
            first, last = span((level,))
            for comp in range(first, last):
                at = (comp - base) * width
                mixed_ref[(comp - first) * rows : (comp - first + 1) * rows, :] = jnp.dot(
                    gate_ref[level],
                    local_ref[:, at : at + width],
                    preferred_element_type=jnp.float32,
                ).astype(jnp.bfloat16)
            depth = (last - first) * rows
            flipped = jnp.dot(
                cots[slot][...], mixed_ref[0:depth, :], preferred_element_type=jnp.float32
            )
            sum_ref[slot * width : (slot + 1) * width, :] = flipped.T
            slot += 1
    half = pieces // 2
    height = near_ref.shape[0] // half
    for step in range(half):
        to = slice(step * height, (step + 1) * height)
        row = pl.multiple_of((place_ref[0] ^ step) * height, height)
        near_ref[to, :] = sum_ref[pl.ds(row, height), :]
        row = pl.multiple_of((place_ref[0] ^ (step + half)) * height, height)
        far_ref[to, :] = sum_ref[pl.ds(row, height), :].astype(jnp.bfloat16)


def outer_sum(place, gate, locals_, cots, width, groups, pieces):
    rows = gate.shape[1]
    levels = sum(groups, ())
    half = len(levels) * width // 2
    deepest = 2 * max(levels) + 1
    total = sum(2 * level + 1 for level in levels)
    return pl.pallas_call(
        functools.partial(outer_kernel, pieces=pieces, groups=groups),
        in_specs=[SCALARS] + [WHOLE] * (1 + len(locals_) + len(levels)),
        out_specs=[WHOLE] * 2,
        out_shape=[
            jax.ShapeDtypeStruct((half, width), jnp.float32),
            jax.ShapeDtypeStruct((half, width), jnp.bfloat16),
        ],
        scratch_shapes=[
            pltpu.VMEM((deepest * rows, width), jnp.bfloat16),
            pltpu.VMEM((len(levels) * width, width), jnp.float32),
        ],
        compiler_params=params(),
        cost_estimate=pl.CostEstimate(
            flops=2 * total * rows * width * (rows + width),
            bytes_accessed=4 * total * rows * width,
            transcendentals=0,
        ),
        name="outer_sum",
    )(place, gate, *locals_, *[cots[level] for level in levels])


def update_kernel(gate_ref, map_ref, local_ref, *refs, degrees):
    out_ref, ready_ref, sems = refs[-3:]
    width = map_ref.shape[1]
    base, last = span(degrees)
    copies = []
    for comp in range(base, last):
        level = math.isqrt(comp)
        at = (comp - base) * width
        hidden = local_ref[:, at : at + width]
        mixed = jnp.dot(gate_ref[level], hidden, preferred_element_type=jnp.float32)
        added = jnp.dot(
            mixed.astype(jnp.bfloat16),
            map_ref[level * width : (level + 1) * width, :],
            preferred_element_type=jnp.float32,
        )
        ready_ref[comp - base] = (hidden.astype(jnp.float32) + added).astype(jnp.bfloat16)
        copies.append(
            pltpu.make_async_copy(
                ready_ref.at[comp - base],
                out_ref.at[:, pl.ds(comp * width, width)],
                sems.at[comp - base],
            )
        )
        copies[-1].start()
    for copy in copies:
        copy.wait()


def update(gate, maps, local, width, degrees, total, held):
    rows = gate.shape[1]
    base, last = span(degrees)
    in_specs = [WHOLE] * 3
    operands = [gate, maps, local]
    aliases = {}
    if held is not None:
        in_specs.append(ANY)
        operands.append(held)
        aliases = {3: 0}
    return pl.pallas_call(
        functools.partial(update_kernel, degrees=degrees),
        in_specs=in_specs,
        out_specs=ANY,
        out_shape=jax.ShapeDtypeStruct((rows, total), jnp.bfloat16),
        scratch_shapes=[
            pltpu.VMEM((last - base, rows, width), jnp.bfloat16),
            pltpu.SemaphoreType.DMA((last - base,)),
        ],
        input_output_aliases=aliases,
        compiler_params=params(),
        cost_estimate=pl.CostEstimate(
            flops=2 * (last - base) * rows * width * (rows + width),
            bytes_accessed=4 * (last - base) * rows * width,
            transcendentals=0,
        ),
        name="update",
    )(*operands)


def finish_kernel(place_ref, map_ref, flip_ref, *refs, piece, pieces, groups):
    halves = refs[:-3]
    mix_ref, out_ref, outer_ref = refs[-3:]
    width = map_ref.shape[0]

    @pl.when(pl.program_id(0) == 0)
    def _():
        for step in range(pieces):
            side, index = divmod(step, pieces // 2)
            start = 0
            for pair, parts in enumerate(groups):
                value = halves[2 * pair + side]
                at = index * (value.shape[0] // (pieces // 2))
                for count in parts:
                    height = count * width // pieces
                    row = start + (place_ref[0] ^ step) * height
                    outer_ref[pl.ds(pl.multiple_of(row, height), height), :] = value[
                        at : at + height, :
                    ]
                    at += height
                    start += count * width

    row = (place_ref[1] + pl.program_id(0)) * piece
    level = row // width
    slot = sum(jnp.where(level == value, index, 0) for index, value in enumerate(ORDER))
    first = pl.multiple_of(slot * width, width)
    mine = pl.multiple_of(slot * width + row % width, piece)
    mix_ref[...] = lax.dot_general(
        outer_ref[pl.ds(mine, piece), :],
        map_ref[...],
        (((1,), (1,)), ((), ())),
        preferred_element_type=jnp.float32,
    )
    out_ref[...] = jnp.dot(
        flip_ref[...], outer_ref[pl.ds(first, width), :], preferred_element_type=jnp.float32
    )


def finish(place, out_weight, flipped, halves, groups, shard, piece, pieces):
    total, width = out_weight.shape
    mine = pl.BlockSpec((piece, width), lambda i, place: (place[1] + i, 0))
    whole = [pl.BlockSpec(value.shape, lambda i, place: (0, 0)) for value in halves]
    return pl.pallas_call(
        functools.partial(finish_kernel, piece=piece, pieces=pieces, groups=groups),
        grid_spec=pltpu.PrefetchScalarGridSpec(
            num_scalar_prefetch=1,
            grid=(shard // piece,),
            in_specs=[
                pl.BlockSpec(
                    (width, width), lambda i, place: ((place[1] + i) * piece // width, 0)
                ),
                mine,
            ]
            + whole,
            out_specs=[pl.BlockSpec((piece, width), lambda i, place: (i, 0))] * 2,
            scratch_shapes=[pltpu.VMEM((total, width), jnp.bfloat16)],
        ),
        out_shape=[jax.ShapeDtypeStruct((shard, width), jnp.float32)] * 2,
        compiler_params=params("arbitrary"),
        name="finish",
    )(place, out_weight, flipped, *halves)


def body(
    features,
    cotangent,
    send_order,
    pair_index,
    edge_mask,
    distance,
    radial_weight,
    mix_weight,
    out_weight,
    *,
    n_dp,
    n_blk,
):
    rows, total = features.shape
    width = mix_weight.shape[1]
    pieces = 2 * n_blk
    shard = mix_weight.shape[0] // n_blk
    piece = math.gcd(shard, width)
    at_dp, at_blk = lax.axis_index("dp"), lax.axis_index("blk")
    place = jnp.stack(
        [at_dp % 2 * n_blk + at_blk, at_blk * (shard // piece), at_dp]
    ).astype(jnp.int32)

    def over_dp(value, step):
        return lax.ppermute(value, "dp", [(i, i ^ step) for i in range(n_dp)])

    def over_blk(value, step):
        return lax.ppermute(value, "blk", [(i, i ^ step) for i in range(n_blk)])

    def all_to_all(value):
        return lax.all_to_all(value, "dp", split_axis=0, concat_axis=0, tiled=True)

    def plane_sum(near, far):
        height = near.shape[0] // n_blk
        chip = near + over_dp(far, 1).astype(jnp.float32)
        own = chip[:height]
        for step in range(1, n_blk):
            part = chip[step * height : (step + 1) * height].astype(jnp.bfloat16)
            own = own + over_blk(part, step).astype(jnp.float32)
        return own

    def z_sum_direct(own):
        own = own.astype(jnp.bfloat16)
        return tree_sum([own] + [over_dp(own, 2 * step) for step in range(1, n_dp // 2)])

    def z_sum_halving(own):
        bits = [1 << i for i in range((n_dp // 2).bit_length() - 1)]
        upper = [(at_dp // 2) & bit for bit in bits]
        for bit, high in zip(bits[:-1], upper):
            half = own.shape[0] // 2
            kept = jnp.where(high > 0, own[half:], own[:half])
            given = jnp.where(high > 0, own[:half], own[half:]).astype(jnp.bfloat16)
            own = kept + over_dp(given, 2 * bit).astype(jnp.float32)
        own = own.astype(jnp.bfloat16)
        own = tree_sum([own, over_dp(own, 2 * bits[-1])])
        for bit, high in reversed(list(zip(bits[:-1], upper))):
            other = over_dp(own, 2 * bit)
            own = jnp.where(
                high > 0,
                jnp.concatenate([other, own], axis=0),
                jnp.concatenate([own, other], axis=0),
            )
        return own

    def plane_gather(own):
        near = jnp.concatenate([own] + [over_blk(own, step) for step in range(1, n_blk)], axis=0)
        return near, over_dp(near, 1)

    sent_first = pick_rows(send_order, features, width, FIRST)
    came_first = all_to_all(sent_first)
    features = after(features, sent_first)
    sent_second = pick_rows(send_order, features, width, SECOND)
    spread = pick_pieces(place, send_order, features, width, SPREAD, n_dp)
    sent_last = pick_rows(send_order, features, width, LAST)

    distance = after(distance, sent_second, sent_last, spread[0])
    gate = gate_matrices(pair_index, edge_mask, distance, radial_weight, rows)
    cotangent, mix_weight, out_weight, *spread = lax.optimization_barrier(
        (cotangent, mix_weight, out_weight, *spread, gate)
    )[:-1]
    early = list(range(n_dp - 1, n_dp - 1 - n_dp // 4, -1)) + list(range(n_dp // 2 - 1, 0, -1))
    late = [step for step in range(n_dp - 1, 0, -1) if step not in early]
    moved = {0: spread[0]}
    for step in early:
        moved[step] = over_dp(spread[step], step)
    came_second = all_to_all(after(sent_second, came_first, gate))

    cotangent, *far = lax.optimization_barrier(
        (cotangent, *[moved[step] for step in early[: n_dp // 4]])
    )
    moved.update(zip(early, far))
    cots = [flip_cotangent(cotangent, width, level) for level in range(LMAX + 1)]
    maps = degree_products(mix_weight, out_weight)
    flipped = mix_weight.reshape(LMAX + 1, width, width).swapaxes(1, 2).reshape(mix_weight.shape)
    local = after(came_first, gate, maps, flipped, *cots)
    own_first = plane_sum(*outer_sum(place, gate, [local], cots, width, (FIRST,), pieces))
    updated = update(gate, maps, local, width, FIRST, total, None)
    for step in late:
        moved[step] = over_dp(after(spread[step], own_first), step)
    came_last = all_to_all(after(sent_last, came_second, own_first, updated))

    joined = join_pieces(place, [moved[step] for step in range(n_dp)])
    own_rest = plane_sum(
        *outer_sum(place, gate, [joined, came_second], cots, width, (SPREAD, SECOND), pieces)
    )
    updated = update(gate, maps, joined, width, SPREAD, total, updated)
    updated = update(gate, maps, came_second, width, SECOND, total, updated)
    most = z_sum_halving(jnp.concatenate([own_first, own_rest], axis=0))

    local = after(came_last, updated)
    own_last = z_sum_direct(
        plane_sum(*outer_sum(place, gate, [local], cots, width, (LAST,), pieces))
    )
    updated = update(gate, maps, local, width, LAST, total, updated)
    halves = [*plane_gather(most), *plane_gather(after(own_last, updated))]
    groups = ((len(FIRST), len(SPREAD) + len(SECOND)), (len(LAST),))
    mix_grad, out_grad = finish(place, out_weight, flipped, halves, groups, shard, piece, pieces)
    return updated, mix_grad, out_grad


def solution(mesh):
    in_specs = (
        P(("dp", "blk"), None),
        P(("dp", "blk"), None),
        P(("dp", "blk"), None),
        P(("dp", "blk"), None),
        P(("dp", "blk"), None, None),
        P(("dp", "blk"), None, None),
        P(),
        P(),
        P(),
    )
    out_specs = (P(("dp", "blk"), None), P("blk", None), P("blk", None))
    run = functools.partial(body, n_dp=mesh.shape["dp"], n_blk=mesh.shape["blk"])
    return jax.shard_map(run, mesh=mesh, in_specs=in_specs, out_specs=out_specs, check_vma=False)
```

```python
import functools
import math

import jax
import jax.numpy as jnp
from jax import lax
from jax.experimental import pallas as pl
from jax.experimental.pallas import tpu as pltpu
from jax.sharding import PartitionSpec as P

LMAX = 4
BLOCK = 128
CUT_RADIUS = 5.0
EDGE_SCALE = 0.25
MOST, LAST = (0, 1, 2, 4), (3,)
ORDER = MOST + LAST
VMEM_LIMIT = 48 * 1024 * 1024
GATE_ROWS = 16
WHOLE = pl.BlockSpec(memory_space=pltpu.VMEM)
ANY = pl.BlockSpec(memory_space=pl.ANY)
SCALARS = pl.BlockSpec(memory_space=pltpu.SMEM)


def params(*semantics):
    return pltpu.CompilerParams(dimension_semantics=semantics, vmem_limit_bytes=VMEM_LIMIT)


def after(value, *others):
    return lax.optimization_barrier((value, *others))[0]


def span(degrees):
    return degrees[0] ** 2, (degrees[-1] + 1) ** 2


def comps_of(degrees):
    return [comp for level in degrees for comp in range(*span((level,)))]


def tree_sum(parts):
    parts = [part.astype(jnp.float32) for part in parts]
    while len(parts) > 1:
        parts = [parts[i] + parts[i + 1] for i in range(0, len(parts), 2)]
    return parts[0].astype(jnp.bfloat16)


def chosen_rows(order_ref, rows):
    local = lax.broadcasted_iota(jnp.int32, (rows, rows), 0)
    return (local == order_ref[...]).astype(jnp.float32).T.astype(jnp.bfloat16)


def pick_kernel(order_ref, rows_ref, out_ref, held_ref, ready_ref, in_sems, out_sems, *, comps):
    _, rows, width = held_ref.shape
    loads = [
        pltpu.make_async_copy(
            rows_ref.at[:, pl.ds(comp * width, width)], held_ref.at[i], in_sems.at[i]
        )
        for i, comp in enumerate(comps)
    ]
    for load in loads:
        load.start()
    pick = chosen_rows(order_ref, rows)
    stores = []
    for i, load in enumerate(loads):
        load.wait()
        ready_ref[i] = jnp.dot(pick, held_ref[i], preferred_element_type=jnp.float32).astype(
            jnp.bfloat16
        )
        stores.append(
            pltpu.make_async_copy(
                ready_ref.at[i], out_ref.at[:, pl.ds(i * width, width)], out_sems.at[i]
            )
        )
        stores[-1].start()
    for store in stores:
        store.wait()


def pick_rows(order, features, width, degrees):
    rows = features.shape[0]
    comps = comps_of(degrees)
    count = len(comps)
    return pl.pallas_call(
        functools.partial(pick_kernel, comps=comps),
        in_specs=[WHOLE, ANY],
        out_specs=ANY,
        out_shape=jax.ShapeDtypeStruct((rows, count * width), jnp.bfloat16),
        scratch_shapes=[
            pltpu.VMEM((count, rows, width), jnp.bfloat16),
            pltpu.VMEM((count, rows, width), jnp.bfloat16),
            pltpu.SemaphoreType.DMA((count,)),
            pltpu.SemaphoreType.DMA((count,)),
        ],
        compiler_params=params(),
        name="pick_rows",
    )(order, features)


def gate_kernel(pairs_ref, mask_ref, dist_ref, weight_ref, out_ref, radial_ref, *, basis_count):
    pair, step = pl.program_id(0), pl.program_id(1)

    @pl.when((pair == 0) & (step == 0))
    def _():
        out_ref[...] = jnp.zeros_like(out_ref)

    half = math.sqrt(0.5 * math.log2(math.e))
    dist = dist_ref[0]
    scaled = dist * (half * (basis_count - 1) / CUT_RADIUS)
    centers = lax.broadcasted_iota(jnp.int32, (basis_count, BLOCK), 0).astype(jnp.float32) * half
    weights = weight_ref[...]
    levels = LMAX + 1
    for row in range(GATE_ROWS):
        offset = scaled[row : row + 1, :] - centers
        phi = jnp.exp2(-(offset * offset))
        high = phi.astype(jnp.bfloat16)
        low = (phi - high.astype(jnp.float32)).astype(jnp.bfloat16)
        radial = jnp.dot(weights, high, preferred_element_type=jnp.float32)
        radial = radial + jnp.dot(weights, low, preferred_element_type=jnp.float32)
        radial = radial[0:8] + radial[8:16]
        for level in range(levels):
            radial_ref[level, row : row + 1, :] = radial[level : level + 1, :]
    envelope = (
        (0.5 * EDGE_SCALE)
        * (jnp.cos((math.pi / CUT_RADIUS) * dist) + 1.0)
        * mask_ref[0].astype(jnp.float32)
    )
    dest = pl.multiple_of(pairs_ref[pair, 0] * BLOCK + step * GATE_ROWS, GATE_ROWS)
    src = pl.multiple_of(pairs_ref[pair, 1] * BLOCK, BLOCK)
    for level in range(levels):
        out_ref[level, pl.ds(dest, GATE_ROWS), pl.ds(src, BLOCK)] = (
            radial_ref[level] * envelope
        ).astype(jnp.bfloat16)


def gate_matrices(pairs, mask, dist, radial_weight, rows):
    count = pairs.shape[0]
    levels = radial_weight.shape[1]
    transposed = radial_weight.T
    high = transposed.astype(jnp.bfloat16)
    low = (transposed - high.astype(jnp.float32)).astype(jnp.bfloat16)
    pad = ((0, 8 - levels), (0, 0))
    weights = jnp.concatenate([jnp.pad(high, pad), jnp.pad(low, pad)], axis=0)
    kernel = functools.partial(gate_kernel, basis_count=radial_weight.shape[0])
    edges = pl.BlockSpec((1, GATE_ROWS, BLOCK), lambda p, s, pairs: (p, s, 0))
    return pl.pallas_call(
        kernel,
        grid_spec=pltpu.PrefetchScalarGridSpec(
            num_scalar_prefetch=1,
            grid=(count, BLOCK // GATE_ROWS),
            in_specs=[edges, edges, pl.BlockSpec(weights.shape, lambda p, s, pairs: (0, 0))],
            out_specs=pl.BlockSpec((levels, rows, rows), lambda p, s, pairs: (0, 0, 0)),
            scratch_shapes=[pltpu.VMEM((levels, GATE_ROWS, BLOCK), jnp.float32)],
        ),
        out_shape=jax.ShapeDtypeStruct((levels, rows, rows), jnp.bfloat16),
        compiler_params=params("arbitrary", "arbitrary"),
        cost_estimate=pl.CostEstimate(
            flops=2 * 3 * 512 * count * BLOCK * BLOCK * radial_weight.shape[0],
            bytes_accessed=2 * 4 * count * BLOCK * BLOCK,
            transcendentals=count * BLOCK * BLOCK * radial_weight.shape[0],
        ),
        name="gate",
    )(pairs, mask, dist, weights)


def product_kernel(left_ref, right_ref, out_ref):
    out_ref[...] = jnp.dot(
        left_ref[...], right_ref[...], preferred_element_type=jnp.float32
    ).astype(jnp.bfloat16)


def degree_products(left, right):
    width = left.shape[1]
    block = pl.BlockSpec((width, width), lambda i: (i, 0))
    return pl.pallas_call(
        product_kernel,
        grid=(left.shape[0] // width,),
        in_specs=[block, block],
        out_specs=block,
        out_shape=jax.ShapeDtypeStruct(left.shape, jnp.bfloat16),
        compiler_params=params("arbitrary"),
        name="degree_products",
    )(left, right)


def flip_kernel(rows_ref, out_ref):
    out_ref[...] = rows_ref[...].T


def flip_cotangent(cotangent, width, level):
    rows = cotangent.shape[0]
    first, last = span((level,))
    return pl.pallas_call(
        flip_kernel,
        grid=(last - first,),
        in_specs=[pl.BlockSpec((rows, width), lambda i: (0, first + i))],
        out_specs=pl.BlockSpec((width, rows), lambda i: (0, i)),
        out_shape=jax.ShapeDtypeStruct((width, (last - first) * rows), jnp.bfloat16),
        compiler_params=params("arbitrary"),
        name="flip_cotangent",
    )(cotangent)


def outer_kernel(place_ref, gate_ref, local_ref, *refs, pieces, levels):
    cots = refs[: len(levels)]
    *outs, mixed_ref, sum_ref = refs[len(levels) :]
    rows, width = local_ref.shape[0], mixed_ref.shape[1]
    comps = comps_of(levels)
    for slot, level in enumerate(levels):
        first, last = span((level,))
        for comp in range(first, last):
            at = comps.index(comp) * width
            mixed_ref[(comp - first) * rows : (comp - first + 1) * rows, :] = jnp.dot(
                gate_ref[level], local_ref[:, at : at + width], preferred_element_type=jnp.float32
            ).astype(jnp.bfloat16)
        depth = (last - first) * rows
        flipped = jnp.dot(
            cots[slot][...], mixed_ref[0:depth, :], preferred_element_type=jnp.float32
        )
        sum_ref[slot * width : (slot + 1) * width, :] = flipped.T
    if len(outs) == 1:
        outs[0][...] = sum_ref[...].astype(jnp.bfloat16)
        return
    near_ref, far_ref = outs
    half = pieces // 2
    height = near_ref.shape[0] // half
    for step in range(half):
        to = slice(step * height, (step + 1) * height)
        row = pl.multiple_of((place_ref[0] ^ step) * height, height)
        near_ref[to, :] = sum_ref[pl.ds(row, height), :]
        row = pl.multiple_of((place_ref[0] ^ (step + half)) * height, height)
        far_ref[to, :] = sum_ref[pl.ds(row, height), :].astype(jnp.bfloat16)


def outer_sum(place, gate, local, cots, width, levels, pieces=None):
    rows = gate.shape[1]
    whole = len(levels) * width
    deepest = 2 * max(levels) + 1
    total = sum(2 * level + 1 for level in levels)
    if pieces is None:
        out_shape = [jax.ShapeDtypeStruct((whole, width), jnp.bfloat16)]
    else:
        out_shape = [
            jax.ShapeDtypeStruct((whole // 2, width), jnp.float32),
            jax.ShapeDtypeStruct((whole // 2, width), jnp.bfloat16),
        ]
    return pl.pallas_call(
        functools.partial(outer_kernel, pieces=pieces, levels=levels),
        in_specs=[SCALARS] + [WHOLE] * (2 + len(levels)),
        out_specs=[WHOLE] * len(out_shape),
        out_shape=out_shape,
        scratch_shapes=[
            pltpu.VMEM((deepest * rows, width), jnp.bfloat16),
            pltpu.VMEM((whole, width), jnp.float32),
        ],
        compiler_params=params(),
        cost_estimate=pl.CostEstimate(
            flops=2 * total * rows * width * (rows + width),
            bytes_accessed=4 * total * rows * width,
            transcendentals=0,
        ),
        name="outer_sum",
    )(place, gate, local, *[cots[level] for level in levels])


def update_kernel(gate_ref, map_ref, local_ref, *refs, degrees):
    out_ref, ready_ref, sems = refs[-3:]
    width = map_ref.shape[1]
    copies = []
    for index, comp in enumerate(comps_of(degrees)):
        level = math.isqrt(comp)
        at = index * width
        hidden = local_ref[:, at : at + width]
        mixed = jnp.dot(gate_ref[level], hidden, preferred_element_type=jnp.float32)
        added = jnp.dot(
            mixed.astype(jnp.bfloat16),
            map_ref[level * width : (level + 1) * width, :],
            preferred_element_type=jnp.float32,
        )
        ready_ref[index] = (hidden.astype(jnp.float32) + added).astype(jnp.bfloat16)
        copies.append(
            pltpu.make_async_copy(
                ready_ref.at[index],
                out_ref.at[:, pl.ds(comp * width, width)],
                sems.at[index],
            )
        )
        copies[-1].start()
    for copy in copies:
        copy.wait()


def update(gate, maps, local, width, degrees, total, held):
    rows = gate.shape[1]
    count = len(comps_of(degrees))
    in_specs = [WHOLE] * 3
    operands = [gate, maps, local]
    aliases = {}
    if held is not None:
        in_specs.append(ANY)
        operands.append(held)
        aliases = {3: 0}
    return pl.pallas_call(
        functools.partial(update_kernel, degrees=degrees),
        in_specs=in_specs,
        out_specs=ANY,
        out_shape=jax.ShapeDtypeStruct((rows, total), jnp.bfloat16),
        scratch_shapes=[
            pltpu.VMEM((count, rows, width), jnp.bfloat16),
            pltpu.SemaphoreType.DMA((count,)),
        ],
        input_output_aliases=aliases,
        compiler_params=params(),
        cost_estimate=pl.CostEstimate(
            flops=2 * count * rows * width * (rows + width),
            bytes_accessed=4 * count * rows * width,
            transcendentals=0,
        ),
        name="update",
    )(*operands)


def finish_kernel(place_ref, map_ref, flip_ref, near_ref, far_ref, last_ref, *refs, piece, pieces):
    mix_ref, out_ref, outer_ref = refs
    width = map_ref.shape[0]
    most = len(MOST) * width

    @pl.when(pl.program_id(0) == 0)
    def _():
        height = most // pieces
        for step in range(pieces):
            side, index = divmod(step, pieces // 2)
            value = (near_ref, far_ref)[side]
            row = pl.multiple_of((place_ref[0] ^ step) * height, height)
            outer_ref[pl.ds(row, height), :] = value[index * height : (index + 1) * height, :]
        outer_ref[most:, :] = last_ref[...]

    row = (place_ref[1] + pl.program_id(0)) * piece
    level = row // width
    slot = sum(jnp.where(level == value, index, 0) for index, value in enumerate(ORDER))
    first = pl.multiple_of(slot * width, width)
    mine = pl.multiple_of(slot * width + row % width, piece)
    mix_ref[...] = lax.dot_general(
        outer_ref[pl.ds(mine, piece), :],
        map_ref[...],
        (((1,), (1,)), ((), ())),
        preferred_element_type=jnp.float32,
    )
    out_ref[...] = jnp.dot(
        flip_ref[...], outer_ref[pl.ds(first, width), :], preferred_element_type=jnp.float32
    )


def finish(place, out_weight, flipped, sums, shard, piece, pieces):
    total, width = out_weight.shape
    mine = pl.BlockSpec((piece, width), lambda i, place: (place[1] + i, 0))
    whole = [pl.BlockSpec(value.shape, lambda i, place: (0, 0)) for value in sums]
    return pl.pallas_call(
        functools.partial(finish_kernel, piece=piece, pieces=pieces),
        grid_spec=pltpu.PrefetchScalarGridSpec(
            num_scalar_prefetch=1,
            grid=(shard // piece,),
            in_specs=[
                pl.BlockSpec(
                    (width, width), lambda i, place: ((place[1] + i) * piece // width, 0)
                ),
                mine,
            ]
            + whole,
            out_specs=[pl.BlockSpec((piece, width), lambda i, place: (i, 0))] * 2,
            scratch_shapes=[pltpu.VMEM((total, width), jnp.bfloat16)],
        ),
        out_shape=[jax.ShapeDtypeStruct((shard, width), jnp.float32)] * 2,
        compiler_params=params("arbitrary"),
        name="finish",
    )(place, out_weight, flipped, *sums)


def body(
    features,
    cotangent,
    send_order,
    pair_index,
    edge_mask,
    distance,
    radial_weight,
    mix_weight,
    out_weight,
    *,
    n_dp,
    n_blk,
):
    rows, total = features.shape
    width = mix_weight.shape[1]
    pieces = 2 * n_blk
    shard = mix_weight.shape[0] // n_blk
    piece = math.gcd(shard, width)
    at_dp, at_blk = lax.axis_index("dp"), lax.axis_index("blk")
    place = jnp.stack([at_dp % 2 * n_blk + at_blk, at_blk * (shard // piece)]).astype(jnp.int32)

    def over_dp(value, step):
        return lax.ppermute(value, "dp", [(i, i ^ step) for i in range(n_dp)])

    def over_blk(value, step):
        return lax.ppermute(value, "blk", [(i, i ^ step) for i in range(n_blk)])

    def all_to_all(value):
        return lax.all_to_all(value, "dp", split_axis=0, concat_axis=0, tiled=True)

    def plane_sum(near, far):
        height = near.shape[0] // n_blk
        chip = near + over_dp(far, 1).astype(jnp.float32)
        own = chip[:height]
        for step in range(1, n_blk):
            part = chip[step * height : (step + 1) * height].astype(jnp.bfloat16)
            own = own + over_blk(part, step).astype(jnp.float32)
        return own

    def z_sum_halving(own):
        bits = [1 << i for i in range((n_dp // 2).bit_length() - 1)]
        upper = [(at_dp // 2) & bit for bit in bits]
        for bit, high in zip(bits[:-1], upper):
            half = own.shape[0] // 2
            kept = jnp.where(high > 0, own[half:], own[:half])
            given = jnp.where(high > 0, own[:half], own[half:]).astype(jnp.bfloat16)
            own = kept + over_dp(given, 2 * bit).astype(jnp.float32)
        own = own.astype(jnp.bfloat16)
        own = tree_sum([own, over_dp(own, 2 * bits[-1])])
        for bit, high in reversed(list(zip(bits[:-1], upper))):
            other = over_dp(own, 2 * bit)
            own = jnp.where(
                high > 0,
                jnp.concatenate([other, own], axis=0),
                jnp.concatenate([own, other], axis=0),
            )
        return own

    def plane_gather(own):
        near = jnp.concatenate([own] + [over_blk(own, step) for step in range(1, n_blk)], axis=0)
        return near, over_dp(near, 1)

    sent_most = pick_rows(send_order, features, width, MOST)
    came_most = all_to_all(sent_most)
    sent_last = pick_rows(send_order, after(features, sent_most), width, LAST)
    gate = gate_matrices(pair_index, edge_mask, after(distance, sent_last), radial_weight, rows)
    cotangent, mix_weight, out_weight = lax.optimization_barrier(
        (cotangent, mix_weight, out_weight, gate)
    )[:3]
    cots = [flip_cotangent(cotangent, width, level) for level in range(LMAX + 1)]
    maps = degree_products(mix_weight, out_weight)
    flipped = mix_weight.reshape(LMAX + 1, width, width).swapaxes(1, 2).reshape(mix_weight.shape)
    ready = (gate, maps, flipped, *cots)
    came_last = all_to_all(after(sent_last, came_most, *ready))

    local = after(came_most, *ready)
    own = plane_sum(*outer_sum(place, gate, local, cots, width, MOST, pieces))
    updated = update(gate, maps, local, width, MOST, total, None)

    local = after(came_last, own, updated)
    part = outer_sum(place, gate, local, cots, width, LAST)[0]
    last = lax.psum(part, ("dp", "blk"))
    updated = update(gate, maps, local, width, LAST, total, updated)
    near, far = plane_gather(z_sum_halving(after(own, part)))
    mix_grad, out_grad = finish(place, out_weight, flipped, (near, far, last), shard, piece, pieces)
    return updated, mix_grad, out_grad


def solution(mesh):
    in_specs = (
        P(("dp", "blk"), None),
        P(("dp", "blk"), None),
        P(("dp", "blk"), None),
        P(("dp", "blk"), None),
        P(("dp", "blk"), None, None),
        P(("dp", "blk"), None, None),
        P(),
        P(),
        P(),
    )
    out_specs = (P(("dp", "blk"), None), P("blk", None), P("blk", None))
    run = functools.partial(body, n_dp=mesh.shape["dp"], n_blk=mesh.shape["blk"])
    return jax.shard_map(run, mesh=mesh, in_specs=in_specs, out_specs=out_specs, check_vma=False)
```

```python
import functools
import math

import jax
import jax.numpy as jnp
from jax import lax
from jax.experimental import pallas as pl
from jax.experimental.pallas import tpu as pltpu
from jax.sharding import PartitionSpec as P

LMAX = 4
BLOCK = 128
CUT_RADIUS = 5.0
EDGE_SCALE = 0.25
MOST, LAST = (0, 1, 2, 3), (4,)
ORDER = MOST + LAST
VMEM_LIMIT = 48 * 1024 * 1024
PICK_LIMIT = 60 * 1024 * 1024
GATE_ROWS = 16
WHOLE = pl.BlockSpec(memory_space=pltpu.VMEM)
ANY = pl.BlockSpec(memory_space=pl.ANY)
SCALARS = pl.BlockSpec(memory_space=pltpu.SMEM)


def params(*semantics, limit=VMEM_LIMIT):
    return pltpu.CompilerParams(dimension_semantics=semantics, vmem_limit_bytes=limit)


def after(value, *others):
    return lax.optimization_barrier((value, *others))[0]


def span(degrees):
    return degrees[0] ** 2, (degrees[-1] + 1) ** 2


def comps_of(degrees):
    return [comp for level in degrees for comp in range(*span((level,)))]


def tree_sum(parts):
    parts = [part.astype(jnp.float32) for part in parts]
    while len(parts) > 1:
        parts = [parts[i] + parts[i + 1] for i in range(0, len(parts), 2)]
    return parts[0].astype(jnp.bfloat16)


def chosen_rows(order_ref, rows):
    local = lax.broadcasted_iota(jnp.int32, (rows, rows), 0)
    return (local == order_ref[...]).astype(jnp.float32).T.astype(jnp.bfloat16)


def pick_kernel(order_ref, rows_ref, out_ref, held_ref, ready_ref, in_sems, out_sems, *, comps):
    _, rows, width = held_ref.shape
    loads = [
        pltpu.make_async_copy(
            rows_ref.at[:, pl.ds(comp * width, width)], held_ref.at[i], in_sems.at[i]
        )
        for i, comp in enumerate(comps)
    ]
    for load in loads:
        load.start()
    pick = chosen_rows(order_ref, rows)
    stores = []
    for i, load in enumerate(loads):
        load.wait()
        ready_ref[i] = jnp.dot(pick, held_ref[i], preferred_element_type=jnp.float32).astype(
            jnp.bfloat16
        )
        stores.append(
            pltpu.make_async_copy(
                ready_ref.at[i], out_ref.at[:, pl.ds(i * width, width)], out_sems.at[i]
            )
        )
        stores[-1].start()
    for store in stores:
        store.wait()


def pick_rows(order, features, width, degrees):
    rows = features.shape[0]
    comps = comps_of(degrees)
    count = len(comps)
    return pl.pallas_call(
        functools.partial(pick_kernel, comps=comps),
        in_specs=[WHOLE, ANY],
        out_specs=ANY,
        out_shape=jax.ShapeDtypeStruct((rows, count * width), jnp.bfloat16),
        scratch_shapes=[
            pltpu.VMEM((count, rows, width), jnp.bfloat16),
            pltpu.VMEM((count, rows, width), jnp.bfloat16),
            pltpu.SemaphoreType.DMA((count,)),
            pltpu.SemaphoreType.DMA((count,)),
        ],
        compiler_params=params(limit=PICK_LIMIT),
        name="pick_rows",
    )(order, features)


def gate_kernel(pairs_ref, mask_ref, dist_ref, weight_ref, out_ref, radial_ref, *, basis_count):
    pair, step = pl.program_id(0), pl.program_id(1)

    @pl.when((pair == 0) & (step == 0))
    def _():
        out_ref[...] = jnp.zeros_like(out_ref)

    half = math.sqrt(0.5 * math.log2(math.e))
    dist = dist_ref[0]
    scaled = dist * (half * (basis_count - 1) / CUT_RADIUS)
    centers = lax.broadcasted_iota(jnp.int32, (basis_count, BLOCK), 0).astype(jnp.float32) * half
    weights = weight_ref[...]
    levels = LMAX + 1
    for row in range(GATE_ROWS):
        offset = scaled[row : row + 1, :] - centers
        phi = jnp.exp2(-(offset * offset))
        high = phi.astype(jnp.bfloat16)
        low = (phi - high.astype(jnp.float32)).astype(jnp.bfloat16)
        radial = jnp.dot(weights, high, preferred_element_type=jnp.float32)
        radial = radial + jnp.dot(weights, low, preferred_element_type=jnp.float32)
        radial = radial[0:8] + radial[8:16]
        for level in range(levels):
            radial_ref[level, row : row + 1, :] = radial[level : level + 1, :]
    envelope = (
        (0.5 * EDGE_SCALE)
        * (jnp.cos((math.pi / CUT_RADIUS) * dist) + 1.0)
        * mask_ref[0].astype(jnp.float32)
    )
    dest = pl.multiple_of(pairs_ref[pair, 0] * BLOCK + step * GATE_ROWS, GATE_ROWS)
    src = pl.multiple_of(pairs_ref[pair, 1] * BLOCK, BLOCK)
    for level in range(levels):
        out_ref[level, pl.ds(dest, GATE_ROWS), pl.ds(src, BLOCK)] = (
            radial_ref[level] * envelope
        ).astype(jnp.bfloat16)


def gate_matrices(pairs, mask, dist, radial_weight, rows):
    count = pairs.shape[0]
    levels = radial_weight.shape[1]
    transposed = radial_weight.T
    high = transposed.astype(jnp.bfloat16)
    low = (transposed - high.astype(jnp.float32)).astype(jnp.bfloat16)
    pad = ((0, 8 - levels), (0, 0))
    weights = jnp.concatenate([jnp.pad(high, pad), jnp.pad(low, pad)], axis=0)
    kernel = functools.partial(gate_kernel, basis_count=radial_weight.shape[0])
    edges = pl.BlockSpec((1, GATE_ROWS, BLOCK), lambda p, s, pairs: (p, s, 0))
    return pl.pallas_call(
        kernel,
        grid_spec=pltpu.PrefetchScalarGridSpec(
            num_scalar_prefetch=1,
            grid=(count, BLOCK // GATE_ROWS),
            in_specs=[edges, edges, pl.BlockSpec(weights.shape, lambda p, s, pairs: (0, 0))],
            out_specs=pl.BlockSpec((levels, rows, rows), lambda p, s, pairs: (0, 0, 0)),
            scratch_shapes=[pltpu.VMEM((levels, GATE_ROWS, BLOCK), jnp.float32)],
        ),
        out_shape=jax.ShapeDtypeStruct((levels, rows, rows), jnp.bfloat16),
        compiler_params=params("arbitrary", "arbitrary"),
        cost_estimate=pl.CostEstimate(
            flops=2 * 3 * 512 * count * BLOCK * BLOCK * radial_weight.shape[0],
            bytes_accessed=2 * 4 * count * BLOCK * BLOCK,
            transcendentals=count * BLOCK * BLOCK * radial_weight.shape[0],
        ),
        name="gate",
    )(pairs, mask, dist, weights)


def product_kernel(left_ref, right_ref, out_ref):
    out_ref[...] = jnp.dot(
        left_ref[...], right_ref[...], preferred_element_type=jnp.float32
    ).astype(jnp.bfloat16)


def degree_products(left, right):
    width = left.shape[1]
    block = pl.BlockSpec((width, width), lambda i: (i, 0))
    return pl.pallas_call(
        product_kernel,
        grid=(left.shape[0] // width,),
        in_specs=[block, block],
        out_specs=block,
        out_shape=jax.ShapeDtypeStruct(left.shape, jnp.bfloat16),
        compiler_params=params("arbitrary"),
        name="degree_products",
    )(left, right)


def flip_kernel(rows_ref, out_ref):
    out_ref[...] = rows_ref[...].T


def flip_cotangent(cotangent, width, level):
    rows = cotangent.shape[0]
    first, last = span((level,))
    return pl.pallas_call(
        flip_kernel,
        grid=(last - first,),
        in_specs=[pl.BlockSpec((rows, width), lambda i: (0, first + i))],
        out_specs=pl.BlockSpec((width, rows), lambda i: (0, i)),
        out_shape=jax.ShapeDtypeStruct((width, (last - first) * rows), jnp.bfloat16),
        compiler_params=params("arbitrary"),
        name="flip_cotangent",
    )(cotangent)


def outer_kernel(place_ref, gate_ref, local_ref, *refs, pieces, levels):
    cots = refs[: len(levels)]
    near_ref, far_ref, mixed_ref, sum_ref = refs[len(levels) :]
    rows, width = local_ref.shape[0], mixed_ref.shape[1]
    comps = comps_of(levels)
    for slot, level in enumerate(levels):
        first, last = span((level,))
        for comp in range(first, last):
            at = comps.index(comp) * width
            mixed_ref[(comp - first) * rows : (comp - first + 1) * rows, :] = jnp.dot(
                gate_ref[level], local_ref[:, at : at + width], preferred_element_type=jnp.float32
            ).astype(jnp.bfloat16)
        depth = (last - first) * rows
        flipped = jnp.dot(
            cots[slot][...], mixed_ref[0:depth, :], preferred_element_type=jnp.float32
        )
        sum_ref[slot * width : (slot + 1) * width, :] = flipped.T
    half = pieces // 2
    height = near_ref.shape[0] // half
    for step in range(half):
        to = slice(step * height, (step + 1) * height)
        row = pl.multiple_of((place_ref[0] ^ step) * height, height)
        near_ref[to, :] = sum_ref[pl.ds(row, height), :]
        row = pl.multiple_of((place_ref[0] ^ (step + half)) * height, height)
        far_ref[to, :] = sum_ref[pl.ds(row, height), :].astype(jnp.bfloat16)


def outer_sum(place, gate, local, cots, width, levels, pieces):
    rows = gate.shape[1]
    whole = len(levels) * width
    deepest = 2 * max(levels) + 1
    total = sum(2 * level + 1 for level in levels)
    return pl.pallas_call(
        functools.partial(outer_kernel, pieces=pieces, levels=levels),
        in_specs=[SCALARS] + [WHOLE] * (2 + len(levels)),
        out_specs=[WHOLE] * 2,
        out_shape=[
            jax.ShapeDtypeStruct((whole // 2, width), jnp.float32),
            jax.ShapeDtypeStruct((whole // 2, width), jnp.bfloat16),
        ],
        scratch_shapes=[
            pltpu.VMEM((deepest * rows, width), jnp.bfloat16),
            pltpu.VMEM((whole, width), jnp.float32),
        ],
        compiler_params=params(),
        cost_estimate=pl.CostEstimate(
            flops=2 * total * rows * width * (rows + width),
            bytes_accessed=4 * total * rows * width,
            transcendentals=0,
        ),
        name="outer_sum",
    )(place, gate, local, *[cots[level] for level in levels])


def update_kernel(gate_ref, map_ref, local_ref, *refs, degrees):
    out_ref, ready_ref, sems = refs[-3:]
    width = map_ref.shape[1]
    copies = []
    for index, comp in enumerate(comps_of(degrees)):
        level = math.isqrt(comp)
        at = index * width
        hidden = local_ref[:, at : at + width]
        mixed = jnp.dot(gate_ref[level], hidden, preferred_element_type=jnp.float32)
        added = jnp.dot(
            mixed.astype(jnp.bfloat16),
            map_ref[level * width : (level + 1) * width, :],
            preferred_element_type=jnp.float32,
        )
        ready_ref[index] = (hidden.astype(jnp.float32) + added).astype(jnp.bfloat16)
        copies.append(
            pltpu.make_async_copy(
                ready_ref.at[index],
                out_ref.at[:, pl.ds(comp * width, width)],
                sems.at[index],
            )
        )
        copies[-1].start()
    for copy in copies:
        copy.wait()


def update(gate, maps, local, width, degrees, total, held):
    rows = gate.shape[1]
    count = len(comps_of(degrees))
    in_specs = [WHOLE] * 3
    operands = [gate, maps, local]
    aliases = {}
    if held is not None:
        in_specs.append(ANY)
        operands.append(held)
        aliases = {3: 0}
    return pl.pallas_call(
        functools.partial(update_kernel, degrees=degrees),
        in_specs=in_specs,
        out_specs=ANY,
        out_shape=jax.ShapeDtypeStruct((rows, total), jnp.bfloat16),
        scratch_shapes=[
            pltpu.VMEM((count, rows, width), jnp.bfloat16),
            pltpu.SemaphoreType.DMA((count,)),
        ],
        input_output_aliases=aliases,
        compiler_params=params(),
        cost_estimate=pl.CostEstimate(
            flops=2 * count * rows * width * (rows + width),
            bytes_accessed=4 * count * rows * width,
            transcendentals=0,
        ),
        name="update",
    )(*operands)


def place_parts(place_ref, parts, outer_ref):
    height = parts[0].shape[0]
    for step, part in enumerate(parts):
        row = pl.multiple_of((place_ref[0] ^ step) * height, height)
        outer_ref[pl.ds(row, height), :] = part[...]


def gradients(rows, outer, flipped, weight):
    mix = lax.dot_general(
        rows, weight, (((1,), (1,)), ((), ())), preferred_element_type=jnp.float32
    )
    return mix, jnp.dot(flipped, outer, preferred_element_type=jnp.float32)


def most_kernel(place_ref, weight_ref, flip_ref, *refs, piece):
    *parts, mix_ref, out_ref, outer_ref = refs
    width = weight_ref.shape[0]

    @pl.when(pl.program_id(0) == 0)
    def _():
        place_parts(place_ref, parts, outer_ref)

    row = (place_ref[1] + pl.program_id(0)) * piece

    @pl.when(row < len(MOST) * width)
    def _():
        first = pl.multiple_of(row // width * width, width)
        mix_ref[...], out_ref[...] = gradients(
            outer_ref[pl.ds(pl.multiple_of(row, piece), piece), :],
            outer_ref[pl.ds(first, width), :],
            flip_ref[...],
            weight_ref[...],
        )


def most_gradients(place, weight, flipped, parts, shard, piece):
    width = weight.shape[1]
    whole = pl.BlockSpec(parts[0].shape, lambda i, place: (0, 0))
    return pl.pallas_call(
        functools.partial(most_kernel, piece=piece),
        grid_spec=pltpu.PrefetchScalarGridSpec(
            num_scalar_prefetch=1,
            grid=(shard // piece,),
            in_specs=[
                pl.BlockSpec(
                    (width, width), lambda i, place: ((place[1] + i) * piece // width, 0)
                ),
                pl.BlockSpec((piece, width), lambda i, place: (place[1] + i, 0)),
            ]
            + [whole] * len(parts),
            out_specs=[pl.BlockSpec((piece, width), lambda i, place: (i, 0))] * 2,
            scratch_shapes=[pltpu.VMEM((len(MOST) * width, width), jnp.bfloat16)],
        ),
        out_shape=[jax.ShapeDtypeStruct((shard, width), jnp.float32)] * 2,
        compiler_params=params("arbitrary"),
        name="most_gradients",
    )(place, weight, flipped, *parts)


def last_kernel(place_ref, weight_ref, flip_ref, *refs, piece):
    *parts, _, _, mix_out, out_out, outer_ref, mix_ref, out_ref, sems = refs
    width = weight_ref.shape[0]
    place_parts(place_ref, parts, outer_ref)
    count = mix_ref.shape[0]

    def each(index):
        row = (place_ref[1] + index) * piece - LAST[0] * width
        to = pl.ds(index * piece, piece)
        copies = [
            pltpu.make_async_copy(mix_ref.at[index], mix_out.at[to, :], sems.at[index, 0]),
            pltpu.make_async_copy(out_ref.at[index], out_out.at[to, :], sems.at[index, 1]),
        ]
        return row, (row >= 0) & (row < width), copies

    for index in range(count):
        row, held, copies = each(index)

        @pl.when(held)
        def _():
            mine = pl.ds(pl.multiple_of(row, piece), piece)
            mix_ref[index], out_ref[index] = gradients(
                outer_ref[mine, :], outer_ref[...], flip_ref[mine, :], weight_ref[...]
            )
            for copy in copies:
                copy.start()

    for index in range(count):
        _, held, copies = each(index)

        @pl.when(held)
        def _():
            for copy in copies:
                copy.wait()


def last_gradients(place, weight, flipped, parts, mix_grad, out_grad, piece):
    shard, width = mix_grad.shape
    own = pl.BlockSpec((width, width), lambda i: (LAST[0], 0))
    whole = pl.BlockSpec(parts[0].shape, lambda i: (0, 0))
    count = shard // piece
    return pl.pallas_call(
        functools.partial(last_kernel, piece=piece),
        grid=(1,),
        in_specs=[SCALARS, own, own] + [whole] * len(parts) + [ANY] * 2,
        out_specs=[ANY] * 2,
        out_shape=[jax.ShapeDtypeStruct(mix_grad.shape, jnp.float32)] * 2,
        scratch_shapes=[
            pltpu.VMEM((width, width), jnp.bfloat16),
            pltpu.VMEM((count, piece, width), jnp.float32),
            pltpu.VMEM((count, piece, width), jnp.float32),
            pltpu.SemaphoreType.DMA((count, 2)),
        ],
        input_output_aliases={3 + len(parts): 0, 4 + len(parts): 1},
        compiler_params=params("arbitrary"),
        name="last_gradients",
    )(place, weight, flipped, *parts, mix_grad, out_grad)


def body(
    features,
    cotangent,
    send_order,
    pair_index,
    edge_mask,
    distance,
    radial_weight,
    mix_weight,
    out_weight,
    *,
    n_dp,
    n_blk,
):
    rows, total = features.shape
    width = mix_weight.shape[1]
    pieces = 2 * n_blk
    shard = mix_weight.shape[0] // n_blk
    piece = math.gcd(shard, width)
    at_dp, at_blk = lax.axis_index("dp"), lax.axis_index("blk")
    place = jnp.stack([at_dp % 2 * n_blk + at_blk, at_blk * (shard // piece)]).astype(jnp.int32)

    def over_dp(value, step):
        return lax.ppermute(value, "dp", [(i, i ^ step) for i in range(n_dp)])

    def over_blk(value, step):
        return lax.ppermute(value, "blk", [(i, i ^ step) for i in range(n_blk)])

    def all_to_all(value):
        return lax.all_to_all(value, "dp", split_axis=0, concat_axis=0, tiled=True)

    def plane_sum(near, far):
        height = near.shape[0] // n_blk
        chip = near + over_dp(far, 1).astype(jnp.float32)
        own = chip[:height]
        for step in range(1, n_blk):
            part = chip[step * height : (step + 1) * height].astype(jnp.bfloat16)
            own = own + over_blk(part, step).astype(jnp.float32)
        return own

    def z_sum_direct(own):
        own = own.astype(jnp.bfloat16)
        return tree_sum([own] + [over_dp(own, 2 * step) for step in range(1, n_dp // 2)])

    bits = [1 << i for i in range((n_dp // 2).bit_length() - 1)]
    upper = [(at_dp // 2) & bit for bit in bits]

    def z_halved(own):
        for bit, high in zip(bits[:-1], upper):
            half = own.shape[0] // 2
            kept = jnp.where(high > 0, own[half:], own[:half])
            given = jnp.where(high > 0, own[:half], own[half:]).astype(jnp.bfloat16)
            own = kept + over_dp(given, 2 * bit).astype(jnp.float32)
        own = own.astype(jnp.bfloat16)
        return own, over_dp(own, 2 * bits[-1])

    def z_joined(own, other):
        own = tree_sum([own, other])
        for bit, high in reversed(list(zip(bits[:-1], upper))):
            other = over_dp(own, 2 * bit)
            own = jnp.where(
                high > 0,
                jnp.concatenate([other, own], axis=0),
                jnp.concatenate([own, other], axis=0),
            )
        return own

    def plane_gather(own, *others):
        near = [own] + [over_blk(own, step) for step in range(1, n_blk)]
        return near + [over_dp(after(part, *others), 1) for part in near]

    sent_most = pick_rows(send_order, features, width, MOST)
    came_most = all_to_all(sent_most)
    sent_last = pick_rows(send_order, after(features, sent_most), width, LAST)
    gate = gate_matrices(pair_index, edge_mask, after(distance, sent_last), radial_weight, rows)
    cotangent, mix_weight, out_weight = lax.optimization_barrier(
        (cotangent, mix_weight, out_weight, gate)
    )[:3]
    cots = [flip_cotangent(cotangent, width, level) for level in range(LMAX + 1)]
    maps = degree_products(mix_weight, out_weight)
    flipped = mix_weight.reshape(LMAX + 1, width, width).swapaxes(1, 2).reshape(mix_weight.shape)
    ready = (gate, maps, flipped, *cots)
    came_last = all_to_all(after(sent_last, came_most, *ready))

    local = after(came_most, *ready)
    own = plane_sum(*outer_sum(place, gate, local, cots, width, MOST, pieces))
    own, other = z_halved(own)
    updated = update(gate, maps, local, width, MOST, total, None)

    local = after(came_last, own, updated)
    near, far = outer_sum(place, gate, local, cots, width, LAST, pieces)
    most = plane_gather(z_joined(own, after(other, near)))
    last = z_sum_direct(plane_sum(near, far))
    updated = update(gate, maps, local, width, LAST, total, updated)
    mix_grad, out_grad = most_gradients(place, out_weight, flipped, most, shard, piece)
    last = plane_gather(after(last, updated, *most), mix_grad)
    mix_grad, out_grad = last_gradients(
        place, out_weight, flipped, last, mix_grad, out_grad, piece
    )
    return updated, mix_grad, out_grad


def solution(mesh):
    in_specs = (
        P(("dp", "blk"), None),
        P(("dp", "blk"), None),
        P(("dp", "blk"), None),
        P(("dp", "blk"), None),
        P(("dp", "blk"), None, None),
        P(("dp", "blk"), None, None),
        P(),
        P(),
        P(),
    )
    out_specs = (P(("dp", "blk"), None), P("blk", None), P("blk", None))
    run = functools.partial(body, n_dp=mesh.shape["dp"], n_blk=mesh.shape["blk"])
    return jax.shard_map(run, mesh=mesh, in_specs=in_specs, out_specs=out_specs, check_vma=False)
```

```python
import functools
import math

import jax
import jax.numpy as jnp
from jax import lax
from jax.experimental import pallas as pl
from jax.experimental.pallas import tpu as pltpu
from jax.sharding import PartitionSpec as P

LMAX = 4
BLOCK = 128
CUT_RADIUS = 5.0
EDGE_SCALE = 0.25
MOST, LAST = (0, 1, 2, 3), (4,)
ORDER = MOST + LAST
VMEM_LIMIT = 48 * 1024 * 1024
PICK_LIMIT = 60 * 1024 * 1024
GATE_ROWS = 16
WHOLE = pl.BlockSpec(memory_space=pltpu.VMEM)
ANY = pl.BlockSpec(memory_space=pl.ANY)
SCALARS = pl.BlockSpec(memory_space=pltpu.SMEM)


def params(*semantics, limit=VMEM_LIMIT):
    return pltpu.CompilerParams(dimension_semantics=semantics, vmem_limit_bytes=limit)


def after(value, *others):
    return lax.optimization_barrier((value, *others))[0]


def span(degrees):
    return degrees[0] ** 2, (degrees[-1] + 1) ** 2


def comps_of(degrees):
    return [comp for level in degrees for comp in range(*span((level,)))]


def tree_sum(parts):
    parts = [part.astype(jnp.float32) for part in parts]
    while len(parts) > 1:
        parts = [parts[i] + parts[i + 1] for i in range(0, len(parts), 2)]
    return parts[0].astype(jnp.bfloat16)


def chosen_rows(order_ref, rows):
    local = lax.broadcasted_iota(jnp.int32, (rows, rows), 0)
    return (local == order_ref[...]).astype(jnp.float32).T.astype(jnp.bfloat16)


def pick_kernel(order_ref, rows_ref, out_ref, held_ref, ready_ref, in_sems, out_sems, *, first):
    count, rows, width = ready_ref.shape
    slab = rows // in_sems.shape[0]
    loads = [
        pltpu.make_async_copy(
            rows_ref.at[pl.ds(i * slab, slab), pl.ds(first * width, count * width)],
            held_ref.at[pl.ds(i * slab, slab), :],
            in_sems.at[i],
        )
        for i in range(in_sems.shape[0])
    ]
    for load in loads:
        load.start()
    pick = chosen_rows(order_ref, rows)
    for load in loads:
        load.wait()
    stores = []
    for i in range(count):
        ready_ref[i] = jnp.dot(
            pick, held_ref[:, i * width : (i + 1) * width], preferred_element_type=jnp.float32
        ).astype(jnp.bfloat16)
        stores.append(
            pltpu.make_async_copy(
                ready_ref.at[i], out_ref.at[:, pl.ds(i * width, width)], out_sems.at[i]
            )
        )
        stores[-1].start()
    for store in stores:
        store.wait()


def pick_rows(order, features, width, degrees):
    rows = features.shape[0]
    first, last = span(degrees)
    count = last - first
    return pl.pallas_call(
        functools.partial(pick_kernel, first=first),
        in_specs=[WHOLE, ANY],
        out_specs=ANY,
        out_shape=jax.ShapeDtypeStruct((rows, count * width), jnp.bfloat16),
        scratch_shapes=[
            pltpu.VMEM((rows, count * width), jnp.bfloat16),
            pltpu.VMEM((count, rows, width), jnp.bfloat16),
            pltpu.SemaphoreType.DMA((8,)),
            pltpu.SemaphoreType.DMA((count,)),
        ],
        compiler_params=params(limit=PICK_LIMIT),
        name="pick_rows",
    )(order, features)


def gate_kernel(pairs_ref, mask_ref, dist_ref, weight_ref, out_ref, radial_ref, *, basis_count):
    pair, step = pl.program_id(0), pl.program_id(1)

    @pl.when((pair == 0) & (step == 0))
    def _():
        out_ref[...] = jnp.zeros_like(out_ref)

    half = math.sqrt(0.5 * math.log2(math.e))
    dist = dist_ref[0]
    scaled = dist * (half * (basis_count - 1) / CUT_RADIUS)
    centers = lax.broadcasted_iota(jnp.int32, (basis_count, BLOCK), 0).astype(jnp.float32) * half
    weights = weight_ref[...]
    levels = LMAX + 1
    for row in range(GATE_ROWS):
        offset = scaled[row : row + 1, :] - centers
        phi = jnp.exp2(-(offset * offset))
        high = phi.astype(jnp.bfloat16)
        low = (phi - high.astype(jnp.float32)).astype(jnp.bfloat16)
        radial = jnp.dot(weights, high, preferred_element_type=jnp.float32)
        radial = radial + jnp.dot(weights, low, preferred_element_type=jnp.float32)
        radial = radial[0:8] + radial[8:16]
        for level in range(levels):
            radial_ref[level, row : row + 1, :] = radial[level : level + 1, :]
    envelope = (
        (0.5 * EDGE_SCALE)
        * (jnp.cos((math.pi / CUT_RADIUS) * dist) + 1.0)
        * mask_ref[0].astype(jnp.float32)
    )
    dest = pl.multiple_of(pairs_ref[pair, 0] * BLOCK + step * GATE_ROWS, GATE_ROWS)
    src = pl.multiple_of(pairs_ref[pair, 1] * BLOCK, BLOCK)
    for level in range(levels):
        out_ref[level, pl.ds(dest, GATE_ROWS), pl.ds(src, BLOCK)] = (
            radial_ref[level] * envelope
        ).astype(jnp.bfloat16)


def gate_matrices(pairs, mask, dist, radial_weight, rows):
    count = pairs.shape[0]
    levels = radial_weight.shape[1]
    transposed = radial_weight.T
    high = transposed.astype(jnp.bfloat16)
    low = (transposed - high.astype(jnp.float32)).astype(jnp.bfloat16)
    pad = ((0, 8 - levels), (0, 0))
    weights = jnp.concatenate([jnp.pad(high, pad), jnp.pad(low, pad)], axis=0)
    kernel = functools.partial(gate_kernel, basis_count=radial_weight.shape[0])
    edges = pl.BlockSpec((1, GATE_ROWS, BLOCK), lambda p, s, pairs: (p, s, 0))
    return pl.pallas_call(
        kernel,
        grid_spec=pltpu.PrefetchScalarGridSpec(
            num_scalar_prefetch=1,
            grid=(count, BLOCK // GATE_ROWS),
            in_specs=[edges, edges, pl.BlockSpec(weights.shape, lambda p, s, pairs: (0, 0))],
            out_specs=pl.BlockSpec((levels, rows, rows), lambda p, s, pairs: (0, 0, 0)),
            scratch_shapes=[pltpu.VMEM((levels, GATE_ROWS, BLOCK), jnp.float32)],
        ),
        out_shape=jax.ShapeDtypeStruct((levels, rows, rows), jnp.bfloat16),
        compiler_params=params("arbitrary", "arbitrary"),
        cost_estimate=pl.CostEstimate(
            flops=2 * 3 * 512 * count * BLOCK * BLOCK * radial_weight.shape[0],
            bytes_accessed=2 * 4 * count * BLOCK * BLOCK,
            transcendentals=count * BLOCK * BLOCK * radial_weight.shape[0],
        ),
        name="gate",
    )(pairs, mask, dist, weights)


def product_kernel(left_ref, right_ref, out_ref):
    out_ref[...] = jnp.dot(
        left_ref[...], right_ref[...], preferred_element_type=jnp.float32
    ).astype(jnp.bfloat16)


def degree_products(left, right):
    width = left.shape[1]
    block = pl.BlockSpec((width, width), lambda i: (i, 0))
    return pl.pallas_call(
        product_kernel,
        grid=(left.shape[0] // width,),
        in_specs=[block, block],
        out_specs=block,
        out_shape=jax.ShapeDtypeStruct(left.shape, jnp.bfloat16),
        compiler_params=params("arbitrary"),
        name="degree_products",
    )(left, right)


def flip_kernel(rows_ref, out_ref):
    out_ref[...] = rows_ref[...].T


def flip_cotangent(cotangent, width, level):
    rows = cotangent.shape[0]
    first, last = span((level,))
    return pl.pallas_call(
        flip_kernel,
        grid=(last - first,),
        in_specs=[pl.BlockSpec((rows, width), lambda i: (0, first + i))],
        out_specs=pl.BlockSpec((width, rows), lambda i: (0, i)),
        out_shape=jax.ShapeDtypeStruct((width, (last - first) * rows), jnp.bfloat16),
        compiler_params=params("arbitrary"),
        name="flip_cotangent",
    )(cotangent)


def comp_loads(local_ref, held_ref, sems):
    width = held_ref.shape[2]
    loads = [
        pltpu.make_async_copy(local_ref.at[:, pl.ds(i * width, width)], held_ref.at[i], sems.at[i])
        for i in range(held_ref.shape[0])
    ]
    for load in loads:
        load.start()
    return loads


def outer_kernel(place_ref, gate_ref, local_ref, *refs, pieces, levels):
    cots = refs[: len(levels)]
    near_ref, far_ref, held_ref, cot_ref, mixed_ref, sum_ref, sems, cot_sems = refs[len(levels) :]
    rows, width = held_ref.shape[1:]
    loads = comp_loads(local_ref, held_ref, sems)
    cot_loads, at = [], 0
    for slot, cot in enumerate(cots):
        to = cot_ref.at[:, pl.ds(at, cot.shape[1])]
        cot_loads.append(pltpu.make_async_copy(cot, to, cot_sems.at[slot]))
        cot_loads[-1].start()
        at += cot.shape[1]
    index, at = 0, 0
    for slot, level in enumerate(levels):
        depth = (2 * level + 1) * rows
        for row in range(0, depth, rows):
            loads[index].wait()
            mixed_ref[row : row + rows, :] = jnp.dot(
                gate_ref[level], held_ref[index], preferred_element_type=jnp.float32
            ).astype(jnp.bfloat16)
            index += 1
        cot_loads[slot].wait()
        flipped = jnp.dot(
            cot_ref[:, at : at + depth], mixed_ref[0:depth, :], preferred_element_type=jnp.float32
        )
        sum_ref[slot * width : (slot + 1) * width, :] = flipped.T
        at += depth
    half, height = pieces // 2, width // pieces
    for step in range(half):
        near = pl.multiple_of((place_ref[0] ^ step) * height, height)
        far = pl.multiple_of((place_ref[0] ^ (step + half)) * height, height)
        for slot in range(len(levels)):
            to = (step * len(levels) + slot) * height
            near_ref[to : to + height, :] = sum_ref[pl.ds(slot * width + near, height), :]
            far_ref[to : to + height, :] = sum_ref[pl.ds(slot * width + far, height), :].astype(
                jnp.bfloat16
            )


def outer_sum(place, gate, local, cots, width, levels, pieces):
    rows = gate.shape[1]
    whole = len(levels) * width
    deepest = 2 * max(levels) + 1
    total = sum(2 * level + 1 for level in levels)
    return pl.pallas_call(
        functools.partial(outer_kernel, pieces=pieces, levels=levels),
        in_specs=[SCALARS, WHOLE] + [ANY] * (1 + len(levels)),
        out_specs=[WHOLE] * 2,
        out_shape=[
            jax.ShapeDtypeStruct((whole // 2, width), jnp.float32),
            jax.ShapeDtypeStruct((whole // 2, width), jnp.bfloat16),
        ],
        scratch_shapes=[
            pltpu.VMEM((total, rows, width), jnp.bfloat16),
            pltpu.VMEM((width, total * rows), jnp.bfloat16),
            pltpu.VMEM((deepest * rows, width), jnp.bfloat16),
            pltpu.VMEM((whole, width), jnp.float32),
            pltpu.SemaphoreType.DMA((total,)),
            pltpu.SemaphoreType.DMA((len(levels),)),
        ],
        compiler_params=params(),
        cost_estimate=pl.CostEstimate(
            flops=2 * total * rows * width * (rows + width),
            bytes_accessed=4 * total * rows * width,
            transcendentals=0,
        ),
        name="outer_sum",
    )(place, gate, local, *[cots[level] for level in levels])


def update_kernel(gate_ref, map_ref, local_ref, *refs, degrees):
    out_ref, held_ref, maps_ref, ready_ref, sems, map_sems, out_sems = refs[-7:]
    width = held_ref.shape[2]
    loads = comp_loads(local_ref, held_ref, sems)
    map_loads = []
    for slot, level in enumerate(degrees):
        rows = pl.ds(level * width, width)
        map_loads.append(
            pltpu.make_async_copy(map_ref.at[rows, :], maps_ref.at[slot], map_sems.at[slot])
        )
        map_loads[-1].start()
    copies = []
    for index, comp in enumerate(comps_of(degrees)):
        level = math.isqrt(comp)
        slot = degrees.index(level)
        loads[index].wait()
        if comp == level * level:
            map_loads[slot].wait()
        hidden = held_ref[index]
        mixed = jnp.dot(gate_ref[level], hidden, preferred_element_type=jnp.float32)
        added = jnp.dot(
            mixed.astype(jnp.bfloat16), maps_ref[slot], preferred_element_type=jnp.float32
        )
        ready_ref[index] = (hidden.astype(jnp.float32) + added).astype(jnp.bfloat16)
        copies.append(
            pltpu.make_async_copy(
                ready_ref.at[index],
                out_ref.at[:, pl.ds(comp * width, width)],
                out_sems.at[index],
            )
        )
        copies[-1].start()
    for copy in copies:
        copy.wait()


def update(gate, maps, local, width, degrees, total, held):
    rows = gate.shape[1]
    count = len(comps_of(degrees))
    in_specs = [WHOLE, ANY, ANY]
    operands = [gate, maps, local]
    aliases = {}
    if held is not None:
        in_specs.append(ANY)
        operands.append(held)
        aliases = {3: 0}
    return pl.pallas_call(
        functools.partial(update_kernel, degrees=degrees),
        in_specs=in_specs,
        out_specs=ANY,
        out_shape=jax.ShapeDtypeStruct((rows, total), jnp.bfloat16),
        scratch_shapes=[
            pltpu.VMEM((count, rows, width), jnp.bfloat16),
            pltpu.VMEM((len(degrees), width, width), jnp.bfloat16),
            pltpu.VMEM((count, rows, width), jnp.bfloat16),
            pltpu.SemaphoreType.DMA((count,)),
            pltpu.SemaphoreType.DMA((len(degrees),)),
            pltpu.SemaphoreType.DMA((count,)),
        ],
        input_output_aliases=aliases,
        compiler_params=params(),
        cost_estimate=pl.CostEstimate(
            flops=2 * count * rows * width * (rows + width),
            bytes_accessed=4 * count * rows * width,
            transcendentals=0,
        ),
        name="update",
    )(*operands)


def place_parts(place_ref, parts, outer_ref):
    width = outer_ref.shape[1]
    height = width // len(parts)
    for step, part in enumerate(parts):
        row = pl.multiple_of((place_ref[0] ^ step) * height, height)
        for slot in range(part.shape[0] // height):
            outer_ref[pl.ds(slot * width + row, height), :] = part[
                slot * height : (slot + 1) * height, :
            ]


def gradients(rows, outer, flipped, weight):
    mix = lax.dot_general(
        rows, weight, (((1,), (1,)), ((), ())), preferred_element_type=jnp.float32
    )
    return mix, jnp.dot(flipped, outer, preferred_element_type=jnp.float32)


def most_kernel(place_ref, weight_ref, flip_ref, *refs, piece):
    *parts, mix_ref, out_ref, outer_ref = refs
    width = weight_ref.shape[0]

    @pl.when(pl.program_id(0) == 0)
    def _():
        place_parts(place_ref, parts, outer_ref)

    row = (place_ref[1] + pl.program_id(0)) * piece

    @pl.when(row < len(MOST) * width)
    def _():
        first = pl.multiple_of((row // width - place_ref[2]) * width, width)
        mix_ref[...], out_ref[...] = gradients(
            outer_ref[pl.ds(pl.multiple_of(first + row % width, piece), piece), :],
            outer_ref[pl.ds(first, width), :],
            flip_ref[...],
            weight_ref[...],
        )


def most_gradients(place, weight, flipped, parts, shard, piece):
    width = weight.shape[1]
    whole = pl.BlockSpec(parts[0].shape, lambda i, place: (0, 0))
    return pl.pallas_call(
        functools.partial(most_kernel, piece=piece),
        grid_spec=pltpu.PrefetchScalarGridSpec(
            num_scalar_prefetch=1,
            grid=(shard // piece,),
            in_specs=[
                pl.BlockSpec(
                    (width, width), lambda i, place: ((place[1] + i) * piece // width, 0)
                ),
                pl.BlockSpec((piece, width), lambda i, place: (place[1] + i, 0)),
            ]
            + [whole] * len(parts),
            out_specs=[pl.BlockSpec((piece, width), lambda i, place: (i, 0))] * 2,
            scratch_shapes=[pltpu.VMEM((len(parts) * parts[0].shape[0], width), jnp.bfloat16)],
        ),
        out_shape=[jax.ShapeDtypeStruct((shard, width), jnp.float32)] * 2,
        compiler_params=params("arbitrary"),
        name="most_gradients",
    )(place, weight, flipped, *parts)


def last_kernel(place_ref, weight_ref, flip_ref, *refs, piece):
    *parts, _, _, mix_out, out_out, outer_ref, mix_ref, out_ref, sems = refs
    width = weight_ref.shape[0]
    place_parts(place_ref, parts, outer_ref)
    count = mix_ref.shape[0]

    def each(index):
        row = (place_ref[1] + index) * piece - LAST[0] * width
        to = pl.ds(index * piece, piece)
        copies = [
            pltpu.make_async_copy(mix_ref.at[index], mix_out.at[to, :], sems.at[index, 0]),
            pltpu.make_async_copy(out_ref.at[index], out_out.at[to, :], sems.at[index, 1]),
        ]
        return row, (row >= 0) & (row < width), copies

    for index in range(count):
        row, held, copies = each(index)

        @pl.when(held)
        def _():
            mine = pl.ds(pl.multiple_of(row, piece), piece)
            mix_ref[index], out_ref[index] = gradients(
                outer_ref[mine, :], outer_ref[...], flip_ref[mine, :], weight_ref[...]
            )
            for copy in copies:
                copy.start()

    for index in range(count):
        _, held, copies = each(index)

        @pl.when(held)
        def _():
            for copy in copies:
                copy.wait()


def last_gradients(place, weight, flipped, parts, mix_grad, out_grad, piece):
    shard, width = mix_grad.shape
    own = pl.BlockSpec((width, width), lambda i: (LAST[0], 0))
    whole = pl.BlockSpec(parts[0].shape, lambda i: (0, 0))
    count = shard // piece
    return pl.pallas_call(
        functools.partial(last_kernel, piece=piece),
        grid=(1,),
        in_specs=[SCALARS, own, own] + [whole] * len(parts) + [ANY] * 2,
        out_specs=[ANY] * 2,
        out_shape=[jax.ShapeDtypeStruct(mix_grad.shape, jnp.float32)] * 2,
        scratch_shapes=[
            pltpu.VMEM((width, width), jnp.bfloat16),
            pltpu.VMEM((count, piece, width), jnp.float32),
            pltpu.VMEM((count, piece, width), jnp.float32),
            pltpu.SemaphoreType.DMA((count, 2)),
        ],
        input_output_aliases={3 + len(parts): 0, 4 + len(parts): 1},
        compiler_params=params("arbitrary"),
        name="last_gradients",
    )(place, weight, flipped, *parts, mix_grad, out_grad)


def body(
    features,
    cotangent,
    send_order,
    pair_index,
    edge_mask,
    distance,
    radial_weight,
    mix_weight,
    out_weight,
    *,
    n_dp,
    n_blk,
):
    rows, total = features.shape
    width = mix_weight.shape[1]
    pieces = 2 * n_blk
    shard = mix_weight.shape[0] // n_blk
    piece = math.gcd(shard, width)
    at_dp, at_blk = lax.axis_index("dp"), lax.axis_index("blk")
    reach = max(((i + 1) * shard - 1) // width - i * shard // width + 1 for i in range(n_blk))
    reach = min(reach, len(MOST))

    def first_degree(at):
        return jnp.minimum(at * shard // width, len(MOST) - reach)

    place = jnp.stack(
        [at_dp % 2 * n_blk + at_blk, at_blk * (shard // piece), first_degree(at_blk)]
    ).astype(jnp.int32)

    def over_dp(value, step):
        return lax.ppermute(value, "dp", [(i, i ^ step) for i in range(n_dp)])

    def over_blk(value, step):
        return lax.ppermute(value, "blk", [(i, i ^ step) for i in range(n_blk)])

    def all_to_all(value):
        return lax.all_to_all(value, "dp", split_axis=0, concat_axis=0, tiled=True)

    def plane_sum(near, far):
        height = near.shape[0] // n_blk
        chip = near + over_dp(far, 1).astype(jnp.float32)
        own = chip[:height]
        for step in range(1, n_blk):
            part = chip[step * height : (step + 1) * height].astype(jnp.bfloat16)
            own = own + over_blk(part, step).astype(jnp.float32)
        return own

    bits = [1 << i for i in range((n_dp // 2).bit_length() - 1)]
    upper = [(at_dp // 2) & bit for bit in bits]

    def z_halved(own):
        for bit, high in zip(bits[:-1], upper):
            half = own.shape[0] // 2
            kept = jnp.where(high > 0, own[half:], own[:half])
            given = jnp.where(high > 0, own[:half], own[half:]).astype(jnp.bfloat16)
            own = kept + over_dp(given, 2 * bit).astype(jnp.float32)
        own = own.astype(jnp.bfloat16)
        return own, over_dp(own, 2 * bits[-1])

    def z_joined(own, *others):
        for bit, high in reversed(list(zip(bits[:-1], upper))):
            other = after(over_dp(own, 2 * bit), *others)
            own = jnp.where(
                high > 0,
                jnp.concatenate([other, own], axis=0),
                jnp.concatenate([own, other], axis=0),
            )
        return own

    def plane_gather(own, needed, *others):
        near = [needed(own, at_blk)]
        near += [over_blk(needed(own, at_blk ^ step), step) for step in range(1, n_blk)]
        return near + [over_dp(after(part, *others), 1) for part in near]

    def needed_degrees(own, at):
        height = width // pieces
        return lax.dynamic_slice_in_dim(own, first_degree(at) * height, reach * height, axis=0)

    sent_most = pick_rows(send_order, features, width, MOST)
    came_most = all_to_all(sent_most)
    sent_last = pick_rows(send_order, after(features, sent_most), width, LAST)
    gate = gate_matrices(pair_index, edge_mask, after(distance, sent_last), radial_weight, rows)
    cotangent, mix_weight, out_weight = lax.optimization_barrier(
        (cotangent, mix_weight, out_weight, gate)
    )[:3]
    cots = [flip_cotangent(cotangent, width, level) for level in range(LMAX + 1)]
    maps = degree_products(mix_weight, out_weight)
    flipped = mix_weight.reshape(LMAX + 1, width, width).swapaxes(1, 2).reshape(mix_weight.shape)
    ready = (gate, maps, flipped, *cots)
    came_last = all_to_all(after(sent_last, came_most, *ready))

    local = after(came_most, *ready)
    own = plane_sum(*outer_sum(place, gate, local, cots, width, MOST, pieces))
    own, other = z_halved(own)
    updated = update(gate, maps, local, width, MOST, total, None)

    most = tree_sum([own, after(other, came_last)])
    local = after(came_last, updated, most)
    near, far = outer_sum(place, gate, local, cots, width, LAST, pieces)
    last = plane_sum(near, far).astype(jnp.bfloat16)
    most = z_joined(most, last)
    others = [over_dp(last, 2 * step) for step in range(1, n_dp // 2)]
    most = plane_gather(after(most, others[0]), needed_degrees)
    last = tree_sum([last, *others])
    updated = update(gate, maps, local, width, LAST, total, updated)
    mix_grad, out_grad = most_gradients(place, out_weight, flipped, most, shard, piece)
    last = plane_gather(after(last, updated), lambda own, at: own, mix_grad)
    mix_grad, out_grad = last_gradients(
        place, out_weight, flipped, last, mix_grad, out_grad, piece
    )
    return updated, mix_grad, out_grad


def solution(mesh):
    in_specs = (
        P(("dp", "blk"), None),
        P(("dp", "blk"), None),
        P(("dp", "blk"), None),
        P(("dp", "blk"), None),
        P(("dp", "blk"), None, None),
        P(("dp", "blk"), None, None),
        P(),
        P(),
        P(),
    )
    out_specs = (P(("dp", "blk"), None), P("blk", None), P("blk", None))
    run = functools.partial(body, n_dp=mesh.shape["dp"], n_blk=mesh.shape["blk"])
    return jax.shard_map(run, mesh=mesh, in_specs=in_specs, out_specs=out_specs, check_vma=False)
```

```python
import functools
import math

import jax
import jax.numpy as jnp
from jax import lax
from jax.experimental import pallas as pl
from jax.experimental.pallas import tpu as pltpu
from jax.sharding import PartitionSpec as P

LMAX = 4
BLOCK = 128
CUT_RADIUS = 5.0
EDGE_SCALE = 0.25
MOST, LAST = (0, 1, 2, 3), (4,)
ORDER = MOST + LAST
VMEM_LIMIT = 20 * 1024 * 1024
PICK_LIMIT = 60 * 1024 * 1024
GATE_ROWS = 16
WHOLE = pl.BlockSpec(memory_space=pltpu.VMEM)
ANY = pl.BlockSpec(memory_space=pl.ANY)
SCALARS = pl.BlockSpec(memory_space=pltpu.SMEM)


def params(*semantics, limit=VMEM_LIMIT):
    return pltpu.CompilerParams(dimension_semantics=semantics, vmem_limit_bytes=limit)


def after(value, *others):
    return lax.optimization_barrier((value, *others))[0]


def span(degrees):
    return degrees[0] ** 2, (degrees[-1] + 1) ** 2


def comps_of(degrees):
    return [comp for level in degrees for comp in range(*span((level,)))]


def tree_sum(parts):
    parts = [part.astype(jnp.float32) for part in parts]
    while len(parts) > 1:
        parts = [parts[i] + parts[i + 1] for i in range(0, len(parts), 2)]
    return parts[0].astype(jnp.bfloat16)


def chosen_rows(order_ref, rows):
    local = lax.broadcasted_iota(jnp.int32, (rows, rows), 0)
    return (local == order_ref[...]).astype(jnp.float32).T.astype(jnp.bfloat16)


def pick_kernel(order_ref, rows_ref, out_ref, held_ref, ready_ref, in_sems, out_sems, *, first):
    count, rows, width = ready_ref.shape
    slab = rows // in_sems.shape[0]
    loads = [
        pltpu.make_async_copy(
            rows_ref.at[pl.ds(i * slab, slab), pl.ds(first * width, count * width)],
            held_ref.at[pl.ds(i * slab, slab), :],
            in_sems.at[i],
        )
        for i in range(in_sems.shape[0])
    ]
    for load in loads:
        load.start()
    pick = chosen_rows(order_ref, rows)
    for load in loads:
        load.wait()
    stores = []
    for i in range(count):
        ready_ref[i] = jnp.dot(
            pick, held_ref[:, i * width : (i + 1) * width], preferred_element_type=jnp.float32
        ).astype(jnp.bfloat16)
        stores.append(
            pltpu.make_async_copy(
                ready_ref.at[i], out_ref.at[:, pl.ds(i * width, width)], out_sems.at[i]
            )
        )
        stores[-1].start()
    for store in stores:
        store.wait()


def pick_rows(order, features, width, degrees):
    rows = features.shape[0]
    first, last = span(degrees)
    count = last - first
    return pl.pallas_call(
        functools.partial(pick_kernel, first=first),
        in_specs=[WHOLE, ANY],
        out_specs=ANY,
        out_shape=jax.ShapeDtypeStruct((rows, count * width), jnp.bfloat16),
        scratch_shapes=[
            pltpu.VMEM((rows, count * width), jnp.bfloat16),
            pltpu.VMEM((count, rows, width), jnp.bfloat16),
            pltpu.SemaphoreType.DMA((8,)),
            pltpu.SemaphoreType.DMA((count,)),
        ],
        compiler_params=params(limit=PICK_LIMIT),
        name="pick_rows",
    )(order, features)


def gate_kernel(pairs_ref, mask_ref, dist_ref, weight_ref, out_ref, radial_ref, *, basis_count):
    pair, step = pl.program_id(0), pl.program_id(1)

    @pl.when((pair == 0) & (step == 0))
    def _():
        out_ref[...] = jnp.zeros_like(out_ref)

    half = math.sqrt(0.5 * math.log2(math.e))
    dist = dist_ref[0]
    scaled = dist * (half * (basis_count - 1) / CUT_RADIUS)
    centers = lax.broadcasted_iota(jnp.int32, (basis_count, BLOCK), 0).astype(jnp.float32) * half
    weights = weight_ref[...]
    levels = LMAX + 1
    for row in range(GATE_ROWS):
        offset = scaled[row : row + 1, :] - centers
        phi = jnp.exp2(-(offset * offset))
        high = phi.astype(jnp.bfloat16)
        low = (phi - high.astype(jnp.float32)).astype(jnp.bfloat16)
        radial = jnp.dot(weights, high, preferred_element_type=jnp.float32)
        radial = radial + jnp.dot(weights, low, preferred_element_type=jnp.float32)
        radial = radial[0:8] + radial[8:16]
        for level in range(levels):
            radial_ref[level, row : row + 1, :] = radial[level : level + 1, :]
    envelope = (
        (0.5 * EDGE_SCALE)
        * (jnp.cos((math.pi / CUT_RADIUS) * dist) + 1.0)
        * mask_ref[0].astype(jnp.float32)
    )
    dest = pl.multiple_of(pairs_ref[pair, 0] * BLOCK + step * GATE_ROWS, GATE_ROWS)
    src = pl.multiple_of(pairs_ref[pair, 1] * BLOCK, BLOCK)
    for level in range(levels):
        out_ref[level, pl.ds(dest, GATE_ROWS), pl.ds(src, BLOCK)] = (
            radial_ref[level] * envelope
        ).astype(jnp.bfloat16)


def gate_matrices(pairs, mask, dist, radial_weight, rows):
    count = pairs.shape[0]
    levels = radial_weight.shape[1]
    transposed = radial_weight.T
    high = transposed.astype(jnp.bfloat16)
    low = (transposed - high.astype(jnp.float32)).astype(jnp.bfloat16)
    pad = ((0, 8 - levels), (0, 0))
    weights = jnp.concatenate([jnp.pad(high, pad), jnp.pad(low, pad)], axis=0)
    kernel = functools.partial(gate_kernel, basis_count=radial_weight.shape[0])
    edges = pl.BlockSpec((1, GATE_ROWS, BLOCK), lambda p, s, pairs: (p, s, 0))
    return pl.pallas_call(
        kernel,
        grid_spec=pltpu.PrefetchScalarGridSpec(
            num_scalar_prefetch=1,
            grid=(count, BLOCK // GATE_ROWS),
            in_specs=[edges, edges, pl.BlockSpec(weights.shape, lambda p, s, pairs: (0, 0))],
            out_specs=pl.BlockSpec((levels, rows, rows), lambda p, s, pairs: (0, 0, 0)),
            scratch_shapes=[pltpu.VMEM((levels, GATE_ROWS, BLOCK), jnp.float32)],
        ),
        out_shape=jax.ShapeDtypeStruct((levels, rows, rows), jnp.bfloat16),
        compiler_params=params("arbitrary", "arbitrary"),
        cost_estimate=pl.CostEstimate(
            flops=2 * 3 * 512 * count * BLOCK * BLOCK * radial_weight.shape[0],
            bytes_accessed=2 * 4 * count * BLOCK * BLOCK,
            transcendentals=count * BLOCK * BLOCK * radial_weight.shape[0],
        ),
        name="gate",
    )(pairs, mask, dist, weights)


def product_kernel(left_ref, right_ref, out_ref):
    out_ref[...] = jnp.dot(
        left_ref[...], right_ref[...], preferred_element_type=jnp.float32
    ).astype(jnp.bfloat16)


def degree_products(left, right):
    width = left.shape[1]
    block = pl.BlockSpec((width, width), lambda i: (i, 0))
    return pl.pallas_call(
        product_kernel,
        grid=(left.shape[0] // width,),
        in_specs=[block, block],
        out_specs=block,
        out_shape=jax.ShapeDtypeStruct(left.shape, jnp.bfloat16),
        compiler_params=params("arbitrary"),
        name="degree_products",
    )(left, right)


def flip_kernel(rows_ref, out_ref):
    out_ref[...] = rows_ref[...].T


def flip_cotangent(cotangent, width, level):
    rows = cotangent.shape[0]
    first, last = span((level,))
    return pl.pallas_call(
        flip_kernel,
        grid=(last - first,),
        in_specs=[pl.BlockSpec((rows, width), lambda i: (0, first + i))],
        out_specs=pl.BlockSpec((width, rows), lambda i: (0, i)),
        out_shape=jax.ShapeDtypeStruct((width, (last - first) * rows), jnp.bfloat16),
        compiler_params=params("arbitrary"),
        name="flip_cotangent",
    )(cotangent)


def outer_kernel(place_ref, gate_ref, local_ref, *refs, pieces, levels):
    cots = refs[: len(levels)]
    near_ref, far_ref, mixed_ref, sum_ref = refs[len(levels) :]
    rows, width = local_ref.shape[0], mixed_ref.shape[1]
    comps = comps_of(levels)
    for slot, level in enumerate(levels):
        first, last = span((level,))
        for comp in range(first, last):
            at = comps.index(comp) * width
            mixed_ref[(comp - first) * rows : (comp - first + 1) * rows, :] = jnp.dot(
                gate_ref[level], local_ref[:, at : at + width], preferred_element_type=jnp.float32
            ).astype(jnp.bfloat16)
        depth = (last - first) * rows
        flipped = jnp.dot(
            cots[slot][...], mixed_ref[0:depth, :], preferred_element_type=jnp.float32
        )
        sum_ref[slot * width : (slot + 1) * width, :] = flipped.T
    half, height = pieces // 2, width // pieces
    for step in range(half):
        near = pl.multiple_of((place_ref[0] ^ step) * height, height)
        far = pl.multiple_of((place_ref[0] ^ (step + half)) * height, height)
        for slot in range(len(levels)):
            to = (step * len(levels) + slot) * height
            near_ref[to : to + height, :] = sum_ref[pl.ds(slot * width + near, height), :]
            far_ref[to : to + height, :] = sum_ref[pl.ds(slot * width + far, height), :].astype(
                jnp.bfloat16
            )


def outer_sum(place, gate, local, cots, width, levels, pieces):
    rows = gate.shape[1]
    whole = len(levels) * width
    deepest = 2 * max(levels) + 1
    total = sum(2 * level + 1 for level in levels)
    return pl.pallas_call(
        functools.partial(outer_kernel, pieces=pieces, levels=levels),
        in_specs=[SCALARS] + [WHOLE] * (2 + len(levels)),
        out_specs=[WHOLE] * 2,
        out_shape=[
            jax.ShapeDtypeStruct((whole // 2, width), jnp.float32),
            jax.ShapeDtypeStruct((whole // 2, width), jnp.bfloat16),
        ],
        scratch_shapes=[
            pltpu.VMEM((deepest * rows, width), jnp.bfloat16),
            pltpu.VMEM((whole, width), jnp.float32),
        ],
        compiler_params=params(),
        cost_estimate=pl.CostEstimate(
            flops=2 * total * rows * width * (rows + width),
            bytes_accessed=4 * total * rows * width,
            transcendentals=0,
        ),
        name="outer_sum",
    )(place, gate, local, *[cots[level] for level in levels])


def update_kernel(gate_ref, map_ref, local_ref, *refs, comps, base):
    out_ref, ready_ref, sems = refs[-3:]
    width = map_ref.shape[1]
    copies = []
    for index, comp in enumerate(comps):
        level = math.isqrt(comp)
        at = (comp - base) * width
        hidden = local_ref[:, at : at + width]
        mixed = jnp.dot(gate_ref[level], hidden, preferred_element_type=jnp.float32)
        added = jnp.dot(
            mixed.astype(jnp.bfloat16),
            map_ref[level * width : (level + 1) * width, :],
            preferred_element_type=jnp.float32,
        )
        ready_ref[index] = (hidden.astype(jnp.float32) + added).astype(jnp.bfloat16)
        copies.append(
            pltpu.make_async_copy(
                ready_ref.at[index],
                out_ref.at[:, pl.ds(comp * width, width)],
                sems.at[index],
            )
        )
        copies[-1].start()
    for copy in copies:
        copy.wait()


def update(gate, maps, local, width, comps, base, total, held):
    rows = gate.shape[1]
    count = len(comps)
    in_specs = [WHOLE] * 3
    operands = [gate, maps, local]
    aliases = {}
    if held is not None:
        in_specs.append(ANY)
        operands.append(held)
        aliases = {3: 0}
    return pl.pallas_call(
        functools.partial(update_kernel, comps=comps, base=base),
        in_specs=in_specs,
        out_specs=ANY,
        out_shape=jax.ShapeDtypeStruct((rows, total), jnp.bfloat16),
        scratch_shapes=[
            pltpu.VMEM((count, rows, width), jnp.bfloat16),
            pltpu.SemaphoreType.DMA((count,)),
        ],
        input_output_aliases=aliases,
        compiler_params=params(),
        cost_estimate=pl.CostEstimate(
            flops=2 * count * rows * width * (rows + width),
            bytes_accessed=4 * count * rows * width,
            transcendentals=0,
        ),
        name="update",
    )(*operands)


def place_parts(place_ref, parts, outer_ref):
    width = outer_ref.shape[1]
    height = width // len(parts)
    for step, part in enumerate(parts):
        row = pl.multiple_of((place_ref[0] ^ step) * height, height)
        for slot in range(part.shape[0] // height):
            outer_ref[pl.ds(slot * width + row, height), :] = part[
                slot * height : (slot + 1) * height, :
            ]


def gradients(rows, outer, flipped, weight):
    mix = jnp.dot(rows, weight, preferred_element_type=jnp.float32)
    return mix, jnp.dot(flipped, outer, preferred_element_type=jnp.float32)


def most_kernel(place_ref, weight_ref, flip_ref, *refs, piece):
    *parts, mix_ref, out_ref, outer_ref = refs
    width = weight_ref.shape[0]

    @pl.when(pl.program_id(0) == 0)
    def _():
        place_parts(place_ref, parts, outer_ref)

    row = (place_ref[1] + pl.program_id(0)) * piece

    @pl.when(row < len(MOST) * width)
    def _():
        first = pl.multiple_of((row // width - place_ref[2]) * width, width)
        mix_ref[...], out_ref[...] = gradients(
            outer_ref[pl.ds(pl.multiple_of(first + row % width, piece), piece), :],
            outer_ref[pl.ds(first, width), :],
            flip_ref[...],
            weight_ref[...],
        )


def most_gradients(place, weight, flipped, parts, shard, piece):
    width = weight.shape[1]
    whole = pl.BlockSpec(parts[0].shape, lambda i, place: (0, 0))
    return pl.pallas_call(
        functools.partial(most_kernel, piece=piece),
        grid_spec=pltpu.PrefetchScalarGridSpec(
            num_scalar_prefetch=1,
            grid=(shard // piece,),
            in_specs=[
                pl.BlockSpec(
                    (width, width), lambda i, place: ((place[1] + i) * piece // width, 0)
                ),
                pl.BlockSpec((piece, width), lambda i, place: (place[1] + i, 0)),
            ]
            + [whole] * len(parts),
            out_specs=[pl.BlockSpec((piece, width), lambda i, place: (i, 0))] * 2,
            scratch_shapes=[pltpu.VMEM((len(parts) * parts[0].shape[0], width), jnp.bfloat16)],
        ),
        out_shape=[jax.ShapeDtypeStruct((shard, width), jnp.float32)] * 2,
        compiler_params=params("arbitrary"),
        name="most_gradients",
    )(place, weight, flipped, *parts)


def last_kernel(place_ref, weight_ref, flip_ref, *refs, piece):
    *parts, _, _, mix_out, out_out, outer_ref, mix_ref, out_ref, sems = refs
    width = weight_ref.shape[0]
    place_parts(place_ref, parts, outer_ref)
    count = mix_ref.shape[0]

    def each(index):
        row = (place_ref[1] + index) * piece - LAST[0] * width
        to = pl.ds(index * piece, piece)
        copies = [
            pltpu.make_async_copy(mix_ref.at[index], mix_out.at[to, :], sems.at[index, 0]),
            pltpu.make_async_copy(out_ref.at[index], out_out.at[to, :], sems.at[index, 1]),
        ]
        return row, (row >= 0) & (row < width), copies

    for index in range(count):
        row, held, copies = each(index)

        @pl.when(held)
        def _():
            mine = pl.ds(pl.multiple_of(row, piece), piece)
            mix_ref[index], out_ref[index] = gradients(
                outer_ref[mine, :], outer_ref[...], flip_ref[mine, :], weight_ref[...]
            )
            for copy in copies:
                copy.start()

    for index in range(count):
        _, held, copies = each(index)

        @pl.when(held)
        def _():
            for copy in copies:
                copy.wait()


def last_gradients(place, weight, flipped, parts, mix_grad, out_grad, piece):
    shard, width = mix_grad.shape
    own = pl.BlockSpec((width, width), lambda i: (LAST[0], 0))
    whole = pl.BlockSpec(parts[0].shape, lambda i: (0, 0))
    count = shard // piece
    return pl.pallas_call(
        functools.partial(last_kernel, piece=piece),
        grid=(1,),
        in_specs=[SCALARS, own, own] + [whole] * len(parts) + [ANY] * 2,
        out_specs=[ANY] * 2,
        out_shape=[jax.ShapeDtypeStruct(mix_grad.shape, jnp.float32)] * 2,
        scratch_shapes=[
            pltpu.VMEM((width, width), jnp.bfloat16),
            pltpu.VMEM((count, piece, width), jnp.float32),
            pltpu.VMEM((count, piece, width), jnp.float32),
            pltpu.SemaphoreType.DMA((count, 2)),
        ],
        input_output_aliases={3 + len(parts): 0, 4 + len(parts): 1},
        compiler_params=params("arbitrary"),
        name="last_gradients",
    )(place, weight, flipped, *parts, mix_grad, out_grad)


def body(
    features,
    cotangent,
    send_order,
    pair_index,
    edge_mask,
    distance,
    radial_weight,
    mix_weight,
    out_weight,
    *,
    n_dp,
    n_blk,
):
    rows, total = features.shape
    width = mix_weight.shape[1]
    pieces = 2 * n_blk
    shard = mix_weight.shape[0] // n_blk
    piece = math.gcd(shard, width)
    at_dp, at_blk = lax.axis_index("dp"), lax.axis_index("blk")
    reach = max(((i + 1) * shard - 1) // width - i * shard // width + 1 for i in range(n_blk))
    reach = min(reach, len(MOST))

    def first_degree(at):
        return jnp.minimum(at * shard // width, len(MOST) - reach)

    place = jnp.stack(
        [at_dp % 2 * n_blk + at_blk, at_blk * (shard // piece), first_degree(at_blk)]
    ).astype(jnp.int32)

    def over_dp(value, step):
        return lax.ppermute(value, "dp", [(i, i ^ step) for i in range(n_dp)])

    def over_blk(value, step):
        return lax.ppermute(value, "blk", [(i, i ^ step) for i in range(n_blk)])

    def all_to_all(value):
        return lax.all_to_all(value, "dp", split_axis=0, concat_axis=0, tiled=True)

    def plane_sum(near, far):
        height = near.shape[0] // n_blk
        chip = near + over_dp(far, 1).astype(jnp.float32)
        own = chip[:height]
        for step in range(1, n_blk):
            part = chip[step * height : (step + 1) * height].astype(jnp.bfloat16)
            own = own + over_blk(part, step).astype(jnp.float32)
        return own

    bits = [1 << i for i in range((n_dp // 2).bit_length() - 1)]
    upper = [(at_dp // 2) & bit for bit in bits]

    def z_halved(own):
        for bit, high in zip(bits[:-1], upper):
            half = own.shape[0] // 2
            kept = jnp.where(high > 0, own[half:], own[:half])
            given = jnp.where(high > 0, own[:half], own[half:]).astype(jnp.bfloat16)
            own = kept + over_dp(given, 2 * bit).astype(jnp.float32)
        own = own.astype(jnp.bfloat16)
        return own, over_dp(own, 2 * bits[-1])

    def z_joined(own, *others):
        for bit, high in reversed(list(zip(bits[:-1], upper))):
            other = after(over_dp(own, 2 * bit), *others)
            own = jnp.where(
                high > 0,
                jnp.concatenate([other, own], axis=0),
                jnp.concatenate([own, other], axis=0),
            )
        return own

    def plane_gather(own, needed, *others):
        near = [needed(own, at_blk)]
        near += [over_blk(needed(own, at_blk ^ step), step) for step in range(1, n_blk)]
        return near + [over_dp(after(part, *others), 1) for part in near]

    def needed_degrees(own, at):
        height = width // pieces
        return lax.dynamic_slice_in_dim(own, first_degree(at) * height, reach * height, axis=0)

    sent_most = pick_rows(send_order, features, width, MOST)
    came_most = all_to_all(sent_most)
    sent_last = pick_rows(send_order, after(features, sent_most), width, LAST)
    gate = gate_matrices(pair_index, edge_mask, after(distance, sent_last), radial_weight, rows)
    cotangent, mix_weight, out_weight = lax.optimization_barrier(
        (cotangent, mix_weight, out_weight, gate)
    )[:3]
    cots = [flip_cotangent(cotangent, width, level) for level in range(LMAX + 1)]
    maps = degree_products(mix_weight, out_weight)
    flipped, out_flipped = (
        weight.reshape(LMAX + 1, width, width).swapaxes(1, 2).reshape(weight.shape)
        for weight in (mix_weight, out_weight)
    )
    ready = (gate, maps, flipped, out_flipped, *cots)
    came_last = all_to_all(after(sent_last, came_most, *ready))

    local = after(came_most, *ready)
    own = plane_sum(*outer_sum(place, gate, local, cots, width, MOST, pieces))
    own, other = z_halved(own)
    base, end = span(MOST)
    updated = update(gate, maps, local, width, range(base, end), base, total, None)

    local = after(came_last, own, updated)
    base, end = span(LAST)
    cut = (base + end) // 2
    near, far = outer_sum(place, gate, local, cots, width, LAST, pieces)
    most = z_joined(tree_sum([own, after(other, near)]))
    last = plane_sum(near, far).astype(jnp.bfloat16)
    last = tree_sum([last] + [over_dp(last, 2 * step) for step in range(1, n_dp // 2)])
    updated = update(gate, maps, local, width, range(base, cut), base, total, updated)
    most = plane_gather(most, needed_degrees)
    mix_grad, out_grad = most_gradients(place, out_flipped, flipped, most, shard, piece)
    last = plane_gather(after(last, updated), lambda own, at: own, mix_grad)
    local = after(local, mix_grad)
    updated = update(gate, maps, local, width, range(cut, end), base, total, updated)
    last = [after(part, updated) for part in last]
    mix_grad, out_grad = last_gradients(
        place, out_flipped, flipped, last, mix_grad, out_grad, piece
    )
    return updated, mix_grad, out_grad


def solution(mesh):
    in_specs = (
        P(("dp", "blk"), None),
        P(("dp", "blk"), None),
        P(("dp", "blk"), None),
        P(("dp", "blk"), None),
        P(("dp", "blk"), None, None),
        P(("dp", "blk"), None, None),
        P(),
        P(),
        P(),
    )
    out_specs = (P(("dp", "blk"), None), P("blk", None), P("blk", None))
    run = functools.partial(body, n_dp=mesh.shape["dp"], n_blk=mesh.shape["blk"])
    return jax.shard_map(run, mesh=mesh, in_specs=in_specs, out_specs=out_specs, check_vma=False)
```

```python
import functools
import math

import jax
import jax.numpy as jnp
from jax import lax
from jax.experimental import pallas as pl
from jax.experimental.pallas import tpu as pltpu
from jax.sharding import PartitionSpec as P

LMAX = 4
BLOCK = 128
CUT_RADIUS = 5.0
EDGE_SCALE = 0.25
MOST, LAST = (0, 1, 2, 3), (4,)
ORDER = MOST + LAST
VMEM_LIMIT = 32 * 1024 * 1024
PICK_LIMIT = 60 * 1024 * 1024
GATE_ROWS = 16
WHOLE = pl.BlockSpec(memory_space=pltpu.VMEM)
ANY = pl.BlockSpec(memory_space=pl.ANY)
SCALARS = pl.BlockSpec(memory_space=pltpu.SMEM)


def params(*semantics, limit=VMEM_LIMIT):
    return pltpu.CompilerParams(dimension_semantics=semantics, vmem_limit_bytes=limit)


def after(value, *others):
    return lax.optimization_barrier((value, *others))[0]


def span(degrees):
    return degrees[0] ** 2, (degrees[-1] + 1) ** 2


def comps_of(degrees):
    return [comp for level in degrees for comp in range(*span((level,)))]


def tree_sum(parts):
    parts = [part.astype(jnp.float32) for part in parts]
    while len(parts) > 1:
        parts = [parts[i] + parts[i + 1] for i in range(0, len(parts), 2)]
    return parts[0].astype(jnp.bfloat16)


def chosen_rows(order_ref, rows):
    local = lax.broadcasted_iota(jnp.int32, (rows, rows), 0)
    return (local == order_ref[...]).astype(jnp.float32).T.astype(jnp.bfloat16)


def pick_kernel(
    order_ref, rows_ref, out_ref, list_ref, held_ref, ready_ref, list_sem, in_sems, out_sems, *, first
):
    count, rows, width = ready_ref.shape
    order_load = pltpu.make_async_copy(order_ref, list_ref, list_sem)
    order_load.start()
    slab = rows // in_sems.shape[0]
    loads = [
        pltpu.make_async_copy(
            rows_ref.at[pl.ds(i * slab, slab), pl.ds(first * width, count * width)],
            held_ref.at[pl.ds(i * slab, slab), :],
            in_sems.at[i],
        )
        for i in range(in_sems.shape[0])
    ]
    for load in loads:
        load.start()
    order_load.wait()
    pick = chosen_rows(list_ref, rows)
    for load in loads:
        load.wait()
    stores = []
    for i in range(count):
        ready_ref[i] = jnp.dot(
            pick, held_ref[:, i * width : (i + 1) * width], preferred_element_type=jnp.float32
        ).astype(jnp.bfloat16)
        stores.append(
            pltpu.make_async_copy(
                ready_ref.at[i], out_ref.at[:, pl.ds(i * width, width)], out_sems.at[i]
            )
        )
        stores[-1].start()
    for store in stores:
        store.wait()


def pick_rows(order, features, width, degrees):
    rows = features.shape[0]
    first, last = span(degrees)
    count = last - first
    return pl.pallas_call(
        functools.partial(pick_kernel, first=first),
        in_specs=[ANY, ANY],
        out_specs=ANY,
        out_shape=jax.ShapeDtypeStruct((rows, count * width), jnp.bfloat16),
        scratch_shapes=[
            pltpu.VMEM(order.shape, jnp.int32),
            pltpu.VMEM((rows, count * width), jnp.bfloat16),
            pltpu.VMEM((count, rows, width), jnp.bfloat16),
            pltpu.SemaphoreType.DMA,
            pltpu.SemaphoreType.DMA((8,)),
            pltpu.SemaphoreType.DMA((count,)),
        ],
        compiler_params=params(limit=PICK_LIMIT),
        name="pick_rows",
    )(order, features)


def gate_kernel(pairs_ref, mask_ref, dist_ref, weight_ref, out_ref, radial_ref, *, basis_count):
    pair, step = pl.program_id(0), pl.program_id(1)

    @pl.when((pair == 0) & (step == 0))
    def _():
        out_ref[...] = jnp.zeros_like(out_ref)

    half = math.sqrt(0.5 * math.log2(math.e))
    dist = dist_ref[0]
    scaled = dist * (half * (basis_count - 1) / CUT_RADIUS)
    centers = lax.broadcasted_iota(jnp.int32, (basis_count, BLOCK), 0).astype(jnp.float32) * half
    weights = weight_ref[...]
    levels = LMAX + 1
    for row in range(GATE_ROWS):
        offset = scaled[row : row + 1, :] - centers
        phi = jnp.exp2(-(offset * offset))
        high = phi.astype(jnp.bfloat16)
        low = (phi - high.astype(jnp.float32)).astype(jnp.bfloat16)
        radial = jnp.dot(weights, high, preferred_element_type=jnp.float32)
        radial = radial + jnp.dot(weights, low, preferred_element_type=jnp.float32)
        radial = radial[0:8] + radial[8:16]
        for level in range(levels):
            radial_ref[level, row : row + 1, :] = radial[level : level + 1, :]
    envelope = (
        (0.5 * EDGE_SCALE)
        * (jnp.cos((math.pi / CUT_RADIUS) * dist) + 1.0)
        * mask_ref[0].astype(jnp.float32)
    )
    dest = pl.multiple_of(pairs_ref[pair, 0] * BLOCK + step * GATE_ROWS, GATE_ROWS)
    src = pl.multiple_of(pairs_ref[pair, 1] * BLOCK, BLOCK)
    for level in range(levels):
        out_ref[level, pl.ds(dest, GATE_ROWS), pl.ds(src, BLOCK)] = (
            radial_ref[level] * envelope
        ).astype(jnp.bfloat16)


def gate_matrices(pairs, mask, dist, radial_weight, rows):
    count = pairs.shape[0]
    levels = radial_weight.shape[1]
    transposed = radial_weight.T
    high = transposed.astype(jnp.bfloat16)
    low = (transposed - high.astype(jnp.float32)).astype(jnp.bfloat16)
    pad = ((0, 8 - levels), (0, 0))
    weights = jnp.concatenate([jnp.pad(high, pad), jnp.pad(low, pad)], axis=0)
    kernel = functools.partial(gate_kernel, basis_count=radial_weight.shape[0])
    edges = pl.BlockSpec((1, GATE_ROWS, BLOCK), lambda p, s, pairs: (p, s, 0))
    return pl.pallas_call(
        kernel,
        grid_spec=pltpu.PrefetchScalarGridSpec(
            num_scalar_prefetch=1,
            grid=(count, BLOCK // GATE_ROWS),
            in_specs=[edges, edges, pl.BlockSpec(weights.shape, lambda p, s, pairs: (0, 0))],
            out_specs=pl.BlockSpec((levels, rows, rows), lambda p, s, pairs: (0, 0, 0)),
            scratch_shapes=[pltpu.VMEM((levels, GATE_ROWS, BLOCK), jnp.float32)],
        ),
        out_shape=jax.ShapeDtypeStruct((levels, rows, rows), jnp.bfloat16),
        compiler_params=params("arbitrary", "arbitrary"),
        cost_estimate=pl.CostEstimate(
            flops=2 * 3 * 512 * count * BLOCK * BLOCK * radial_weight.shape[0],
            bytes_accessed=2 * 4 * count * BLOCK * BLOCK,
            transcendentals=count * BLOCK * BLOCK * radial_weight.shape[0],
        ),
        name="gate",
    )(pairs, mask, dist, weights)


def product_kernel(left_ref, right_ref, out_ref):
    out_ref[...] = jnp.dot(
        left_ref[...], right_ref[...], preferred_element_type=jnp.float32
    ).astype(jnp.bfloat16)


def degree_products(left, right):
    width = left.shape[1]
    block = pl.BlockSpec((width, width), lambda i: (i, 0))
    return pl.pallas_call(
        product_kernel,
        grid=(left.shape[0] // width,),
        in_specs=[block, block],
        out_specs=block,
        out_shape=jax.ShapeDtypeStruct(left.shape, jnp.bfloat16),
        compiler_params=params("arbitrary"),
        name="degree_products",
    )(left, right)


def flip_kernel(rows_ref, out_ref):
    out_ref[...] = rows_ref[...].T


def flip_cotangent(cotangent, width, level):
    rows = cotangent.shape[0]
    first, last = span((level,))
    return pl.pallas_call(
        flip_kernel,
        grid=(last - first,),
        in_specs=[pl.BlockSpec((rows, width), lambda i: (0, first + i))],
        out_specs=pl.BlockSpec((width, rows), lambda i: (0, i)),
        out_shape=jax.ShapeDtypeStruct((width, (last - first) * rows), jnp.bfloat16),
        compiler_params=params("arbitrary"),
        name="flip_cotangent",
    )(cotangent)


def outer_kernel(place_ref, gate_ref, local_ref, *refs, pieces, levels):
    cots = refs[: len(levels)]
    near_ref, far_ref, mixed_ref, sum_ref = refs[len(levels) :]
    rows, width = local_ref.shape[0], mixed_ref.shape[1]
    comps = comps_of(levels)
    for slot, level in enumerate(levels):
        first, last = span((level,))
        for comp in range(first, last):
            at = comps.index(comp) * width
            mixed_ref[(comp - first) * rows : (comp - first + 1) * rows, :] = jnp.dot(
                gate_ref[level], local_ref[:, at : at + width], preferred_element_type=jnp.float32
            ).astype(jnp.bfloat16)
        depth = (last - first) * rows
        flipped = jnp.dot(
            cots[slot][...], mixed_ref[0:depth, :], preferred_element_type=jnp.float32
        )
        sum_ref[slot * width : (slot + 1) * width, :] = flipped.T
    half, height = pieces // 2, width // pieces
    for step in range(half):
        near = pl.multiple_of((place_ref[0] ^ step) * height, height)
        far = pl.multiple_of((place_ref[0] ^ (step + half)) * height, height)
        for slot in range(len(levels)):
            to = (step * len(levels) + slot) * height
            near_ref[to : to + height, :] = sum_ref[pl.ds(slot * width + near, height), :]
            far_ref[to : to + height, :] = sum_ref[pl.ds(slot * width + far, height), :].astype(
                jnp.bfloat16
            )


def outer_sum(place, gate, local, cots, width, levels, pieces, keep=False):
    rows = gate.shape[1]
    whole = len(levels) * width
    deepest = 2 * max(levels) + 1
    total = sum(2 * level + 1 for level in levels)
    mixed = (deepest * rows, width)
    out_shape = [
        jax.ShapeDtypeStruct((whole // 2, width), jnp.float32),
        jax.ShapeDtypeStruct((whole // 2, width), jnp.bfloat16),
    ]
    scratch_shapes = [pltpu.VMEM((whole, width), jnp.float32)]
    if keep:
        out_shape.append(jax.ShapeDtypeStruct(mixed, jnp.bfloat16))
    else:
        scratch_shapes.insert(0, pltpu.VMEM(mixed, jnp.bfloat16))
    return pl.pallas_call(
        functools.partial(outer_kernel, pieces=pieces, levels=levels),
        in_specs=[SCALARS] + [WHOLE] * (2 + len(levels)),
        out_specs=[WHOLE] * len(out_shape),
        out_shape=out_shape,
        scratch_shapes=scratch_shapes,
        compiler_params=params(),
        cost_estimate=pl.CostEstimate(
            flops=2 * total * rows * width * (rows + width),
            bytes_accessed=4 * total * rows * width,
            transcendentals=0,
        ),
        name="outer_sum",
    )(place, gate, local, *[cots[level] for level in levels])


def update_kernel(gate_ref, map_ref, local_ref, *refs, degrees, mixed_given):
    out_ref, ready_ref, sems = refs[-3:]
    width = map_ref.shape[1]
    copies = []
    for index, comp in enumerate(comps_of(degrees)):
        level = math.isqrt(comp)
        at = index * width
        hidden = local_ref[:, at : at + width]
        if mixed_given:
            rows = hidden.shape[0]
            mixed = gate_ref[index * rows : (index + 1) * rows, :]
            weight = map_ref[...]
        else:
            mixed = jnp.dot(gate_ref[level], hidden, preferred_element_type=jnp.float32)
            mixed = mixed.astype(jnp.bfloat16)
            weight = map_ref[level * width : (level + 1) * width, :]
        added = jnp.dot(mixed, weight, preferred_element_type=jnp.float32)
        ready_ref[index] = (hidden.astype(jnp.float32) + added).astype(jnp.bfloat16)
        copies.append(
            pltpu.make_async_copy(
                ready_ref.at[index],
                out_ref.at[:, pl.ds(comp * width, width)],
                sems.at[index],
            )
        )
        copies[-1].start()
    for copy in copies:
        copy.wait()


def update(gate, maps, local, width, degrees, total, held):
    rows = local.shape[0]
    count = len(comps_of(degrees))
    in_specs = [WHOLE] * 3
    operands = [gate, maps, local]
    aliases = {}
    if held is not None:
        in_specs.append(ANY)
        operands.append(held)
        aliases = {3: 0}
    return pl.pallas_call(
        functools.partial(update_kernel, degrees=degrees, mixed_given=gate.ndim == 2),
        in_specs=in_specs,
        out_specs=ANY,
        out_shape=jax.ShapeDtypeStruct((rows, total), jnp.bfloat16),
        scratch_shapes=[
            pltpu.VMEM((count, rows, width), jnp.bfloat16),
            pltpu.SemaphoreType.DMA((count,)),
        ],
        input_output_aliases=aliases,
        compiler_params=params(),
        cost_estimate=pl.CostEstimate(
            flops=2 * count * rows * width * (rows + width),
            bytes_accessed=4 * count * rows * width,
            transcendentals=0,
        ),
        name="update",
    )(*operands)


def place_parts(place_ref, parts, outer_ref):
    width = outer_ref.shape[1]
    height = width // len(parts)
    for step, part in enumerate(parts):
        row = pl.multiple_of((place_ref[0] ^ step) * height, height)
        for slot in range(part.shape[0] // height):
            outer_ref[pl.ds(slot * width + row, height), :] = part[
                slot * height : (slot + 1) * height, :
            ]


def gradients(rows, outer, flipped, weight):
    mix = jnp.dot(rows, weight, preferred_element_type=jnp.float32)
    return mix, jnp.dot(flipped, outer, preferred_element_type=jnp.float32)


def most_kernel(place_ref, weight_ref, flip_ref, *refs, piece):
    *parts, mix_ref, out_ref, outer_ref = refs
    width = weight_ref.shape[0]

    @pl.when(pl.program_id(0) == 0)
    def _():
        place_parts(place_ref, parts, outer_ref)

    row = (place_ref[1] + pl.program_id(0)) * piece

    @pl.when(row < len(MOST) * width)
    def _():
        first = pl.multiple_of((row // width - place_ref[2]) * width, width)
        mix_ref[...], out_ref[...] = gradients(
            outer_ref[pl.ds(pl.multiple_of(first + row % width, piece), piece), :],
            outer_ref[pl.ds(first, width), :],
            flip_ref[...],
            weight_ref[...],
        )


def most_gradients(place, weight, flipped, parts, shard, piece):
    width = weight.shape[1]
    whole = pl.BlockSpec(parts[0].shape, lambda i, place: (0, 0))
    return pl.pallas_call(
        functools.partial(most_kernel, piece=piece),
        grid_spec=pltpu.PrefetchScalarGridSpec(
            num_scalar_prefetch=1,
            grid=(shard // piece,),
            in_specs=[
                pl.BlockSpec(
                    (width, width), lambda i, place: ((place[1] + i) * piece // width, 0)
                ),
                pl.BlockSpec((piece, width), lambda i, place: (place[1] + i, 0)),
            ]
            + [whole] * len(parts),
            out_specs=[pl.BlockSpec((piece, width), lambda i, place: (i, 0))] * 2,
            scratch_shapes=[pltpu.VMEM((len(parts) * parts[0].shape[0], width), jnp.bfloat16)],
        ),
        out_shape=[jax.ShapeDtypeStruct((shard, width), jnp.float32)] * 2,
        compiler_params=params("arbitrary"),
        name="most_gradients",
    )(place, weight, flipped, *parts)


def last_kernel(place_ref, weight_ref, flip_ref, *refs, piece):
    *parts, _, _, mix_out, out_out, outer_ref, mix_ref, out_ref, sems = refs
    width = weight_ref.shape[0]
    place_parts(place_ref, parts, outer_ref)
    count = mix_ref.shape[0]

    def each(index):
        row = (place_ref[1] + index) * piece - LAST[0] * width
        to = pl.ds(index * piece, piece)
        copies = [
            pltpu.make_async_copy(mix_ref.at[index], mix_out.at[to, :], sems.at[index, 0]),
            pltpu.make_async_copy(out_ref.at[index], out_out.at[to, :], sems.at[index, 1]),
        ]
        return row, (row >= 0) & (row < width), copies

    for index in range(count):
        row, held, copies = each(index)

        @pl.when(held)
        def _():
            mine = pl.ds(pl.multiple_of(row, piece), piece)
            mix_ref[index], out_ref[index] = gradients(
                outer_ref[mine, :], outer_ref[...], flip_ref[mine, :], weight_ref[...]
            )
            for copy in copies:
                copy.start()

    for index in range(count):
        _, held, copies = each(index)

        @pl.when(held)
        def _():
            for copy in copies:
                copy.wait()


def last_gradients(place, weight, flipped, parts, mix_grad, out_grad, piece):
    shard, width = mix_grad.shape
    own = pl.BlockSpec((width, width), lambda i: (LAST[0], 0))
    whole = pl.BlockSpec(parts[0].shape, lambda i: (0, 0))
    count = shard // piece
    return pl.pallas_call(
        functools.partial(last_kernel, piece=piece),
        grid=(1,),
        in_specs=[SCALARS, own, own] + [whole] * len(parts) + [ANY] * 2,
        out_specs=[ANY] * 2,
        out_shape=[jax.ShapeDtypeStruct(mix_grad.shape, jnp.float32)] * 2,
        scratch_shapes=[
            pltpu.VMEM((width, width), jnp.bfloat16),
            pltpu.VMEM((count, piece, width), jnp.float32),
            pltpu.VMEM((count, piece, width), jnp.float32),
            pltpu.SemaphoreType.DMA((count, 2)),
        ],
        input_output_aliases={3 + len(parts): 0, 4 + len(parts): 1},
        compiler_params=params("arbitrary"),
        name="last_gradients",
    )(place, weight, flipped, *parts, mix_grad, out_grad)


def body(
    features,
    cotangent,
    send_order,
    pair_index,
    edge_mask,
    distance,
    radial_weight,
    mix_weight,
    out_weight,
    *,
    n_dp,
    n_blk,
):
    rows, total = features.shape
    width = mix_weight.shape[1]
    pieces = 2 * n_blk
    shard = mix_weight.shape[0] // n_blk
    piece = math.gcd(shard, width)
    at_dp, at_blk = lax.axis_index("dp"), lax.axis_index("blk")
    reach = max(((i + 1) * shard - 1) // width - i * shard // width + 1 for i in range(n_blk))
    reach = min(reach, len(MOST))

    def first_degree(at):
        return jnp.minimum(at * shard // width, len(MOST) - reach)

    place = jnp.stack(
        [at_dp % 2 * n_blk + at_blk, at_blk * (shard // piece), first_degree(at_blk)]
    ).astype(jnp.int32)

    def over_dp(value, step):
        return lax.ppermute(value, "dp", [(i, i ^ step) for i in range(n_dp)])

    def over_blk(value, step):
        return lax.ppermute(value, "blk", [(i, i ^ step) for i in range(n_blk)])

    def all_to_all(value):
        return lax.all_to_all(value, "dp", split_axis=0, concat_axis=0, tiled=True)

    def chip_sum(near, far):
        return near + over_dp(far, 1).astype(jnp.float32)

    def plane_sum(chip):
        height = chip.shape[0] // n_blk
        own = chip[:height]
        for step in range(1, n_blk):
            part = chip[step * height : (step + 1) * height].astype(jnp.bfloat16)
            own = own + over_blk(part, step).astype(jnp.float32)
        return own

    bits = [1 << i for i in range((n_dp // 2).bit_length() - 1)]
    upper = [(at_dp // 2) & bit for bit in bits]

    def z_halved(own):
        for bit, high in zip(bits[:-1], upper):
            half = own.shape[0] // 2
            kept = jnp.where(high > 0, own[half:], own[:half])
            given = jnp.where(high > 0, own[:half], own[half:]).astype(jnp.bfloat16)
            own = kept + over_dp(given, 2 * bit).astype(jnp.float32)
        own = own.astype(jnp.bfloat16)
        return own, over_dp(own, 2 * bits[-1])

    def z_joined(own, *others):
        for bit, high in reversed(list(zip(bits[:-1], upper))):
            other = after(over_dp(own, 2 * bit), *others)
            own = jnp.where(
                high > 0,
                jnp.concatenate([other, own], axis=0),
                jnp.concatenate([own, other], axis=0),
            )
        return own

    def plane_gather(own, needed, *others):
        near = [needed(own, at_blk)]
        near += [over_blk(needed(own, at_blk ^ step), step) for step in range(1, n_blk)]
        return near + [over_dp(after(part, *others), 1) for part in near]

    def needed_degrees(own, at):
        height = width // pieces
        return lax.dynamic_slice_in_dim(own, first_degree(at) * height, reach * height, axis=0)

    sent_most = pick_rows(send_order, features, width, MOST)
    came_most = all_to_all(sent_most)
    sent_last = pick_rows(send_order, after(features, sent_most), width, LAST)
    gate = gate_matrices(pair_index, edge_mask, after(distance, sent_last), radial_weight, rows)
    cotangent, mix_weight, out_weight = lax.optimization_barrier(
        (cotangent, mix_weight, out_weight, gate)
    )[:3]
    cots = {level: flip_cotangent(cotangent, width, level) for level in MOST}
    maps = degree_products(mix_weight, out_weight)
    flipped, out_flipped = (
        weight.reshape(LMAX + 1, width, width).swapaxes(1, 2).reshape(weight.shape)
        for weight in (mix_weight, out_weight)
    )
    last_map = maps[LAST[0] * width : (LAST[0] + 1) * width]
    ready = (gate, maps, last_map, flipped, out_flipped, *cots.values())
    came_last = all_to_all(after(sent_last, came_most, *ready))

    local = after(came_most, *ready)
    own = plane_sum(chip_sum(*outer_sum(place, gate, local, cots, width, MOST, pieces)))
    source = after(cotangent, own)
    cots = {level: flip_cotangent(source, width, level) for level in LAST}
    own, other = z_halved(own)
    updated = update(gate, maps, after(local, own), width, MOST, total, None)
    most = z_joined(tree_sum([own, after(other, updated)]))

    local = after(came_last, updated, most)
    near, far, mixed = outer_sum(place, gate, local, cots, width, LAST, pieces, keep=True)
    chip, most = lax.optimization_barrier((chip_sum(near, far), most))
    last = plane_sum(chip).astype(jnp.bfloat16)
    most = plane_gather(most, needed_degrees)
    last = tree_sum([last] + [over_dp(last, 2 * step) for step in range(1, n_dp // 2)])
    updated = update(mixed, last_map, local, width, LAST, total, updated)
    mix_grad, out_grad = most_gradients(place, out_flipped, flipped, most, shard, piece)
    last = plane_gather(after(last, updated), lambda own, at: own, mix_grad)
    mix_grad, out_grad = last_gradients(
        place, out_flipped, flipped, last, mix_grad, out_grad, piece
    )
    return updated, mix_grad, out_grad


def solution(mesh):
    in_specs = (
        P(("dp", "blk"), None),
        P(("dp", "blk"), None),
        P(("dp", "blk"), None),
        P(("dp", "blk"), None),
        P(("dp", "blk"), None, None),
        P(("dp", "blk"), None, None),
        P(),
        P(),
        P(),
    )
    out_specs = (P(("dp", "blk"), None), P("blk", None), P("blk", None))
    run = functools.partial(body, n_dp=mesh.shape["dp"], n_blk=mesh.shape["blk"])
    return jax.shard_map(run, mesh=mesh, in_specs=in_specs, out_specs=out_specs, check_vma=False)
```

```python
import functools
import math

import jax
import jax.numpy as jnp
from jax import lax
from jax.experimental import pallas as pl
from jax.experimental.pallas import tpu as pltpu
from jax.sharding import PartitionSpec as P

LMAX = 4
BLOCK = 128
CUT_RADIUS = 5.0
EDGE_SCALE = 0.25
MOST, LAST = (0, 1, 2, 3), (4,)
ORDER = MOST + LAST
VMEM_LIMIT = 48 * 1024 * 1024
PICK_LIMIT = 60 * 1024 * 1024
GATE_ROWS = 16
WHOLE = pl.BlockSpec(memory_space=pltpu.VMEM)
ANY = pl.BlockSpec(memory_space=pl.ANY)
SCALARS = pl.BlockSpec(memory_space=pltpu.SMEM)


def params(*semantics, limit=VMEM_LIMIT):
    return pltpu.CompilerParams(dimension_semantics=semantics, vmem_limit_bytes=limit)


def after(value, *others):
    return lax.optimization_barrier((value, *others))[0]


def span(degrees):
    return degrees[0] ** 2, (degrees[-1] + 1) ** 2


def comps_of(degrees):
    return [comp for level in degrees for comp in range(*span((level,)))]


def tree_sum(parts):
    parts = [part.astype(jnp.float32) for part in parts]
    while len(parts) > 1:
        parts = [parts[i] + parts[i + 1] for i in range(0, len(parts), 2)]
    return parts[0].astype(jnp.bfloat16)


def chosen_rows(order_ref, rows):
    local = lax.broadcasted_iota(jnp.int32, (rows, rows), 0)
    return (local == order_ref[...]).astype(jnp.float32).T.astype(jnp.bfloat16)


def pick_kernel(
    order_ref, rows_ref, out_ref, list_ref, held_ref, ready_ref, list_sem, in_sems, out_sems, *, first
):
    count, rows, width = ready_ref.shape
    order_load = pltpu.make_async_copy(order_ref, list_ref, list_sem)
    order_load.start()
    slab = rows // in_sems.shape[0]
    loads = [
        pltpu.make_async_copy(
            rows_ref.at[pl.ds(i * slab, slab), pl.ds(first * width, count * width)],
            held_ref.at[pl.ds(i * slab, slab), :],
            in_sems.at[i],
        )
        for i in range(in_sems.shape[0])
    ]
    for load in loads:
        load.start()
    order_load.wait()
    pick = chosen_rows(list_ref, rows)
    for load in loads:
        load.wait()
    stores = []
    for i in range(count):
        ready_ref[i] = jnp.dot(
            pick, held_ref[:, i * width : (i + 1) * width], preferred_element_type=jnp.float32
        ).astype(jnp.bfloat16)
        stores.append(
            pltpu.make_async_copy(
                ready_ref.at[i], out_ref.at[:, pl.ds(i * width, width)], out_sems.at[i]
            )
        )
        stores[-1].start()
    for store in stores:
        store.wait()


def pick_rows(order, features, width, degrees):
    rows = features.shape[0]
    first, last = span(degrees)
    count = last - first
    return pl.pallas_call(
        functools.partial(pick_kernel, first=first),
        in_specs=[ANY, ANY],
        out_specs=ANY,
        out_shape=jax.ShapeDtypeStruct((rows, count * width), jnp.bfloat16),
        scratch_shapes=[
            pltpu.VMEM(order.shape, jnp.int32),
            pltpu.VMEM((rows, count * width), jnp.bfloat16),
            pltpu.VMEM((count, rows, width), jnp.bfloat16),
            pltpu.SemaphoreType.DMA,
            pltpu.SemaphoreType.DMA((8,)),
            pltpu.SemaphoreType.DMA((count,)),
        ],
        compiler_params=params(limit=PICK_LIMIT),
        name="pick_rows",
    )(order, features)


def gate_kernel(pairs_ref, mask_ref, dist_ref, weight_ref, out_ref, radial_ref, *, basis_count):
    pair, step = pl.program_id(0), pl.program_id(1)

    @pl.when((pair == 0) & (step == 0))
    def _():
        out_ref[...] = jnp.zeros_like(out_ref)

    half = math.sqrt(0.5 * math.log2(math.e))
    dist = dist_ref[0]
    scaled = dist * (half * (basis_count - 1) / CUT_RADIUS)
    centers = lax.broadcasted_iota(jnp.int32, (basis_count, BLOCK), 0).astype(jnp.float32) * half
    weights = weight_ref[...]
    levels = LMAX + 1
    for row in range(GATE_ROWS):
        offset = scaled[row : row + 1, :] - centers
        phi = jnp.exp2(-(offset * offset))
        high = phi.astype(jnp.bfloat16)
        low = (phi - high.astype(jnp.float32)).astype(jnp.bfloat16)
        radial = jnp.dot(weights, high, preferred_element_type=jnp.float32)
        radial = radial + jnp.dot(weights, low, preferred_element_type=jnp.float32)
        radial = radial[0:8] + radial[8:16]
        for level in range(levels):
            radial_ref[level, row : row + 1, :] = radial[level : level + 1, :]
    envelope = (
        (0.5 * EDGE_SCALE)
        * (jnp.cos((math.pi / CUT_RADIUS) * dist) + 1.0)
        * mask_ref[0].astype(jnp.float32)
    )
    dest = pl.multiple_of(pairs_ref[pair, 0] * BLOCK + step * GATE_ROWS, GATE_ROWS)
    src = pl.multiple_of(pairs_ref[pair, 1] * BLOCK, BLOCK)
    for level in range(levels):
        out_ref[level, pl.ds(dest, GATE_ROWS), pl.ds(src, BLOCK)] = (
            radial_ref[level] * envelope
        ).astype(jnp.bfloat16)


def gate_matrices(pairs, mask, dist, radial_weight, rows):
    count = pairs.shape[0]
    levels = radial_weight.shape[1]
    transposed = radial_weight.T
    high = transposed.astype(jnp.bfloat16)
    low = (transposed - high.astype(jnp.float32)).astype(jnp.bfloat16)
    pad = ((0, 8 - levels), (0, 0))
    weights = jnp.concatenate([jnp.pad(high, pad), jnp.pad(low, pad)], axis=0)
    kernel = functools.partial(gate_kernel, basis_count=radial_weight.shape[0])
    edges = pl.BlockSpec((1, GATE_ROWS, BLOCK), lambda p, s, pairs: (p, s, 0))
    return pl.pallas_call(
        kernel,
        grid_spec=pltpu.PrefetchScalarGridSpec(
            num_scalar_prefetch=1,
            grid=(count, BLOCK // GATE_ROWS),
            in_specs=[edges, edges, pl.BlockSpec(weights.shape, lambda p, s, pairs: (0, 0))],
            out_specs=pl.BlockSpec((levels, rows, rows), lambda p, s, pairs: (0, 0, 0)),
            scratch_shapes=[pltpu.VMEM((levels, GATE_ROWS, BLOCK), jnp.float32)],
        ),
        out_shape=jax.ShapeDtypeStruct((levels, rows, rows), jnp.bfloat16),
        compiler_params=params("arbitrary", "arbitrary"),
        cost_estimate=pl.CostEstimate(
            flops=2 * 3 * 512 * count * BLOCK * BLOCK * radial_weight.shape[0],
            bytes_accessed=2 * 4 * count * BLOCK * BLOCK,
            transcendentals=count * BLOCK * BLOCK * radial_weight.shape[0],
        ),
        name="gate",
    )(pairs, mask, dist, weights)


def product_kernel(left_ref, right_ref, out_ref):
    out_ref[...] = jnp.dot(
        left_ref[...], right_ref[...], preferred_element_type=jnp.float32
    ).astype(jnp.bfloat16)


def degree_products(left, right):
    width = left.shape[1]
    block = pl.BlockSpec((width, width), lambda i: (i, 0))
    return pl.pallas_call(
        product_kernel,
        grid=(left.shape[0] // width,),
        in_specs=[block, block],
        out_specs=block,
        out_shape=jax.ShapeDtypeStruct(left.shape, jnp.bfloat16),
        compiler_params=params("arbitrary"),
        name="degree_products",
    )(left, right)


def flip_kernel(rows_ref, out_ref):
    out_ref[...] = rows_ref[...].T


def flip_cotangent(cotangent, width, level):
    rows = cotangent.shape[0]
    first, last = span((level,))
    return pl.pallas_call(
        flip_kernel,
        grid=(last - first,),
        in_specs=[pl.BlockSpec((rows, width), lambda i: (0, first + i))],
        out_specs=pl.BlockSpec((width, rows), lambda i: (0, i)),
        out_shape=jax.ShapeDtypeStruct((width, (last - first) * rows), jnp.bfloat16),
        compiler_params=params("arbitrary"),
        name="flip_cotangent",
    )(cotangent)


def outer_kernel(place_ref, gate_ref, local_ref, *refs, pieces, levels):
    cots = refs[: len(levels)]
    near_ref, far_ref, mixed_ref, sum_ref = refs[len(levels) :]
    rows, width = local_ref.shape[0], mixed_ref.shape[1]
    comps = comps_of(levels)
    for slot, level in enumerate(levels):
        first, last = span((level,))
        for comp in range(first, last):
            at = comps.index(comp) * width
            mixed_ref[(comp - first) * rows : (comp - first + 1) * rows, :] = jnp.dot(
                gate_ref[level], local_ref[:, at : at + width], preferred_element_type=jnp.float32
            ).astype(jnp.bfloat16)
        depth = (last - first) * rows
        flipped = jnp.dot(
            cots[slot][...], mixed_ref[0:depth, :], preferred_element_type=jnp.float32
        )
        sum_ref[slot * width : (slot + 1) * width, :] = flipped.T
    half, height = pieces // 2, width // pieces
    for step in range(half):
        near = pl.multiple_of((place_ref[0] ^ step) * height, height)
        far = pl.multiple_of((place_ref[0] ^ (step + half)) * height, height)
        for slot in range(len(levels)):
            to = (step * len(levels) + slot) * height
            near_ref[to : to + height, :] = sum_ref[pl.ds(slot * width + near, height), :]
            far_ref[to : to + height, :] = sum_ref[pl.ds(slot * width + far, height), :].astype(
                jnp.bfloat16
            )


def outer_sum(place, gate, local, cots, width, levels, pieces, keep=False):
    rows = gate.shape[1]
    whole = len(levels) * width
    deepest = 2 * max(levels) + 1
    total = sum(2 * level + 1 for level in levels)
    mixed = (deepest * rows, width)
    out_shape = [
        jax.ShapeDtypeStruct((whole // 2, width), jnp.float32),
        jax.ShapeDtypeStruct((whole // 2, width), jnp.bfloat16),
    ]
    scratch_shapes = [pltpu.VMEM((whole, width), jnp.float32)]
    if keep:
        out_shape.append(jax.ShapeDtypeStruct(mixed, jnp.bfloat16))
    else:
        scratch_shapes.insert(0, pltpu.VMEM(mixed, jnp.bfloat16))
    return pl.pallas_call(
        functools.partial(outer_kernel, pieces=pieces, levels=levels),
        in_specs=[SCALARS] + [WHOLE] * (2 + len(levels)),
        out_specs=[WHOLE] * len(out_shape),
        out_shape=out_shape,
        scratch_shapes=scratch_shapes,
        compiler_params=params(),
        cost_estimate=pl.CostEstimate(
            flops=2 * total * rows * width * (rows + width),
            bytes_accessed=4 * total * rows * width,
            transcendentals=0,
        ),
        name="outer_sum",
    )(place, gate, local, *[cots[level] for level in levels])


def update_kernel(gate_ref, map_ref, local_ref, *refs, degrees, mixed_given):
    out_ref, ready_ref, sems = refs[-3:]
    width = map_ref.shape[1]
    copies = []
    for index, comp in enumerate(comps_of(degrees)):
        level = math.isqrt(comp)
        at = index * width
        hidden = local_ref[:, at : at + width]
        if mixed_given:
            rows = hidden.shape[0]
            mixed = gate_ref[index * rows : (index + 1) * rows, :]
            weight = map_ref[...]
        else:
            mixed = jnp.dot(gate_ref[level], hidden, preferred_element_type=jnp.float32)
            mixed = mixed.astype(jnp.bfloat16)
            weight = map_ref[level * width : (level + 1) * width, :]
        added = jnp.dot(mixed, weight, preferred_element_type=jnp.float32)
        ready_ref[index] = (hidden.astype(jnp.float32) + added).astype(jnp.bfloat16)
        copies.append(
            pltpu.make_async_copy(
                ready_ref.at[index],
                out_ref.at[:, pl.ds(comp * width, width)],
                sems.at[index],
            )
        )
        copies[-1].start()
    for copy in copies:
        copy.wait()


def update(gate, maps, local, width, degrees, total, held):
    rows = local.shape[0]
    count = len(comps_of(degrees))
    in_specs = [WHOLE] * 3
    operands = [gate, maps, local]
    aliases = {}
    if held is not None:
        in_specs.append(ANY)
        operands.append(held)
        aliases = {3: 0}
    return pl.pallas_call(
        functools.partial(update_kernel, degrees=degrees, mixed_given=gate.ndim == 2),
        in_specs=in_specs,
        out_specs=ANY,
        out_shape=jax.ShapeDtypeStruct((rows, total), jnp.bfloat16),
        scratch_shapes=[
            pltpu.VMEM((count, rows, width), jnp.bfloat16),
            pltpu.SemaphoreType.DMA((count,)),
        ],
        input_output_aliases=aliases,
        compiler_params=params(),
        cost_estimate=pl.CostEstimate(
            flops=2 * count * rows * width * (rows + width),
            bytes_accessed=4 * count * rows * width,
            transcendentals=0,
        ),
        name="update",
    )(*operands)


def place_parts(place_ref, parts, outer_ref):
    width = outer_ref.shape[1]
    height = width // len(parts)
    for step, part in enumerate(parts):
        row = pl.multiple_of((place_ref[0] ^ step) * height, height)
        for slot in range(part.shape[0] // height):
            outer_ref[pl.ds(slot * width + row, height), :] = part[
                slot * height : (slot + 1) * height, :
            ]


def gradients(rows, outer, flipped, weight):
    mix = jnp.dot(rows, weight, preferred_element_type=jnp.float32)
    return mix, jnp.dot(flipped, outer, preferred_element_type=jnp.float32)


def most_kernel(place_ref, weight_ref, flip_ref, *refs, piece):
    *parts, mix_ref, out_ref, outer_ref = refs
    width = weight_ref.shape[0]

    @pl.when(pl.program_id(0) == 0)
    def _():
        place_parts(place_ref, parts, outer_ref)

    row = (place_ref[1] + pl.program_id(0)) * piece

    @pl.when(row < len(MOST) * width)
    def _():
        first = pl.multiple_of((row // width - place_ref[2]) * width, width)
        mix_ref[...], out_ref[...] = gradients(
            outer_ref[pl.ds(pl.multiple_of(first + row % width, piece), piece), :],
            outer_ref[pl.ds(first, width), :],
            flip_ref[...],
            weight_ref[...],
        )


def most_gradients(place, weight, flipped, parts, shard, piece):
    width = weight.shape[1]
    whole = pl.BlockSpec(parts[0].shape, lambda i, place: (0, 0))
    return pl.pallas_call(
        functools.partial(most_kernel, piece=piece),
        grid_spec=pltpu.PrefetchScalarGridSpec(
            num_scalar_prefetch=1,
            grid=(shard // piece,),
            in_specs=[
                pl.BlockSpec(
                    (width, width), lambda i, place: ((place[1] + i) * piece // width, 0)
                ),
                pl.BlockSpec((piece, width), lambda i, place: (place[1] + i, 0)),
            ]
            + [whole] * len(parts),
            out_specs=[pl.BlockSpec((piece, width), lambda i, place: (i, 0))] * 2,
            scratch_shapes=[pltpu.VMEM((len(parts) * parts[0].shape[0], width), jnp.bfloat16)],
        ),
        out_shape=[jax.ShapeDtypeStruct((shard, width), jnp.float32)] * 2,
        compiler_params=params("arbitrary"),
        name="most_gradients",
    )(place, weight, flipped, *parts)


def last_kernel(place_ref, weight_ref, flip_ref, *refs, piece):
    *parts, _, _, mix_out, out_out, outer_ref, mix_ref, out_ref, sems = refs
    width = weight_ref.shape[0]
    place_parts(place_ref, parts, outer_ref)
    count = mix_ref.shape[0]

    def each(index):
        row = (place_ref[1] + index) * piece - LAST[0] * width
        to = pl.ds(index * piece, piece)
        copies = [
            pltpu.make_async_copy(mix_ref.at[index], mix_out.at[to, :], sems.at[index, 0]),
            pltpu.make_async_copy(out_ref.at[index], out_out.at[to, :], sems.at[index, 1]),
        ]
        return row, (row >= 0) & (row < width), copies

    for index in range(count):
        row, held, copies = each(index)

        @pl.when(held)
        def _():
            mine = pl.ds(pl.multiple_of(row, piece), piece)
            mix_ref[index], out_ref[index] = gradients(
                outer_ref[mine, :], outer_ref[...], flip_ref[mine, :], weight_ref[...]
            )
            for copy in copies:
                copy.start()

    for index in range(count):
        _, held, copies = each(index)

        @pl.when(held)
        def _():
            for copy in copies:
                copy.wait()


def last_gradients(place, weight, flipped, parts, mix_grad, out_grad, piece):
    shard, width = mix_grad.shape
    own = pl.BlockSpec((width, width), lambda i: (LAST[0], 0))
    whole = pl.BlockSpec(parts[0].shape, lambda i: (0, 0))
    count = shard // piece
    return pl.pallas_call(
        functools.partial(last_kernel, piece=piece),
        grid=(1,),
        in_specs=[SCALARS, own, own] + [whole] * len(parts) + [ANY] * 2,
        out_specs=[ANY] * 2,
        out_shape=[jax.ShapeDtypeStruct(mix_grad.shape, jnp.float32)] * 2,
        scratch_shapes=[
            pltpu.VMEM((width, width), jnp.bfloat16),
            pltpu.VMEM((count, piece, width), jnp.float32),
            pltpu.VMEM((count, piece, width), jnp.float32),
            pltpu.SemaphoreType.DMA((count, 2)),
        ],
        input_output_aliases={3 + len(parts): 0, 4 + len(parts): 1},
        compiler_params=params("arbitrary"),
        name="last_gradients",
    )(place, weight, flipped, *parts, mix_grad, out_grad)


def body(
    features,
    cotangent,
    send_order,
    pair_index,
    edge_mask,
    distance,
    radial_weight,
    mix_weight,
    out_weight,
    *,
    n_dp,
    n_blk,
):
    rows, total = features.shape
    width = mix_weight.shape[1]
    pieces = 2 * n_blk
    shard = mix_weight.shape[0] // n_blk
    piece = math.gcd(shard, width)
    at_dp, at_blk = lax.axis_index("dp"), lax.axis_index("blk")
    reach = max(((i + 1) * shard - 1) // width - i * shard // width + 1 for i in range(n_blk))
    reach = min(reach, len(MOST))

    def first_degree(at):
        return jnp.minimum(at * shard // width, len(MOST) - reach)

    place = jnp.stack(
        [at_dp % 2 * n_blk + at_blk, at_blk * (shard // piece), first_degree(at_blk)]
    ).astype(jnp.int32)

    def over_dp(value, step):
        return lax.ppermute(value, "dp", [(i, i ^ step) for i in range(n_dp)])

    def over_blk(value, step):
        return lax.ppermute(value, "blk", [(i, i ^ step) for i in range(n_blk)])

    def all_to_all(value):
        return lax.all_to_all(value, "dp", split_axis=0, concat_axis=0, tiled=True)

    def chip_sum(near, far):
        return near + over_dp(far, 1).astype(jnp.float32)

    def plane_sum(chip):
        height = chip.shape[0] // n_blk
        own = chip[:height]
        for step in range(1, n_blk):
            part = chip[step * height : (step + 1) * height].astype(jnp.bfloat16)
            own = own + over_blk(part, step).astype(jnp.float32)
        return own

    bits = [1 << i for i in range((n_dp // 2).bit_length() - 1)]
    upper = [(at_dp // 2) & bit for bit in bits]

    def z_halved(own):
        for bit, high in zip(bits[:-1], upper):
            half = own.shape[0] // 2
            kept = jnp.where(high > 0, own[half:], own[:half])
            given = jnp.where(high > 0, own[:half], own[half:]).astype(jnp.bfloat16)
            own = kept + over_dp(given, 2 * bit).astype(jnp.float32)
        own = own.astype(jnp.bfloat16)
        return own, over_dp(own, 2 * bits[-1])

    def z_joined(own, *others):
        for bit, high in reversed(list(zip(bits[:-1], upper))):
            other = after(over_dp(own, 2 * bit), *others)
            own = jnp.where(
                high > 0,
                jnp.concatenate([other, own], axis=0),
                jnp.concatenate([own, other], axis=0),
            )
        return own

    def plane_gather(own, needed, *others):
        near = [needed(own, at_blk)]
        near += [over_blk(needed(own, at_blk ^ step), step) for step in range(1, n_blk)]
        return near + [over_dp(after(part, *others), 1) for part in near]

    def needed_degrees(own, at):
        height = width // pieces
        return lax.dynamic_slice_in_dim(own, first_degree(at) * height, reach * height, axis=0)

    sent_most = pick_rows(send_order, features, width, MOST)
    came_most = all_to_all(sent_most)
    sent_last = pick_rows(send_order, after(features, sent_most), width, LAST)
    gate = gate_matrices(pair_index, edge_mask, after(distance, sent_last), radial_weight, rows)
    cotangent, mix_weight, out_weight = lax.optimization_barrier(
        (cotangent, mix_weight, out_weight, gate)
    )[:3]
    cots = {level: flip_cotangent(cotangent, width, level) for level in MOST + LAST}
    maps = degree_products(mix_weight, out_weight)
    flipped, out_flipped = (
        weight.reshape(LMAX + 1, width, width).swapaxes(1, 2).reshape(weight.shape)
        for weight in (mix_weight, out_weight)
    )
    last_map = maps[LAST[0] * width : (LAST[0] + 1) * width]
    ready = (gate, maps, last_map, flipped, out_flipped, *cots.values())
    came_last = all_to_all(after(sent_last, came_most, *ready))

    local = after(came_most, *ready)
    own = plane_sum(chip_sum(*outer_sum(place, gate, local, cots, width, MOST, pieces)))
    own, other = z_halved(own)
    updated = update(gate, maps, local, width, MOST, total, None)

    local = after(came_last, own, other, updated)
    near, far, mixed = outer_sum(place, gate, local, cots, width, LAST, pieces, keep=True)
    most = tree_sum([own, after(other, near)])
    last = plane_sum(chip_sum(near, far)).astype(jnp.bfloat16)
    most = z_joined(most, last)
    most = plane_gather(most, needed_degrees)
    last = tree_sum([last] + [over_dp(last, 2 * step) for step in range(1, n_dp // 2)])
    updated = update(mixed, last_map, local, width, LAST, total, updated)
    mix_grad, out_grad = most_gradients(place, out_flipped, flipped, most, shard, piece)
    last = plane_gather(after(last, updated), lambda own, at: own, mix_grad)
    mix_grad, out_grad = last_gradients(
        place, out_flipped, flipped, last, mix_grad, out_grad, piece
    )
    return updated, mix_grad, out_grad


def solution(mesh):
    in_specs = (
        P(("dp", "blk"), None),
        P(("dp", "blk"), None),
        P(("dp", "blk"), None),
        P(("dp", "blk"), None),
        P(("dp", "blk"), None, None),
        P(("dp", "blk"), None, None),
        P(),
        P(),
        P(),
    )
    out_specs = (P(("dp", "blk"), None), P("blk", None), P("blk", None))
    run = functools.partial(body, n_dp=mesh.shape["dp"], n_blk=mesh.shape["blk"])
    return jax.shard_map(run, mesh=mesh, in_specs=in_specs, out_specs=out_specs, check_vma=False)
```

```python
import functools
import math

import jax
import jax.numpy as jnp
from jax import lax
from jax.experimental import pallas as pl
from jax.experimental.pallas import tpu as pltpu
from jax.sharding import PartitionSpec as P

LMAX = 4
BLOCK = 128
CUT_RADIUS = 5.0
EDGE_SCALE = 0.25
MOST, LAST = (0, 1, 2, 3), (4,)
ORDER = MOST + LAST
VMEM_LIMIT = 48 * 1024 * 1024
PICK_LIMIT = 60 * 1024 * 1024
GRADIENT_LIMIT = 16 * 1024 * 1024
GATE_ROWS = 16
WHOLE = pl.BlockSpec(memory_space=pltpu.VMEM)
ANY = pl.BlockSpec(memory_space=pl.ANY)
SCALARS = pl.BlockSpec(memory_space=pltpu.SMEM)


def params(*semantics, limit=VMEM_LIMIT):
    return pltpu.CompilerParams(dimension_semantics=semantics, vmem_limit_bytes=limit)


def after(value, *others):
    return lax.optimization_barrier((value, *others))[0]


def span(degrees):
    return degrees[0] ** 2, (degrees[-1] + 1) ** 2


def comps_of(degrees):
    return [comp for level in degrees for comp in range(*span((level,)))]


def tree_sum(parts):
    parts = [part.astype(jnp.float32) for part in parts]
    while len(parts) > 1:
        parts = [parts[i] + parts[i + 1] for i in range(0, len(parts), 2)]
    return parts[0].astype(jnp.bfloat16)


def chosen_rows(order_ref, rows):
    local = lax.broadcasted_iota(jnp.int32, (rows, rows), 0)
    return (local == order_ref[...]).astype(jnp.float32).T.astype(jnp.bfloat16)


def pick_kernel(
    order_ref, rows_ref, out_ref, list_ref, held_ref, ready_ref, list_sem, in_sems, out_sems, *, first
):
    count, rows, width = ready_ref.shape
    order_load = pltpu.make_async_copy(order_ref, list_ref, list_sem)
    order_load.start()
    slab = rows // in_sems.shape[0]
    loads = [
        pltpu.make_async_copy(
            rows_ref.at[pl.ds(i * slab, slab), pl.ds(first * width, count * width)],
            held_ref.at[pl.ds(i * slab, slab), :],
            in_sems.at[i],
        )
        for i in range(in_sems.shape[0])
    ]
    for load in loads:
        load.start()
    order_load.wait()
    pick = chosen_rows(list_ref, rows)
    for load in loads:
        load.wait()
    stores = []
    for i in range(count):
        ready_ref[i] = jnp.dot(
            pick, held_ref[:, i * width : (i + 1) * width], preferred_element_type=jnp.float32
        ).astype(jnp.bfloat16)
        stores.append(
            pltpu.make_async_copy(
                ready_ref.at[i], out_ref.at[:, pl.ds(i * width, width)], out_sems.at[i]
            )
        )
        stores[-1].start()
    for store in stores:
        store.wait()


def pick_rows(order, features, width, degrees):
    rows = features.shape[0]
    first, last = span(degrees)
    count = last - first
    return pl.pallas_call(
        functools.partial(pick_kernel, first=first),
        in_specs=[ANY, ANY],
        out_specs=ANY,
        out_shape=jax.ShapeDtypeStruct((rows, count * width), jnp.bfloat16),
        scratch_shapes=[
            pltpu.VMEM(order.shape, jnp.int32),
            pltpu.VMEM((rows, count * width), jnp.bfloat16),
            pltpu.VMEM((count, rows, width), jnp.bfloat16),
            pltpu.SemaphoreType.DMA,
            pltpu.SemaphoreType.DMA((8,)),
            pltpu.SemaphoreType.DMA((count,)),
        ],
        compiler_params=params(limit=PICK_LIMIT),
        name="pick_rows",
    )(order, features)


def gate_kernel(pairs_ref, mask_ref, dist_ref, weight_ref, out_ref, radial_ref, *, basis_count):
    pair, step = pl.program_id(0), pl.program_id(1)

    @pl.when((pair == 0) & (step == 0))
    def _():
        out_ref[...] = jnp.zeros_like(out_ref)

    half = math.sqrt(0.5 * math.log2(math.e))
    dist = dist_ref[0]
    scaled = dist * (half * (basis_count - 1) / CUT_RADIUS)
    centers = lax.broadcasted_iota(jnp.int32, (basis_count, BLOCK), 0).astype(jnp.float32) * half
    weights = weight_ref[...]
    levels = LMAX + 1
    for row in range(GATE_ROWS):
        offset = scaled[row : row + 1, :] - centers
        phi = jnp.exp2(-(offset * offset))
        high = phi.astype(jnp.bfloat16)
        low = (phi - high.astype(jnp.float32)).astype(jnp.bfloat16)
        radial = jnp.dot(weights, high, preferred_element_type=jnp.float32)
        radial = radial + jnp.dot(weights, low, preferred_element_type=jnp.float32)
        radial = radial[0:8] + radial[8:16]
        for level in range(levels):
            radial_ref[level, row : row + 1, :] = radial[level : level + 1, :]
    envelope = (
        (0.5 * EDGE_SCALE)
        * (jnp.cos((math.pi / CUT_RADIUS) * dist) + 1.0)
        * mask_ref[0].astype(jnp.float32)
    )
    dest = pl.multiple_of(pairs_ref[pair, 0] * BLOCK + step * GATE_ROWS, GATE_ROWS)
    src = pl.multiple_of(pairs_ref[pair, 1] * BLOCK, BLOCK)
    for level in range(levels):
        out_ref[level, pl.ds(dest, GATE_ROWS), pl.ds(src, BLOCK)] = (
            radial_ref[level] * envelope
        ).astype(jnp.bfloat16)


def gate_matrices(pairs, mask, dist, radial_weight, rows):
    count = pairs.shape[0]
    levels = radial_weight.shape[1]
    transposed = radial_weight.T
    high = transposed.astype(jnp.bfloat16)
    low = (transposed - high.astype(jnp.float32)).astype(jnp.bfloat16)
    pad = ((0, 8 - levels), (0, 0))
    weights = jnp.concatenate([jnp.pad(high, pad), jnp.pad(low, pad)], axis=0)
    kernel = functools.partial(gate_kernel, basis_count=radial_weight.shape[0])
    edges = pl.BlockSpec((1, GATE_ROWS, BLOCK), lambda p, s, pairs: (p, s, 0))
    return pl.pallas_call(
        kernel,
        grid_spec=pltpu.PrefetchScalarGridSpec(
            num_scalar_prefetch=1,
            grid=(count, BLOCK // GATE_ROWS),
            in_specs=[edges, edges, pl.BlockSpec(weights.shape, lambda p, s, pairs: (0, 0))],
            out_specs=pl.BlockSpec((levels, rows, rows), lambda p, s, pairs: (0, 0, 0)),
            scratch_shapes=[pltpu.VMEM((levels, GATE_ROWS, BLOCK), jnp.float32)],
        ),
        out_shape=jax.ShapeDtypeStruct((levels, rows, rows), jnp.bfloat16),
        compiler_params=params("arbitrary", "arbitrary"),
        cost_estimate=pl.CostEstimate(
            flops=2 * 3 * 512 * count * BLOCK * BLOCK * radial_weight.shape[0],
            bytes_accessed=2 * 4 * count * BLOCK * BLOCK,
            transcendentals=count * BLOCK * BLOCK * radial_weight.shape[0],
        ),
        name="gate",
    )(pairs, mask, dist, weights)


def product_kernel(left_ref, right_ref, out_ref):
    out_ref[...] = jnp.dot(
        left_ref[...], right_ref[...], preferred_element_type=jnp.float32
    ).astype(jnp.bfloat16)


def degree_products(left, right):
    width = left.shape[1]
    block = pl.BlockSpec((width, width), lambda i: (i, 0))
    return pl.pallas_call(
        product_kernel,
        grid=(left.shape[0] // width,),
        in_specs=[block, block],
        out_specs=block,
        out_shape=jax.ShapeDtypeStruct(left.shape, jnp.bfloat16),
        compiler_params=params("arbitrary"),
        name="degree_products",
    )(left, right)


def flip_kernel(rows_ref, out_ref):
    out_ref[...] = rows_ref[...].T


def flip_cotangent(cotangent, width, level):
    rows = cotangent.shape[0]
    first, last = span((level,))
    return pl.pallas_call(
        flip_kernel,
        grid=(last - first,),
        in_specs=[pl.BlockSpec((rows, width), lambda i: (0, first + i))],
        out_specs=pl.BlockSpec((width, rows), lambda i: (0, i)),
        out_shape=jax.ShapeDtypeStruct((width, (last - first) * rows), jnp.bfloat16),
        compiler_params=params("arbitrary"),
        name="flip_cotangent",
    )(cotangent)


def outer_kernel(place_ref, gate_ref, local_ref, *refs, pieces, levels):
    cots = refs[: len(levels)]
    near_ref, far_ref, mixed_ref, sum_ref = refs[len(levels) :]
    rows, width = local_ref.shape[0], mixed_ref.shape[1]
    comps = comps_of(levels)
    for slot, level in enumerate(levels):
        first, last = span((level,))
        for comp in range(first, last):
            at = comps.index(comp) * width
            mixed_ref[(comp - first) * rows : (comp - first + 1) * rows, :] = jnp.dot(
                gate_ref[level], local_ref[:, at : at + width], preferred_element_type=jnp.float32
            ).astype(jnp.bfloat16)
        depth = (last - first) * rows
        flipped = jnp.dot(
            cots[slot][...], mixed_ref[0:depth, :], preferred_element_type=jnp.float32
        )
        sum_ref[slot * width : (slot + 1) * width, :] = flipped.T
    half, height = pieces // 2, width // pieces
    for step in range(half):
        near = pl.multiple_of((place_ref[0] ^ step) * height, height)
        far = pl.multiple_of((place_ref[0] ^ (step + half)) * height, height)
        for slot in range(len(levels)):
            to = (step * len(levels) + slot) * height
            near_ref[to : to + height, :] = sum_ref[pl.ds(slot * width + near, height), :]
            far_ref[to : to + height, :] = sum_ref[pl.ds(slot * width + far, height), :].astype(
                jnp.bfloat16
            )


def outer_sum(place, gate, local, cots, width, levels, pieces):
    rows = gate.shape[1]
    whole = len(levels) * width
    deepest = 2 * max(levels) + 1
    total = sum(2 * level + 1 for level in levels)
    return pl.pallas_call(
        functools.partial(outer_kernel, pieces=pieces, levels=levels),
        in_specs=[SCALARS] + [WHOLE] * (2 + len(levels)),
        out_specs=[WHOLE] * 2,
        out_shape=[
            jax.ShapeDtypeStruct((whole // 2, width), jnp.float32),
            jax.ShapeDtypeStruct((whole // 2, width), jnp.bfloat16),
        ],
        scratch_shapes=[
            pltpu.VMEM((deepest * rows, width), jnp.bfloat16),
            pltpu.VMEM((whole, width), jnp.float32),
        ],
        compiler_params=params(),
        cost_estimate=pl.CostEstimate(
            flops=2 * total * rows * width * (rows + width),
            bytes_accessed=4 * total * rows * width,
            transcendentals=0,
        ),
        name="outer_sum",
    )(place, gate, local, *[cots[level] for level in levels])


def update_kernel(gate_ref, map_ref, local_ref, *refs, degrees):
    out_ref, ready_ref, sems = refs[-3:]
    width = map_ref.shape[1]
    copies = []
    for index, comp in enumerate(comps_of(degrees)):
        level = math.isqrt(comp)
        at = index * width
        hidden = local_ref[:, at : at + width]
        mixed = jnp.dot(gate_ref[level], hidden, preferred_element_type=jnp.float32)
        weight = map_ref[level * width : (level + 1) * width, :]
        added = jnp.dot(mixed.astype(jnp.bfloat16), weight, preferred_element_type=jnp.float32)
        ready_ref[index] = (hidden.astype(jnp.float32) + added).astype(jnp.bfloat16)
        copies.append(
            pltpu.make_async_copy(
                ready_ref.at[index],
                out_ref.at[:, pl.ds(comp * width, width)],
                sems.at[index],
            )
        )
        copies[-1].start()
    for copy in copies:
        copy.wait()


def update(gate, maps, local, width, degrees, total, held):
    rows = local.shape[0]
    count = len(comps_of(degrees))
    in_specs = [WHOLE] * 3
    operands = [gate, maps, local]
    aliases = {}
    if held is not None:
        in_specs.append(ANY)
        operands.append(held)
        aliases = {3: 0}
    return pl.pallas_call(
        functools.partial(update_kernel, degrees=degrees),
        in_specs=in_specs,
        out_specs=ANY,
        out_shape=jax.ShapeDtypeStruct((rows, total), jnp.bfloat16),
        scratch_shapes=[
            pltpu.VMEM((count, rows, width), jnp.bfloat16),
            pltpu.SemaphoreType.DMA((count,)),
        ],
        input_output_aliases=aliases,
        compiler_params=params(),
        cost_estimate=pl.CostEstimate(
            flops=2 * count * rows * width * (rows + width),
            bytes_accessed=4 * count * rows * width,
            transcendentals=0,
        ),
        name="update",
    )(*operands)


def place_parts(place_ref, parts, outer_ref):
    width = outer_ref.shape[1]
    height = width // len(parts)
    for step, part in enumerate(parts):
        row = pl.multiple_of((place_ref[0] ^ step) * height, height)
        for slot in range(part.shape[0] // height):
            outer_ref[pl.ds(slot * width + row, height), :] = part[
                slot * height : (slot + 1) * height, :
            ]


def gradients(rows, outer, flipped, weight):
    mix = jnp.dot(rows, weight, preferred_element_type=jnp.float32)
    return mix, jnp.dot(flipped, outer, preferred_element_type=jnp.float32)


def most_kernel(place_ref, weight_ref, flip_ref, *refs, piece):
    *parts, mix_ref, out_ref, outer_ref = refs
    width = weight_ref.shape[0]

    @pl.when(pl.program_id(0) == 0)
    def _():
        place_parts(place_ref, parts, outer_ref)

    row = (place_ref[1] + pl.program_id(0)) * piece

    @pl.when(row < len(MOST) * width)
    def _():
        first = pl.multiple_of((row // width - place_ref[2]) * width, width)
        mix_ref[...], out_ref[...] = gradients(
            outer_ref[pl.ds(pl.multiple_of(first + row % width, piece), piece), :],
            outer_ref[pl.ds(first, width), :],
            flip_ref[...],
            weight_ref[...],
        )


def most_gradients(place, weight, flipped, parts, shard, piece):
    width = weight.shape[1]
    whole = pl.BlockSpec(parts[0].shape, lambda i, place: (0, 0))
    return pl.pallas_call(
        functools.partial(most_kernel, piece=piece),
        grid_spec=pltpu.PrefetchScalarGridSpec(
            num_scalar_prefetch=1,
            grid=(shard // piece,),
            in_specs=[
                pl.BlockSpec(
                    (width, width), lambda i, place: ((place[1] + i) * piece // width, 0)
                ),
                pl.BlockSpec((piece, width), lambda i, place: (place[1] + i, 0)),
            ]
            + [whole] * len(parts),
            out_specs=[pl.BlockSpec((piece, width), lambda i, place: (i, 0))] * 2,
            scratch_shapes=[pltpu.VMEM((len(parts) * parts[0].shape[0], width), jnp.bfloat16)],
        ),
        out_shape=[jax.ShapeDtypeStruct((shard, width), jnp.float32)] * 2,
        compiler_params=params("arbitrary", limit=GRADIENT_LIMIT),
        name="most_gradients",
    )(place, weight, flipped, *parts)


def last_kernel(place_ref, weight_ref, flip_ref, *refs, piece):
    *parts, _, _, mix_out, out_out, outer_ref, mix_ref, out_ref, sems = refs
    width = weight_ref.shape[0]
    place_parts(place_ref, parts, outer_ref)
    count = mix_ref.shape[0]

    def each(index):
        row = (place_ref[1] + index) * piece - LAST[0] * width
        to = pl.ds(index * piece, piece)
        copies = [
            pltpu.make_async_copy(mix_ref.at[index], mix_out.at[to, :], sems.at[index, 0]),
            pltpu.make_async_copy(out_ref.at[index], out_out.at[to, :], sems.at[index, 1]),
        ]
        return row, (row >= 0) & (row < width), copies

    for index in range(count):
        row, held, copies = each(index)

        @pl.when(held)
        def _():
            mine = pl.ds(pl.multiple_of(row, piece), piece)
            mix_ref[index], out_ref[index] = gradients(
                outer_ref[mine, :], outer_ref[...], flip_ref[mine, :], weight_ref[...]
            )
            for copy in copies:
                copy.start()

    for index in range(count):
        _, held, copies = each(index)

        @pl.when(held)
        def _():
            for copy in copies:
                copy.wait()


def last_gradients(place, weight, flipped, parts, mix_grad, out_grad, piece):
    shard, width = mix_grad.shape
    own = pl.BlockSpec((width, width), lambda i: (LAST[0], 0))
    whole = pl.BlockSpec(parts[0].shape, lambda i: (0, 0))
    count = shard // piece
    return pl.pallas_call(
        functools.partial(last_kernel, piece=piece),
        grid=(1,),
        in_specs=[SCALARS, own, own] + [whole] * len(parts) + [ANY] * 2,
        out_specs=[ANY] * 2,
        out_shape=[jax.ShapeDtypeStruct(mix_grad.shape, jnp.float32)] * 2,
        scratch_shapes=[
            pltpu.VMEM((width, width), jnp.bfloat16),
            pltpu.VMEM((count, piece, width), jnp.float32),
            pltpu.VMEM((count, piece, width), jnp.float32),
            pltpu.SemaphoreType.DMA((count, 2)),
        ],
        input_output_aliases={3 + len(parts): 0, 4 + len(parts): 1},
        compiler_params=params("arbitrary", limit=GRADIENT_LIMIT),
        name="last_gradients",
    )(place, weight, flipped, *parts, mix_grad, out_grad)


def body(
    features,
    cotangent,
    send_order,
    pair_index,
    edge_mask,
    distance,
    radial_weight,
    mix_weight,
    out_weight,
    *,
    n_dp,
    n_blk,
):
    rows, total = features.shape
    width = mix_weight.shape[1]
    pieces = 2 * n_blk
    shard = mix_weight.shape[0] // n_blk
    piece = math.gcd(shard, width)
    at_dp, at_blk = lax.axis_index("dp"), lax.axis_index("blk")
    reach = max(((i + 1) * shard - 1) // width - i * shard // width + 1 for i in range(n_blk))
    reach = min(reach, len(MOST))

    def first_degree(at):
        return jnp.minimum(at * shard // width, len(MOST) - reach)

    place = jnp.stack(
        [at_dp % 2 * n_blk + at_blk, at_blk * (shard // piece), first_degree(at_blk)]
    ).astype(jnp.int32)

    def over_dp(value, step):
        return lax.ppermute(value, "dp", [(i, i ^ step) for i in range(n_dp)])

    def over_blk(value, step):
        return lax.ppermute(value, "blk", [(i, i ^ step) for i in range(n_blk)])

    def all_to_all(value):
        return lax.all_to_all(value, "dp", split_axis=0, concat_axis=0, tiled=True)

    def chip_sum(near, far):
        return near + over_dp(far, 1).astype(jnp.float32)

    def plane_sum(chip):
        height = chip.shape[0] // n_blk
        own = chip[:height]
        for step in range(1, n_blk):
            part = chip[step * height : (step + 1) * height].astype(jnp.bfloat16)
            own = own + over_blk(part, step).astype(jnp.float32)
        return own

    bits = [1 << i for i in range((n_dp // 2).bit_length() - 1)]
    upper = [(at_dp // 2) & bit for bit in bits]

    def z_halved(own):
        for bit, high in zip(bits[:-1], upper):
            half = own.shape[0] // 2
            kept = jnp.where(high > 0, own[half:], own[:half])
            given = jnp.where(high > 0, own[:half], own[half:]).astype(jnp.bfloat16)
            own = kept + over_dp(given, 2 * bit).astype(jnp.float32)
        own = own.astype(jnp.bfloat16)
        return own, over_dp(own, 2 * bits[-1])

    def z_joined(own, *others):
        for bit, high in reversed(list(zip(bits[:-1], upper))):
            other = after(over_dp(own, 2 * bit), *others)
            own = jnp.where(
                high > 0,
                jnp.concatenate([other, own], axis=0),
                jnp.concatenate([own, other], axis=0),
            )
        return own

    def plane_gather(own, needed, *others):
        near = [needed(own, at_blk)]
        near += [over_blk(needed(own, at_blk ^ step), step) for step in range(1, n_blk)]
        return near + [over_dp(after(part, *others), 1) for part in near]

    def needed_degrees(own, at):
        height = width // pieces
        return lax.dynamic_slice_in_dim(own, first_degree(at) * height, reach * height, axis=0)

    sent_most = pick_rows(send_order, features, width, MOST)
    came_most = all_to_all(sent_most)
    sent_last = pick_rows(send_order, after(features, sent_most), width, LAST)
    gate = gate_matrices(pair_index, edge_mask, after(distance, sent_last), radial_weight, rows)
    cotangent, mix_weight, out_weight = lax.optimization_barrier(
        (cotangent, mix_weight, out_weight, gate)
    )[:3]
    cots = {level: flip_cotangent(cotangent, width, level) for level in MOST + LAST}
    maps = degree_products(mix_weight, out_weight)
    flipped, out_flipped = (
        weight.reshape(LMAX + 1, width, width).swapaxes(1, 2).reshape(weight.shape)
        for weight in (mix_weight, out_weight)
    )
    ready = (gate, maps, flipped, out_flipped, *cots.values())
    came_last = all_to_all(after(sent_last, came_most, *ready))

    local = after(came_most, *ready)
    own = plane_sum(chip_sum(*outer_sum(place, gate, local, cots, width, MOST, pieces)))
    own, other = z_halved(own)
    updated = update(gate, maps, local, width, MOST, total, None)

    local = after(came_last, own, other, updated)
    near, far = outer_sum(place, gate, local, cots, width, LAST, pieces)
    most = tree_sum([own, after(other, near)])
    last = plane_sum(chip_sum(near, far)).astype(jnp.bfloat16)
    local = after(local, last)
    others = [over_dp(last, 2 * step) for step in range(1, n_dp // 2)]
    updated = update(gate, maps, local, width, LAST, total, updated)
    *others, updated = lax.optimization_barrier((*others, updated))
    last = tree_sum([last, *others])
    most = plane_gather(z_joined(most, *others), needed_degrees)
    mix_grad, out_grad = most_gradients(place, out_flipped, flipped, most, shard, piece)
    last = plane_gather(after(last, updated), lambda own, at: own, mix_grad)
    mix_grad, out_grad = last_gradients(
        place, out_flipped, flipped, last, mix_grad, out_grad, piece
    )
    return updated, mix_grad, out_grad


def solution(mesh):
    in_specs = (
        P(("dp", "blk"), None),
        P(("dp", "blk"), None),
        P(("dp", "blk"), None),
        P(("dp", "blk"), None),
        P(("dp", "blk"), None, None),
        P(("dp", "blk"), None, None),
        P(),
        P(),
        P(),
    )
    out_specs = (P(("dp", "blk"), None), P("blk", None), P("blk", None))
    run = functools.partial(body, n_dp=mesh.shape["dp"], n_blk=mesh.shape["blk"])
    return jax.shard_map(run, mesh=mesh, in_specs=in_specs, out_specs=out_specs, check_vma=False)
```

```python
import functools
import math

import jax
import jax.numpy as jnp
from jax import lax
from jax.experimental import pallas as pl
from jax.experimental.pallas import tpu as pltpu
from jax.sharding import PartitionSpec as P

LMAX = 4
BLOCK = 128
CUT_RADIUS = 5.0
EDGE_SCALE = 0.25
MOST, LAST = (0, 1, 2, 3), (4,)
ORDER = MOST + LAST
VMEM_LIMIT = 48 * 1024 * 1024
PICK_LIMIT = 60 * 1024 * 1024
GRADIENT_LIMIT = 16 * 1024 * 1024
GATE_ROWS = 16
WHOLE = pl.BlockSpec(memory_space=pltpu.VMEM)
ANY = pl.BlockSpec(memory_space=pl.ANY)
SCALARS = pl.BlockSpec(memory_space=pltpu.SMEM)


def params(*semantics, limit=VMEM_LIMIT):
    return pltpu.CompilerParams(dimension_semantics=semantics, vmem_limit_bytes=limit)


def after(value, *others):
    return lax.optimization_barrier((value, *others))[0]


def span(degrees):
    return degrees[0] ** 2, (degrees[-1] + 1) ** 2


def comps_of(degrees):
    return [comp for level in degrees for comp in range(*span((level,)))]


def tree_sum(parts):
    parts = [part.astype(jnp.float32) for part in parts]
    while len(parts) > 1:
        parts = [parts[i] + parts[i + 1] for i in range(0, len(parts), 2)]
    return parts[0].astype(jnp.bfloat16)


def chosen_rows(order_ref, rows):
    local = lax.broadcasted_iota(jnp.int32, (rows, rows), 0)
    return (local == order_ref[...]).astype(jnp.float32).T.astype(jnp.bfloat16)


def pick_kernel(
    order_ref, rows_ref, out_ref, list_ref, held_ref, ready_ref, list_sem, in_sems, out_sems, *, first
):
    count, rows, width = ready_ref.shape
    order_load = pltpu.make_async_copy(order_ref, list_ref, list_sem)
    order_load.start()
    slab = rows // in_sems.shape[0]
    loads = [
        pltpu.make_async_copy(
            rows_ref.at[pl.ds(i * slab, slab), pl.ds(first * width, count * width)],
            held_ref.at[pl.ds(i * slab, slab), :],
            in_sems.at[i],
        )
        for i in range(in_sems.shape[0])
    ]
    for load in loads:
        load.start()
    order_load.wait()
    pick = chosen_rows(list_ref, rows)
    for load in loads:
        load.wait()
    stores = []
    for i in range(count):
        ready_ref[i] = jnp.dot(
            pick, held_ref[:, i * width : (i + 1) * width], preferred_element_type=jnp.float32
        ).astype(jnp.bfloat16)
        stores.append(
            pltpu.make_async_copy(
                ready_ref.at[i], out_ref.at[:, pl.ds(i * width, width)], out_sems.at[i]
            )
        )
        stores[-1].start()
    for store in stores:
        store.wait()


def pick_rows(order, features, width, degrees):
    rows = features.shape[0]
    first, last = span(degrees)
    count = last - first
    return pl.pallas_call(
        functools.partial(pick_kernel, first=first),
        in_specs=[ANY, ANY],
        out_specs=ANY,
        out_shape=jax.ShapeDtypeStruct((rows, count * width), jnp.bfloat16),
        scratch_shapes=[
            pltpu.VMEM(order.shape, jnp.int32),
            pltpu.VMEM((rows, count * width), jnp.bfloat16),
            pltpu.VMEM((count, rows, width), jnp.bfloat16),
            pltpu.SemaphoreType.DMA,
            pltpu.SemaphoreType.DMA((8,)),
            pltpu.SemaphoreType.DMA((count,)),
        ],
        compiler_params=params(limit=PICK_LIMIT),
        name="pick_rows",
    )(order, features)


def gate_kernel(pairs_ref, mask_ref, dist_ref, weight_ref, out_ref, radial_ref, *, basis_count):
    pair, step = pl.program_id(0), pl.program_id(1)

    @pl.when((pair == 0) & (step == 0))
    def _():
        out_ref[...] = jnp.zeros_like(out_ref)

    half = math.sqrt(0.5 * math.log2(math.e))
    dist = dist_ref[0]
    scaled = dist * (half * (basis_count - 1) / CUT_RADIUS)
    centers = lax.broadcasted_iota(jnp.int32, (basis_count, BLOCK), 0).astype(jnp.float32) * half
    weights = weight_ref[...]
    levels = LMAX + 1
    for row in range(GATE_ROWS):
        offset = scaled[row : row + 1, :] - centers
        phi = jnp.exp2(-(offset * offset))
        high = phi.astype(jnp.bfloat16)
        low = (phi - high.astype(jnp.float32)).astype(jnp.bfloat16)
        radial = jnp.dot(weights, high, preferred_element_type=jnp.float32)
        radial = radial + jnp.dot(weights, low, preferred_element_type=jnp.float32)
        radial = radial[0:8] + radial[8:16]
        for level in range(levels):
            radial_ref[level, row : row + 1, :] = radial[level : level + 1, :]
    envelope = (
        (0.5 * EDGE_SCALE)
        * (jnp.cos((math.pi / CUT_RADIUS) * dist) + 1.0)
        * mask_ref[0].astype(jnp.float32)
    )
    dest = pl.multiple_of(pairs_ref[pair, 0] * BLOCK + step * GATE_ROWS, GATE_ROWS)
    src = pl.multiple_of(pairs_ref[pair, 1] * BLOCK, BLOCK)
    for level in range(levels):
        out_ref[level, pl.ds(dest, GATE_ROWS), pl.ds(src, BLOCK)] = (
            radial_ref[level] * envelope
        ).astype(jnp.bfloat16)


def gate_matrices(pairs, mask, dist, radial_weight, rows):
    count = pairs.shape[0]
    levels = radial_weight.shape[1]
    transposed = radial_weight.T
    high = transposed.astype(jnp.bfloat16)
    low = (transposed - high.astype(jnp.float32)).astype(jnp.bfloat16)
    pad = ((0, 8 - levels), (0, 0))
    weights = jnp.concatenate([jnp.pad(high, pad), jnp.pad(low, pad)], axis=0)
    kernel = functools.partial(gate_kernel, basis_count=radial_weight.shape[0])
    edges = pl.BlockSpec((1, GATE_ROWS, BLOCK), lambda p, s, pairs: (p, s, 0))
    return pl.pallas_call(
        kernel,
        grid_spec=pltpu.PrefetchScalarGridSpec(
            num_scalar_prefetch=1,
            grid=(count, BLOCK // GATE_ROWS),
            in_specs=[edges, edges, pl.BlockSpec(weights.shape, lambda p, s, pairs: (0, 0))],
            out_specs=pl.BlockSpec((levels, rows, rows), lambda p, s, pairs: (0, 0, 0)),
            scratch_shapes=[pltpu.VMEM((levels, GATE_ROWS, BLOCK), jnp.float32)],
        ),
        out_shape=jax.ShapeDtypeStruct((levels, rows, rows), jnp.bfloat16),
        compiler_params=params("arbitrary", "arbitrary"),
        cost_estimate=pl.CostEstimate(
            flops=2 * 3 * 512 * count * BLOCK * BLOCK * radial_weight.shape[0],
            bytes_accessed=2 * 4 * count * BLOCK * BLOCK,
            transcendentals=count * BLOCK * BLOCK * radial_weight.shape[0],
        ),
        name="gate",
    )(pairs, mask, dist, weights)


def product_kernel(left_ref, right_ref, out_ref):
    out_ref[...] = jnp.dot(
        left_ref[...], right_ref[...], preferred_element_type=jnp.float32
    ).astype(jnp.bfloat16)


def degree_products(left, right):
    width = left.shape[1]
    block = pl.BlockSpec((width, width), lambda i: (i, 0))
    return pl.pallas_call(
        product_kernel,
        grid=(left.shape[0] // width,),
        in_specs=[block, block],
        out_specs=block,
        out_shape=jax.ShapeDtypeStruct(left.shape, jnp.bfloat16),
        compiler_params=params("arbitrary"),
        name="degree_products",
    )(left, right)


def flip_kernel(rows_ref, out_ref):
    out_ref[...] = rows_ref[...].T


def flip_cotangent(cotangent, width, level):
    rows = cotangent.shape[0]
    first, last = span((level,))
    return pl.pallas_call(
        flip_kernel,
        grid=(last - first,),
        in_specs=[pl.BlockSpec((rows, width), lambda i: (0, first + i))],
        out_specs=pl.BlockSpec((width, rows), lambda i: (0, i)),
        out_shape=jax.ShapeDtypeStruct((width, (last - first) * rows), jnp.bfloat16),
        compiler_params=params("arbitrary"),
        name="flip_cotangent",
    )(cotangent)


def outer_kernel(place_ref, gate_ref, local_ref, *refs, pieces, levels):
    cots = refs[: len(levels)]
    near_ref, far_ref, mixed_ref, sum_ref = refs[len(levels) :]
    rows, width = local_ref.shape[0], mixed_ref.shape[1]
    comps = comps_of(levels)
    for slot, level in enumerate(levels):
        first, last = span((level,))
        for comp in range(first, last):
            at = comps.index(comp) * width
            mixed_ref[(comp - first) * rows : (comp - first + 1) * rows, :] = jnp.dot(
                gate_ref[level], local_ref[:, at : at + width], preferred_element_type=jnp.float32
            ).astype(jnp.bfloat16)
        depth = (last - first) * rows
        flipped = jnp.dot(
            cots[slot][...], mixed_ref[0:depth, :], preferred_element_type=jnp.float32
        )
        sum_ref[slot * width : (slot + 1) * width, :] = flipped.T
    half = pieces // 2
    height = near_ref.shape[0] // half
    for step in range(half):
        to = slice(step * height, (step + 1) * height)
        row = pl.multiple_of((place_ref[0] ^ step) * height, height)
        near_ref[to, :] = sum_ref[pl.ds(row, height), :]
        row = pl.multiple_of((place_ref[0] ^ (step + half)) * height, height)
        far_ref[to, :] = sum_ref[pl.ds(row, height), :].astype(jnp.bfloat16)


def outer_sum(place, gate, local, cots, width, levels, pieces):
    rows = gate.shape[1]
    whole = len(levels) * width
    deepest = 2 * max(levels) + 1
    total = sum(2 * level + 1 for level in levels)
    return pl.pallas_call(
        functools.partial(outer_kernel, pieces=pieces, levels=levels),
        in_specs=[SCALARS] + [WHOLE] * (2 + len(levels)),
        out_specs=[WHOLE] * 2,
        out_shape=[
            jax.ShapeDtypeStruct((whole // 2, width), jnp.float32),
            jax.ShapeDtypeStruct((whole // 2, width), jnp.bfloat16),
        ],
        scratch_shapes=[
            pltpu.VMEM((deepest * rows, width), jnp.bfloat16),
            pltpu.VMEM((whole, width), jnp.float32),
        ],
        compiler_params=params(),
        cost_estimate=pl.CostEstimate(
            flops=2 * total * rows * width * (rows + width),
            bytes_accessed=4 * total * rows * width,
            transcendentals=0,
        ),
        name="outer_sum",
    )(place, gate, local, *[cots[level] for level in levels])


def update_kernel(gate_ref, map_ref, local_ref, *refs, degrees):
    out_ref, ready_ref, sems = refs[-3:]
    width = map_ref.shape[1]
    copies = []
    for index, comp in enumerate(comps_of(degrees)):
        level = math.isqrt(comp)
        at = index * width
        hidden = local_ref[:, at : at + width]
        mixed = jnp.dot(gate_ref[level], hidden, preferred_element_type=jnp.float32)
        added = jnp.dot(
            mixed.astype(jnp.bfloat16),
            map_ref[level * width : (level + 1) * width, :],
            preferred_element_type=jnp.float32,
        )
        ready_ref[index] = (hidden.astype(jnp.float32) + added).astype(jnp.bfloat16)
        copies.append(
            pltpu.make_async_copy(
                ready_ref.at[index],
                out_ref.at[:, pl.ds(comp * width, width)],
                sems.at[index],
            )
        )
        copies[-1].start()
    for copy in copies:
        copy.wait()


def update(gate, maps, local, width, degrees, total, held):
    rows = gate.shape[1]
    count = len(comps_of(degrees))
    in_specs = [WHOLE] * 3
    operands = [gate, maps, local]
    aliases = {}
    if held is not None:
        in_specs.append(ANY)
        operands.append(held)
        aliases = {3: 0}
    return pl.pallas_call(
        functools.partial(update_kernel, degrees=degrees),
        in_specs=in_specs,
        out_specs=ANY,
        out_shape=jax.ShapeDtypeStruct((rows, total), jnp.bfloat16),
        scratch_shapes=[
            pltpu.VMEM((count, rows, width), jnp.bfloat16),
            pltpu.SemaphoreType.DMA((count,)),
        ],
        input_output_aliases=aliases,
        compiler_params=params(),
        cost_estimate=pl.CostEstimate(
            flops=2 * count * rows * width * (rows + width),
            bytes_accessed=4 * count * rows * width,
            transcendentals=0,
        ),
        name="update",
    )(*operands)


def place_parts(place_ref, parts, outer_ref):
    height = parts[0].shape[0]
    for step, part in enumerate(parts):
        row = pl.multiple_of((place_ref[0] ^ step) * height, height)
        outer_ref[pl.ds(row, height), :] = part[...]


def gradients(rows, outer, flipped, weight):
    mix = jnp.dot(rows, weight, preferred_element_type=jnp.float32)
    return mix, jnp.dot(flipped, outer, preferred_element_type=jnp.float32)


def most_kernel(place_ref, weight_ref, flip_ref, *refs, piece):
    *parts, mix_ref, out_ref, outer_ref = refs
    width = weight_ref.shape[0]

    @pl.when(pl.program_id(0) == 0)
    def _():
        place_parts(place_ref, parts, outer_ref)

    row = (place_ref[1] + pl.program_id(0)) * piece

    @pl.when(row < len(MOST) * width)
    def _():
        first = pl.multiple_of(row // width * width, width)
        mix_ref[...], out_ref[...] = gradients(
            outer_ref[pl.ds(pl.multiple_of(row, piece), piece), :],
            outer_ref[pl.ds(first, width), :],
            flip_ref[...],
            weight_ref[...],
        )


def most_gradients(place, weight, flipped, parts, shard, piece):
    width = weight.shape[1]
    whole = pl.BlockSpec(parts[0].shape, lambda i, place: (0, 0))
    return pl.pallas_call(
        functools.partial(most_kernel, piece=piece),
        grid_spec=pltpu.PrefetchScalarGridSpec(
            num_scalar_prefetch=1,
            grid=(shard // piece,),
            in_specs=[
                pl.BlockSpec(
                    (width, width), lambda i, place: ((place[1] + i) * piece // width, 0)
                ),
                pl.BlockSpec((piece, width), lambda i, place: (place[1] + i, 0)),
            ]
            + [whole] * len(parts),
            out_specs=[pl.BlockSpec((piece, width), lambda i, place: (i, 0))] * 2,
            scratch_shapes=[pltpu.VMEM((len(MOST) * width, width), jnp.bfloat16)],
        ),
        out_shape=[jax.ShapeDtypeStruct((shard, width), jnp.float32)] * 2,
        compiler_params=params("arbitrary", limit=GRADIENT_LIMIT),
        name="most_gradients",
    )(place, weight, flipped, *parts)


def last_kernel(place_ref, weight_ref, flip_ref, *refs, piece):
    *parts, _, _, mix_out, out_out, outer_ref, mix_ref, out_ref, sems = refs
    width = weight_ref.shape[0]
    place_parts(place_ref, parts, outer_ref)
    count = mix_ref.shape[0]

    def each(index):
        row = (place_ref[1] + index) * piece - LAST[0] * width
        to = pl.ds(index * piece, piece)
        copies = [
            pltpu.make_async_copy(mix_ref.at[index], mix_out.at[to, :], sems.at[index, 0]),
            pltpu.make_async_copy(out_ref.at[index], out_out.at[to, :], sems.at[index, 1]),
        ]
        return row, (row >= 0) & (row < width), copies

    for index in range(count):
        row, held, copies = each(index)

        @pl.when(held)
        def _():
            mine = pl.ds(pl.multiple_of(row, piece), piece)
            mix_ref[index], out_ref[index] = gradients(
                outer_ref[mine, :], outer_ref[...], flip_ref[mine, :], weight_ref[...]
            )
            for copy in copies:
                copy.start()

    for index in range(count):
        _, held, copies = each(index)

        @pl.when(held)
        def _():
            for copy in copies:
                copy.wait()


def last_gradients(place, weight, flipped, parts, mix_grad, out_grad, piece):
    shard, width = mix_grad.shape
    own = pl.BlockSpec((width, width), lambda i: (LAST[0], 0))
    whole = pl.BlockSpec(parts[0].shape, lambda i: (0, 0))
    count = shard // piece
    return pl.pallas_call(
        functools.partial(last_kernel, piece=piece),
        grid=(1,),
        in_specs=[SCALARS, own, own] + [whole] * len(parts) + [ANY] * 2,
        out_specs=[ANY] * 2,
        out_shape=[jax.ShapeDtypeStruct(mix_grad.shape, jnp.float32)] * 2,
        scratch_shapes=[
            pltpu.VMEM((width, width), jnp.bfloat16),
            pltpu.VMEM((count, piece, width), jnp.float32),
            pltpu.VMEM((count, piece, width), jnp.float32),
            pltpu.SemaphoreType.DMA((count, 2)),
        ],
        input_output_aliases={3 + len(parts): 0, 4 + len(parts): 1},
        compiler_params=params("arbitrary", limit=GRADIENT_LIMIT),
        name="last_gradients",
    )(place, weight, flipped, *parts, mix_grad, out_grad)


def body(
    features,
    cotangent,
    send_order,
    pair_index,
    edge_mask,
    distance,
    radial_weight,
    mix_weight,
    out_weight,
    *,
    n_dp,
    n_blk,
):
    rows, total = features.shape
    width = mix_weight.shape[1]
    pieces = 2 * n_blk
    shard = mix_weight.shape[0] // n_blk
    piece = math.gcd(shard, width)
    at_dp, at_blk = lax.axis_index("dp"), lax.axis_index("blk")
    place = jnp.stack([at_dp % 2 * n_blk + at_blk, at_blk * (shard // piece)]).astype(jnp.int32)

    def over_dp(value, step):
        return lax.ppermute(value, "dp", [(i, i ^ step) for i in range(n_dp)])

    def over_blk(value, step):
        return lax.ppermute(value, "blk", [(i, i ^ step) for i in range(n_blk)])

    def all_to_all(value):
        return lax.all_to_all(value, "dp", split_axis=0, concat_axis=0, tiled=True)

    def plane_sum(near, far):
        height = near.shape[0] // n_blk
        chip = near + over_dp(far, 1).astype(jnp.float32)
        own = chip[:height]
        for step in range(1, n_blk):
            part = chip[step * height : (step + 1) * height].astype(jnp.bfloat16)
            own = own + over_blk(part, step).astype(jnp.float32)
        return own

    def z_sum_direct(own):
        own = own.astype(jnp.bfloat16)
        return tree_sum([own] + [over_dp(own, 2 * step) for step in range(1, n_dp // 2)])

    bits = [1 << i for i in range((n_dp // 2).bit_length() - 1)]
    upper = [(at_dp // 2) & bit for bit in bits]

    def z_halved(own):
        for bit, high in zip(bits[:-1], upper):
            half = own.shape[0] // 2
            kept = jnp.where(high > 0, own[half:], own[:half])
            given = jnp.where(high > 0, own[:half], own[half:]).astype(jnp.bfloat16)
            own = kept + over_dp(given, 2 * bit).astype(jnp.float32)
        own = own.astype(jnp.bfloat16)
        return own, over_dp(own, 2 * bits[-1])

    def z_joined(own, other):
        own = tree_sum([own, other])
        for bit, high in reversed(list(zip(bits[:-1], upper))):
            other = over_dp(own, 2 * bit)
            own = jnp.where(
                high > 0,
                jnp.concatenate([other, own], axis=0),
                jnp.concatenate([own, other], axis=0),
            )
        return own

    def plane_gather(own, *others):
        near = [own] + [over_blk(own, step) for step in range(1, n_blk)]
        return near + [over_dp(after(part, *others), 1) for part in near]

    sent_most = pick_rows(send_order, features, width, MOST)
    came_most = all_to_all(sent_most)
    sent_last = pick_rows(send_order, after(features, sent_most), width, LAST)
    gate = gate_matrices(pair_index, edge_mask, after(distance, sent_last), radial_weight, rows)
    cotangent, mix_weight, out_weight = lax.optimization_barrier(
        (cotangent, mix_weight, out_weight, gate)
    )[:3]
    cots = [flip_cotangent(cotangent, width, level) for level in range(LMAX + 1)]
    maps = degree_products(mix_weight, out_weight)
    flipped, out_flipped = (
        weight.reshape(LMAX + 1, width, width).swapaxes(1, 2).reshape(weight.shape)
        for weight in (mix_weight, out_weight)
    )
    ready = (gate, maps, flipped, out_flipped, *cots)
    came_last = all_to_all(after(sent_last, came_most, *ready))

    local = after(came_most, *ready)
    own = plane_sum(*outer_sum(place, gate, local, cots, width, MOST, pieces))
    own, other = z_halved(own)
    updated = update(gate, maps, local, width, MOST, total, None)

    local = after(came_last, own, updated)
    near, far = outer_sum(place, gate, local, cots, width, LAST, pieces)
    most = plane_gather(z_joined(own, after(other, near)))
    last = z_sum_direct(plane_sum(near, far))
    updated = update(gate, maps, local, width, LAST, total, updated)
    mix_grad, out_grad = most_gradients(place, out_flipped, flipped, most, shard, piece)
    last = plane_gather(after(last, updated, *most), mix_grad)
    mix_grad, out_grad = last_gradients(
        place, out_flipped, flipped, last, mix_grad, out_grad, piece
    )
    return updated, mix_grad, out_grad


def solution(mesh):
    in_specs = (
        P(("dp", "blk"), None),
        P(("dp", "blk"), None),
        P(("dp", "blk"), None),
        P(("dp", "blk"), None),
        P(("dp", "blk"), None, None),
        P(("dp", "blk"), None, None),
        P(),
        P(),
        P(),
    )
    out_specs = (P(("dp", "blk"), None), P("blk", None), P("blk", None))
    run = functools.partial(body, n_dp=mesh.shape["dp"], n_blk=mesh.shape["blk"])
    return jax.shard_map(run, mesh=mesh, in_specs=in_specs, out_specs=out_specs, check_vma=False)
```

```python
import functools
import math

import jax
import jax.numpy as jnp
from jax import lax
from jax.experimental import pallas as pl
from jax.experimental.pallas import tpu as pltpu
from jax.sharding import PartitionSpec as P

LMAX = 4
BLOCK = 128
CUT_RADIUS = 5.0
EDGE_SCALE = 0.25
MOST, LAST = (0, 1, 2, 3), (4,)
ORDER = MOST + LAST
VMEM_LIMIT = 48 * 1024 * 1024
PICK_LIMIT = 60 * 1024 * 1024
GRADIENT_LIMIT = 16 * 1024 * 1024
GATE_ROWS = 16
WHOLE = pl.BlockSpec(memory_space=pltpu.VMEM)
ANY = pl.BlockSpec(memory_space=pl.ANY)
SCALARS = pl.BlockSpec(memory_space=pltpu.SMEM)


def params(*semantics, limit=VMEM_LIMIT):
    return pltpu.CompilerParams(dimension_semantics=semantics, vmem_limit_bytes=limit)


def after(value, *others):
    return lax.optimization_barrier((value, *others))[0]


def span(degrees):
    return degrees[0] ** 2, (degrees[-1] + 1) ** 2


def comps_of(degrees):
    return [comp for level in degrees for comp in range(*span((level,)))]


def tree_sum(parts):
    parts = [part.astype(jnp.float32) for part in parts]
    while len(parts) > 1:
        parts = [parts[i] + parts[i + 1] for i in range(0, len(parts), 2)]
    return parts[0].astype(jnp.bfloat16)


def chosen_rows(order_ref, rows):
    local = lax.broadcasted_iota(jnp.int32, (rows, rows), 0)
    return (local == order_ref[...]).astype(jnp.float32).T.astype(jnp.bfloat16)


def pick_kernel(
    order_ref, rows_ref, out_ref, list_ref, held_ref, ready_ref, list_sem, in_sems, out_sems, *, first
):
    count, rows, width = ready_ref.shape
    order_load = pltpu.make_async_copy(order_ref, list_ref, list_sem)
    order_load.start()
    slab = rows // in_sems.shape[0]
    loads = [
        pltpu.make_async_copy(
            rows_ref.at[pl.ds(i * slab, slab), pl.ds(first * width, count * width)],
            held_ref.at[pl.ds(i * slab, slab), :],
            in_sems.at[i],
        )
        for i in range(in_sems.shape[0])
    ]
    for load in loads:
        load.start()
    order_load.wait()
    pick = chosen_rows(list_ref, rows)
    for load in loads:
        load.wait()
    stores = []
    for i in range(count):
        ready_ref[i] = jnp.dot(
            pick, held_ref[:, i * width : (i + 1) * width], preferred_element_type=jnp.float32
        ).astype(jnp.bfloat16)
        stores.append(
            pltpu.make_async_copy(
                ready_ref.at[i], out_ref.at[:, pl.ds(i * width, width)], out_sems.at[i]
            )
        )
        stores[-1].start()
    for store in stores:
        store.wait()


def pick_rows(order, features, width, degrees):
    rows = features.shape[0]
    first, last = span(degrees)
    count = last - first
    return pl.pallas_call(
        functools.partial(pick_kernel, first=first),
        in_specs=[ANY, ANY],
        out_specs=ANY,
        out_shape=jax.ShapeDtypeStruct((rows, count * width), jnp.bfloat16),
        scratch_shapes=[
            pltpu.VMEM(order.shape, jnp.int32),
            pltpu.VMEM((rows, count * width), jnp.bfloat16),
            pltpu.VMEM((count, rows, width), jnp.bfloat16),
            pltpu.SemaphoreType.DMA,
            pltpu.SemaphoreType.DMA((8,)),
            pltpu.SemaphoreType.DMA((count,)),
        ],
        compiler_params=params(limit=PICK_LIMIT),
        name="pick_rows",
    )(order, features)


def gate_kernel(pairs_ref, mask_ref, dist_ref, weight_ref, out_ref, radial_ref, *, basis_count):
    pair, step = pl.program_id(0), pl.program_id(1)

    @pl.when((pair == 0) & (step == 0))
    def _():
        out_ref[...] = jnp.zeros_like(out_ref)

    half = math.sqrt(0.5 * math.log2(math.e))
    dist = dist_ref[0]
    scaled = dist * (half * (basis_count - 1) / CUT_RADIUS)
    centers = lax.broadcasted_iota(jnp.int32, (basis_count, BLOCK), 0).astype(jnp.float32) * half
    weights = weight_ref[...]
    levels = LMAX + 1
    for row in range(GATE_ROWS):
        offset = scaled[row : row + 1, :] - centers
        phi = jnp.exp2(-(offset * offset))
        high = phi.astype(jnp.bfloat16)
        low = (phi - high.astype(jnp.float32)).astype(jnp.bfloat16)
        radial = jnp.dot(weights, high, preferred_element_type=jnp.float32)
        radial = radial + jnp.dot(weights, low, preferred_element_type=jnp.float32)
        radial = radial[0:8] + radial[8:16]
        for level in range(levels):
            radial_ref[level, row : row + 1, :] = radial[level : level + 1, :]
    envelope = (
        (0.5 * EDGE_SCALE)
        * (jnp.cos((math.pi / CUT_RADIUS) * dist) + 1.0)
        * mask_ref[0].astype(jnp.float32)
    )
    dest = pl.multiple_of(pairs_ref[pair, 0] * BLOCK + step * GATE_ROWS, GATE_ROWS)
    src = pl.multiple_of(pairs_ref[pair, 1] * BLOCK, BLOCK)
    for level in range(levels):
        out_ref[level, pl.ds(dest, GATE_ROWS), pl.ds(src, BLOCK)] = (
            radial_ref[level] * envelope
        ).astype(jnp.bfloat16)


def gate_matrices(pairs, mask, dist, radial_weight, rows):
    count = pairs.shape[0]
    levels = radial_weight.shape[1]
    transposed = radial_weight.T
    high = transposed.astype(jnp.bfloat16)
    low = (transposed - high.astype(jnp.float32)).astype(jnp.bfloat16)
    pad = ((0, 8 - levels), (0, 0))
    weights = jnp.concatenate([jnp.pad(high, pad), jnp.pad(low, pad)], axis=0)
    kernel = functools.partial(gate_kernel, basis_count=radial_weight.shape[0])
    edges = pl.BlockSpec((1, GATE_ROWS, BLOCK), lambda p, s, pairs: (p, s, 0))
    return pl.pallas_call(
        kernel,
        grid_spec=pltpu.PrefetchScalarGridSpec(
            num_scalar_prefetch=1,
            grid=(count, BLOCK // GATE_ROWS),
            in_specs=[edges, edges, pl.BlockSpec(weights.shape, lambda p, s, pairs: (0, 0))],
            out_specs=pl.BlockSpec((levels, rows, rows), lambda p, s, pairs: (0, 0, 0)),
            scratch_shapes=[pltpu.VMEM((levels, GATE_ROWS, BLOCK), jnp.float32)],
        ),
        out_shape=jax.ShapeDtypeStruct((levels, rows, rows), jnp.bfloat16),
        compiler_params=params("arbitrary", "arbitrary"),
        cost_estimate=pl.CostEstimate(
            flops=2 * 3 * 512 * count * BLOCK * BLOCK * radial_weight.shape[0],
            bytes_accessed=2 * 4 * count * BLOCK * BLOCK,
            transcendentals=count * BLOCK * BLOCK * radial_weight.shape[0],
        ),
        name="gate",
    )(pairs, mask, dist, weights)


def product_kernel(left_ref, right_ref, out_ref):
    out_ref[...] = jnp.dot(
        left_ref[...], right_ref[...], preferred_element_type=jnp.float32
    ).astype(jnp.bfloat16)


def degree_products(left, right):
    width = left.shape[1]
    block = pl.BlockSpec((width, width), lambda i: (i, 0))
    return pl.pallas_call(
        product_kernel,
        grid=(left.shape[0] // width,),
        in_specs=[block, block],
        out_specs=block,
        out_shape=jax.ShapeDtypeStruct(left.shape, jnp.bfloat16),
        compiler_params=params("arbitrary"),
        name="degree_products",
    )(left, right)


def flip_kernel(rows_ref, out_ref):
    out_ref[...] = rows_ref[...].T


def flip_cotangent(cotangent, width, level):
    rows = cotangent.shape[0]
    first, last = span((level,))
    return pl.pallas_call(
        flip_kernel,
        grid=(last - first,),
        in_specs=[pl.BlockSpec((rows, width), lambda i: (0, first + i))],
        out_specs=pl.BlockSpec((width, rows), lambda i: (0, i)),
        out_shape=jax.ShapeDtypeStruct((width, (last - first) * rows), jnp.bfloat16),
        compiler_params=params("arbitrary"),
        name="flip_cotangent",
    )(cotangent)


def outer_kernel(place_ref, gate_ref, local_ref, *refs, pieces, levels):
    cots = refs[: len(levels)]
    near_ref, far_ref, mixed_ref, sum_ref = refs[len(levels) :]
    rows, width = local_ref.shape[0], mixed_ref.shape[1]
    comps = comps_of(levels)
    for slot, level in enumerate(levels):
        first, last = span((level,))
        for comp in range(first, last):
            at = comps.index(comp) * width
            mixed_ref[(comp - first) * rows : (comp - first + 1) * rows, :] = jnp.dot(
                gate_ref[level], local_ref[:, at : at + width], preferred_element_type=jnp.float32
            ).astype(jnp.bfloat16)
        depth = (last - first) * rows
        flipped = jnp.dot(
            cots[slot][...], mixed_ref[0:depth, :], preferred_element_type=jnp.float32
        )
        sum_ref[slot * width : (slot + 1) * width, :] = flipped.T
    half, height = pieces // 2, width // pieces
    for step in range(half):
        near = pl.multiple_of((place_ref[0] ^ step) * height, height)
        far = pl.multiple_of((place_ref[0] ^ (step + half)) * height, height)
        for slot in range(len(levels)):
            to = (step * len(levels) + slot) * height
            near_ref[to : to + height, :] = sum_ref[pl.ds(slot * width + near, height), :]
            far_ref[to : to + height, :] = sum_ref[pl.ds(slot * width + far, height), :].astype(
                jnp.bfloat16
            )


def outer_sum(place, gate, local, cots, width, levels, pieces):
    rows = gate.shape[1]
    whole = len(levels) * width
    deepest = 2 * max(levels) + 1
    total = sum(2 * level + 1 for level in levels)
    return pl.pallas_call(
        functools.partial(outer_kernel, pieces=pieces, levels=levels),
        in_specs=[SCALARS] + [WHOLE] * (2 + len(levels)),
        out_specs=[WHOLE] * 2,
        out_shape=[
            jax.ShapeDtypeStruct((whole // 2, width), jnp.float32),
            jax.ShapeDtypeStruct((whole // 2, width), jnp.bfloat16),
        ],
        scratch_shapes=[
            pltpu.VMEM((deepest * rows, width), jnp.bfloat16),
            pltpu.VMEM((whole, width), jnp.float32),
        ],
        compiler_params=params(),
        cost_estimate=pl.CostEstimate(
            flops=2 * total * rows * width * (rows + width),
            bytes_accessed=4 * total * rows * width,
            transcendentals=0,
        ),
        name="outer_sum",
    )(place, gate, local, *[cots[level] for level in levels])


def update_kernel(gate_ref, map_ref, local_ref, *refs, degrees):
    out_ref, ready_ref, sems = refs[-3:]
    width = map_ref.shape[1]
    copies = []
    for index, comp in enumerate(comps_of(degrees)):
        level = math.isqrt(comp)
        at = index * width
        hidden = local_ref[:, at : at + width]
        mixed = jnp.dot(gate_ref[level], hidden, preferred_element_type=jnp.float32)
        weight = map_ref[level * width : (level + 1) * width, :]
        added = jnp.dot(mixed.astype(jnp.bfloat16), weight, preferred_element_type=jnp.float32)
        ready_ref[index] = (hidden.astype(jnp.float32) + added).astype(jnp.bfloat16)
        copies.append(
            pltpu.make_async_copy(
                ready_ref.at[index],
                out_ref.at[:, pl.ds(comp * width, width)],
                sems.at[index],
            )
        )
        copies[-1].start()
    for copy in copies:
        copy.wait()


def update(gate, maps, local, width, degrees, total, held):
    rows = local.shape[0]
    count = len(comps_of(degrees))
    in_specs = [WHOLE] * 3
    operands = [gate, maps, local]
    aliases = {}
    if held is not None:
        in_specs.append(ANY)
        operands.append(held)
        aliases = {3: 0}
    return pl.pallas_call(
        functools.partial(update_kernel, degrees=degrees),
        in_specs=in_specs,
        out_specs=ANY,
        out_shape=jax.ShapeDtypeStruct((rows, total), jnp.bfloat16),
        scratch_shapes=[
            pltpu.VMEM((count, rows, width), jnp.bfloat16),
            pltpu.SemaphoreType.DMA((count,)),
        ],
        input_output_aliases=aliases,
        compiler_params=params(),
        cost_estimate=pl.CostEstimate(
            flops=2 * count * rows * width * (rows + width),
            bytes_accessed=4 * count * rows * width,
            transcendentals=0,
        ),
        name="update",
    )(*operands)


def place_parts(place_ref, parts, outer_ref):
    width = outer_ref.shape[1]
    height = width // len(parts)
    for step, part in enumerate(parts):
        row = pl.multiple_of((place_ref[0] ^ step) * height, height)
        for slot in range(part.shape[0] // height):
            outer_ref[pl.ds(slot * width + row, height), :] = part[
                slot * height : (slot + 1) * height, :
            ]


def gradients(rows, outer, flipped, weight):
    mix = jnp.dot(rows, weight, preferred_element_type=jnp.float32)
    return mix, jnp.dot(flipped, outer, preferred_element_type=jnp.float32)


def most_kernel(place_ref, weight_ref, flip_ref, *refs, piece):
    *parts, mix_ref, out_ref, outer_ref = refs
    width = weight_ref.shape[0]

    @pl.when(pl.program_id(0) == 0)
    def _():
        place_parts(place_ref, parts, outer_ref)

    row = (place_ref[1] + pl.program_id(0)) * piece

    @pl.when(row < len(MOST) * width)
    def _():
        first = pl.multiple_of((row // width - place_ref[2]) * width, width)
        mix_ref[...], out_ref[...] = gradients(
            outer_ref[pl.ds(pl.multiple_of(first + row % width, piece), piece), :],
            outer_ref[pl.ds(first, width), :],
            flip_ref[...],
            weight_ref[...],
        )


def most_gradients(place, weight, flipped, parts, shard, piece):
    width = weight.shape[1]
    whole = pl.BlockSpec(parts[0].shape, lambda i, place: (0, 0))
    return pl.pallas_call(
        functools.partial(most_kernel, piece=piece),
        grid_spec=pltpu.PrefetchScalarGridSpec(
            num_scalar_prefetch=1,
            grid=(shard // piece,),
            in_specs=[
                pl.BlockSpec(
                    (width, width), lambda i, place: ((place[1] + i) * piece // width, 0)
                ),
                pl.BlockSpec((piece, width), lambda i, place: (place[1] + i, 0)),
            ]
            + [whole] * len(parts),
            out_specs=[pl.BlockSpec((piece, width), lambda i, place: (i, 0))] * 2,
            scratch_shapes=[pltpu.VMEM((len(parts) * parts[0].shape[0], width), jnp.bfloat16)],
        ),
        out_shape=[jax.ShapeDtypeStruct((shard, width), jnp.float32)] * 2,
        compiler_params=params("arbitrary", limit=GRADIENT_LIMIT),
        name="most_gradients",
    )(place, weight, flipped, *parts)


def last_kernel(place_ref, weight_ref, flip_ref, *refs, piece):
    *parts, _, _, mix_out, out_out, outer_ref, mix_ref, out_ref, sems = refs
    width = weight_ref.shape[0]
    place_parts(place_ref, parts, outer_ref)
    count = mix_ref.shape[0]

    def each(index):
        row = (place_ref[1] + index) * piece - LAST[0] * width
        to = pl.ds(index * piece, piece)
        copies = [
            pltpu.make_async_copy(mix_ref.at[index], mix_out.at[to, :], sems.at[index, 0]),
            pltpu.make_async_copy(out_ref.at[index], out_out.at[to, :], sems.at[index, 1]),
        ]
        return row, (row >= 0) & (row < width), copies

    for index in range(count):
        row, held, copies = each(index)

        @pl.when(held)
        def _():
            mine = pl.ds(pl.multiple_of(row, piece), piece)
            mix_ref[index], out_ref[index] = gradients(
                outer_ref[mine, :], outer_ref[...], flip_ref[mine, :], weight_ref[...]
            )
            for copy in copies:
                copy.start()

    for index in range(count):
        _, held, copies = each(index)

        @pl.when(held)
        def _():
            for copy in copies:
                copy.wait()


def last_gradients(place, weight, flipped, parts, mix_grad, out_grad, piece):
    shard, width = mix_grad.shape
    own = pl.BlockSpec((width, width), lambda i: (LAST[0], 0))
    whole = pl.BlockSpec(parts[0].shape, lambda i: (0, 0))
    count = shard // piece
    return pl.pallas_call(
        functools.partial(last_kernel, piece=piece),
        grid=(1,),
        in_specs=[SCALARS, own, own] + [whole] * len(parts) + [ANY] * 2,
        out_specs=[ANY] * 2,
        out_shape=[jax.ShapeDtypeStruct(mix_grad.shape, jnp.float32)] * 2,
        scratch_shapes=[
            pltpu.VMEM((width, width), jnp.bfloat16),
            pltpu.VMEM((count, piece, width), jnp.float32),
            pltpu.VMEM((count, piece, width), jnp.float32),
            pltpu.SemaphoreType.DMA((count, 2)),
        ],
        input_output_aliases={3 + len(parts): 0, 4 + len(parts): 1},
        compiler_params=params("arbitrary", limit=GRADIENT_LIMIT),
        name="last_gradients",
    )(place, weight, flipped, *parts, mix_grad, out_grad)


def body(
    features,
    cotangent,
    send_order,
    pair_index,
    edge_mask,
    distance,
    radial_weight,
    mix_weight,
    out_weight,
    *,
    n_dp,
    n_blk,
):
    rows, total = features.shape
    width = mix_weight.shape[1]
    pieces = 2 * n_blk
    shard = mix_weight.shape[0] // n_blk
    piece = math.gcd(shard, width)
    at_dp, at_blk = lax.axis_index("dp"), lax.axis_index("blk")
    reach = max(((i + 1) * shard - 1) // width - i * shard // width + 1 for i in range(n_blk))
    reach = min(reach, len(MOST))

    def first_degree(at):
        return jnp.minimum(at * shard // width, len(MOST) - reach)

    place = jnp.stack(
        [at_dp % 2 * n_blk + at_blk, at_blk * (shard // piece), first_degree(at_blk)]
    ).astype(jnp.int32)

    def over_dp(value, step):
        return lax.ppermute(value, "dp", [(i, i ^ step) for i in range(n_dp)])

    def over_blk(value, step):
        return lax.ppermute(value, "blk", [(i, i ^ step) for i in range(n_blk)])

    def all_to_all(value):
        return lax.all_to_all(value, "dp", split_axis=0, concat_axis=0, tiled=True)

    def chip_sum(near, far):
        return near + over_dp(far, 1).astype(jnp.float32)

    def plane_sum(chip):
        height = chip.shape[0] // n_blk
        own = chip[:height]
        for step in range(1, n_blk):
            part = chip[step * height : (step + 1) * height].astype(jnp.bfloat16)
            own = own + over_blk(part, step).astype(jnp.float32)
        return own

    bits = [1 << i for i in range((n_dp // 2).bit_length() - 1)]
    upper = [(at_dp // 2) & bit for bit in bits]

    def z_halved(own):
        for bit, high in zip(bits[:-1], upper):
            half = own.shape[0] // 2
            kept = jnp.where(high > 0, own[half:], own[:half])
            given = jnp.where(high > 0, own[:half], own[half:]).astype(jnp.bfloat16)
            own = kept + over_dp(given, 2 * bit).astype(jnp.float32)
        own = own.astype(jnp.bfloat16)
        return own, over_dp(own, 2 * bits[-1])

    def z_joined(own, *others):
        for bit, high in reversed(list(zip(bits[:-1], upper))):
            other = after(over_dp(own, 2 * bit), *others)
            own = jnp.where(
                high > 0,
                jnp.concatenate([other, own], axis=0),
                jnp.concatenate([own, other], axis=0),
            )
        return own

    def plane_gather(own, needed, *others):
        near = [needed(own, at_blk)]
        near += [over_blk(needed(own, at_blk ^ step), step) for step in range(1, n_blk)]
        return near + [over_dp(after(part, *others), 1) for part in near]

    def needed_degrees(own, at):
        height = width // pieces
        return lax.dynamic_slice_in_dim(own, first_degree(at) * height, reach * height, axis=0)

    sent_most = pick_rows(send_order, features, width, MOST)
    came_most = all_to_all(sent_most)
    sent_last = pick_rows(send_order, after(features, sent_most), width, LAST)
    gate = gate_matrices(pair_index, edge_mask, after(distance, sent_last), radial_weight, rows)
    cotangent, mix_weight, out_weight = lax.optimization_barrier(
        (cotangent, mix_weight, out_weight, gate)
    )[:3]
    cots = {level: flip_cotangent(cotangent, width, level) for level in MOST + LAST}
    maps = degree_products(mix_weight, out_weight)
    flipped, out_flipped = (
        weight.reshape(LMAX + 1, width, width).swapaxes(1, 2).reshape(weight.shape)
        for weight in (mix_weight, out_weight)
    )
    ready = (gate, maps, flipped, out_flipped, *cots.values())
    came_last = all_to_all(after(sent_last, came_most, *ready))

    local = after(came_most, *ready)
    own = plane_sum(chip_sum(*outer_sum(place, gate, local, cots, width, MOST, pieces)))
    own, other = z_halved(own)
    updated = update(gate, maps, local, width, MOST, total, None)

    local = after(came_last, own, updated)
    near, far = outer_sum(place, gate, local, cots, width, LAST, pieces)
    most = z_joined(tree_sum([own, after(other, near)]))
    most = plane_gather(most, needed_degrees)
    last = plane_sum(chip_sum(near, far)).astype(jnp.bfloat16)
    last = tree_sum([last] + [over_dp(last, 2 * step) for step in range(1, n_dp // 2)])
    updated = update(gate, maps, local, width, LAST, total, updated)
    mix_grad, out_grad = most_gradients(place, out_flipped, flipped, most, shard, piece)
    last = plane_gather(after(last, updated, *most), lambda own, at: own, mix_grad)
    mix_grad, out_grad = last_gradients(
        place, out_flipped, flipped, last, mix_grad, out_grad, piece
    )
    return updated, mix_grad, out_grad


def solution(mesh):
    in_specs = (
        P(("dp", "blk"), None),
        P(("dp", "blk"), None),
        P(("dp", "blk"), None),
        P(("dp", "blk"), None),
        P(("dp", "blk"), None, None),
        P(("dp", "blk"), None, None),
        P(),
        P(),
        P(),
    )
    out_specs = (P(("dp", "blk"), None), P("blk", None), P("blk", None))
    run = functools.partial(body, n_dp=mesh.shape["dp"], n_blk=mesh.shape["blk"])
    return jax.shard_map(run, mesh=mesh, in_specs=in_specs, out_specs=out_specs, check_vma=False)
```
